512 devices in a mesh: animals: 128 (over z, x, core), snps: 4 (over y).
Axes of the slice: x: 4, y: 4, z: 16, core: 2. Of those that a mesh axis runs over, the one named last changes fastest.
Arguments:
- animal_rhs: float32 [4, 131072], P(None, 'animals'), may hold values from -6 to 6
- marker_rhs: float32 [4, 25088], P(None, 'snps'), may hold values from -6 to 6
- animal_diagonal: float32 [131072], P('animals'), may hold values from 0.5 to 4
- marker_diagonal: float32 [25088], P('snps'), may hold values from 0.5 to 4
- marker_scale: float32 [25088], P('snps'), may hold values from 0.0031567267 to 0.012626907
- genotypes: bfloat16 [8192, 25088], P('animals', 'snps'), may hold values from -1 to 1, as said below
- tile_weights: bfloat16 [14336, 128, 128], P('animals'), may hold values from -0.375 to 0.375
- tile_rows: int32 [14336], P('animals'), may hold values from 0 to 7
- tile_owner: int32 [14336, 1], P('animals'), may hold values from 0 to 127; in each aligned block of 112 rows (0 to 111, 112 to 223, ...) at most 2 rows name the same one
- tile_local: int32 [14336], P('animals'), may hold values from 0 to 7
- tile_count: int32 [128], P('animals'), may hold values from 98 to 112, as said below
- genotyped_block: int32 [128], P('animals'), may hold values from 0 to 7
Outputs:
- animal_solution: float32 [4, 131072], P(None, 'animals')
- marker_solution: float32 [4, 25088], P(None, 'snps')
- animal_residual: float32 [4, 131072], P(None, 'animals')
- marker_residual: float32 [4, 25088], P(None, 'snps')
The draws below stay inside these ranges and needn't reach their ends.
Inputs may be any that keep to these rules, and one draw needn't show every extreme that they name: `genotypes`: centred genotype codes, each -1, 0 or 1. `tile_owner`: in the rows of one index of animals (aligned blocks of 112 rows) no owner appears more than 2 times. `tile_count`: some index of animals has all 112 slots live.
All inputs are finite; a program needn't handle non-finite values.
Results may differ from the reference program's by a relative error of at most 0.035.
Values may be sent and summed in bfloat16 or wider, within the bound.
A program may use at most 64 MiB of HBM per device.

```python
import math
import jax
import jax.numpy as jnp
import numpy as np
from jax import lax

TRAITS = 4
BLOCK = 128
NB_DEV = 8
SNPS = 25088
ITERS = 3
TILE_DEV = 112
GENO_DEV = 64
CAP = 2
NBLOCKS = 1024
ANIMALS = 131072
TILES = 14336
GENO_ROWS = 8192
N_ANIMALS = 128


def draw_genotypes(key, part):
    key = jax.random.fold_in(key, 5)
    allele_codes = jax.random.randint(key, (GENO_ROWS, SNPS), 0, 3)
    return (allele_codes.astype(jnp.float32) - 1.0).astype(jnp.bfloat16)


def draw_tile_count(key, part):
    key = jax.random.fold_in(key, 7)
    counts = jax.random.randint(key, (N_ANIMALS,), 7 * TILE_DEV // 8, TILE_DEV + 1)
    fuller = jax.random.randint(jax.random.fold_in(key, 1), (), 0, N_ANIMALS)
    return jnp.where(jnp.arange(N_ANIMALS) == fuller, TILE_DEV, counts).astype(jnp.int32)


def place_ends(entries, key, least, largest):
    place = [jax.random.randint(jax.random.fold_in(key, axis), (), 0, length) for axis, length in enumerate(entries.shape)]
    widest = entries.shape.index(max(entries.shape))
    neighbour = place[:widest] + [(place[widest] + 1) % entries.shape[widest]] + place[widest + 1:]
    return entries.at[tuple(place)].set(least).at[tuple(neighbour)].set(largest)


def levels(key, extent, split, low, high):
    def one(dim, shards_of):
        steps = jax.random.uniform(jax.random.fold_in(jax.random.fold_in(key, 6), dim), (shards_of,), jnp.float32, low / len(split), high / len(split))
        return jnp.repeat(jnp.exp(steps), extent[dim] // shards_of).reshape((-1,) + (1,) * (len(extent) - dim - 1))

    factor_of = one(*split[0])
    for cut in split[1:]:
        factor_of = factor_of * one(*cut)
    return factor_of


def routed_block(rng, own, number, rows, count, top, limit, lean):
    order = jax.random.permutation(rng, count)
    heavy_load, ordinary = load_shares(count, rows * top, limit, lean, True), load_shares(count, rows * top, limit, lean, False)
    places = jnp.arange(count)

    def named(lengths, rotation):
        used = int((lengths > 0).sum())
        fixed = max(1, used // 4)
        shifted = fixed + (places - fixed + rotation * (used - fixed)) % max(1, count - fixed)
        return jnp.zeros((count,), jnp.int32).at[order[jnp.where(places < fixed, places, shifted)]].set(jnp.asarray(lengths, jnp.int32))

    lengths = jnp.where(number % 4 == 0, named(heavy_load, number // 4), named(ordinary, number - number // 4 - 1))
    mixed = jax.random.permutation(jax.random.fold_in(own, 3), count)
    giver, sink = mixed[0:count // 2 * 2:2], mixed[1:count // 2 * 2:2]
    room = jnp.minimum(lengths[giver] - 1, limit - lengths[sink]) // 2
    room = jnp.where((giver == order[0]) | (sink == order[0]) | (lengths[sink] == 0), 0, jnp.maximum(room, 0))
    shifted = jax.random.randint(jax.random.fold_in(own, 4), (count // 2,), 0, 1 << 20) % (room + 1)
    lengths = lengths.at[giver].add(-shifted).at[sink].add(shifted)
    items = jnp.searchsorted(jnp.cumsum(lengths), jnp.arange(rows * top), side="right").astype(jnp.int32)
    grid = items.reshape(top, rows).T
    grid = grid[jax.random.permutation(jax.random.fold_in(own, 1), rows)]
    rotation = jax.random.randint(jax.random.fold_in(own, 2), (rows, 1), 0, top)
    return jnp.take_along_axis(grid, (jnp.arange(top)[None, :] + rotation) % top, axis=1)


def load_shares(count, total, bound, slope, full):
    portions = [(1 << 20) // math.isqrt(grade ** slope) + 1 for grade in range(1, count + 1)]
    largest = bound if full else min(bound, max(-(-total // count), total * portions[0] // sum(portions)))
    least = 1 if total - largest >= count - 1 else 0
    given, surplus = [largest] + [least] * (count - 1), total - largest - least * (count - 1)
    while surplus > 0:
        candidates = [i for i in range(1, count) if given[i] < largest] or [i for i in range(1, count) if given[i] < bound]
        pool, left = sum([portions[i] for i in candidates]), surplus
        for i in candidates:
            addition = min(bound - given[i], max(1, left * portions[i] // pool), surplus)
            given[i] = given[i] + addition
            surplus = surplus - addition
    return np.array(given)


def centred(own_key, extent, width, bound, cuts=(), held_as=jnp.bfloat16):
    values = jax.random.normal(own_key, extent, jnp.float32) * width
    if len(cuts) > 0:
        values = levels(own_key, extent, cuts, -0.22, 0.18) * values
    return jnp.clip(values, min=-bound, max=bound).astype(held_as)


def setup_inputs(seed: int = 0) -> dict:
    arg_keys = jax.random.split(jax.random.key(seed), 13)
    animal_rhs = centred(arg_keys[0], (TRAITS, ANIMALS), 1.0, 6.0, ((1, 128),), jnp.float32)
    marker_rhs = centred(arg_keys[1], (TRAITS, SNPS), 1.0, 6.0, ((1, 4),), jnp.float32)
    animal_diagonal = jnp.clip(jnp.exp(math.log(4.0) - 2.0794415 * jax.random.uniform(arg_keys[2], (ANIMALS,), jnp.float32) ** levels(arg_keys[2], (ANIMALS,), ((0, 128),), -0.2, 0.2)), 0.5, 4.0)
    marker_diagonal = jnp.clip(jnp.exp(math.log(4.0) - 2.0794415 * jax.random.uniform(arg_keys[3], (SNPS,), jnp.float32) ** levels(arg_keys[3], (SNPS,), ((0, 4),), -0.2, 0.2)), 0.5, 4.0)
    marker_scale = jnp.clip(jnp.exp(math.log(0.012626907) - 1.3862944 * jax.random.uniform(arg_keys[4], (SNPS,), jnp.float32) ** levels(arg_keys[4], (SNPS,), ((0, 4),), -0.2, 0.2)), 0.0031567267, 0.012626907)
    genotypes = draw_genotypes(jax.random.fold_in(arg_keys[12], 71), 0)
    tile_weights = centred(arg_keys[6], (TILES, BLOCK, BLOCK), (2 * BLOCK) ** -0.5, 0.375, ((0, 128),))
    tile_rows = place_ends(jax.random.randint(arg_keys[7], (TILES,), 0, NB_DEV), jax.random.fold_in(arg_keys[7], 1), 0, NB_DEV - 1).astype(jnp.int32)
    tile_owner_keys = jax.random.split(jax.random.fold_in(arg_keys[8], 1), TILES // TILE_DEV)
    tile_owner_turns = jax.random.permutation(jax.random.fold_in(arg_keys[8], 3), TILES // TILE_DEV)
    tile_owner = jax.vmap(lambda own, number: routed_block(jax.random.fold_in(arg_keys[8], 2), own, number, TILE_DEV, N_ANIMALS, 1, CAP, 2))(tile_owner_keys, tile_owner_turns).reshape((TILES, 1))
    tile_local = place_ends(jax.random.randint(arg_keys[9], (TILES,), 0, NB_DEV), jax.random.fold_in(arg_keys[9], 1), 0, NB_DEV - 1).astype(jnp.int32)
    tile_count = draw_tile_count(jax.random.fold_in(arg_keys[12], 71), 0)
    genotyped_block = place_ends(jax.random.randint(arg_keys[11], (N_ANIMALS,), 0, NB_DEV), jax.random.fold_in(arg_keys[11], 1), 0, NB_DEV - 1).astype(jnp.int32)
    return {"animal_rhs": animal_rhs, "marker_rhs": marker_rhs, "animal_diagonal": animal_diagonal, "marker_diagonal": marker_diagonal, "marker_scale": marker_scale, "genotypes": genotypes, "tile_weights": tile_weights, "tile_rows": tile_rows, "tile_owner": tile_owner, "tile_local": tile_local, "tile_count": tile_count, "genotyped_block": genotyped_block}


def reference(animal_rhs, marker_rhs, animal_diagonal, marker_diagonal, marker_scale, genotypes, tile_weights, tile_rows, tile_owner, tile_local, tile_count, genotyped_block):
    slot_ids = jnp.arange(TILES, dtype=jnp.int32)
    device_ids = slot_ids // TILE_DEV
    live_mask = ((slot_ids % TILE_DEV) < tile_count[device_ids]).astype(jnp.float32)
    row_ids = device_ids * NB_DEV + tile_rows
    parent_ids = tile_owner[:, 0] * NB_DEV + tile_local
    geno_ids = jnp.arange(N_ANIMALS, dtype=jnp.int32) * NB_DEV + genotyped_block
    weights = tile_weights.astype(jnp.float32)
    highest = lax.Precision.HIGHEST

    def operate(animal_vec, marker_vec):
        blocks = animal_vec.astype(jnp.bfloat16).reshape(TRAITS, NBLOCKS, BLOCK)
        fetched = jnp.transpose(blocks[:, parent_ids, :], (1, 0, 2)).astype(jnp.float32)
        products = jnp.einsum("tik,tsk->tsi", weights, fetched, precision=highest) * live_mask[:, None, None]
        row_sums = jax.ops.segment_sum(products, row_ids, num_segments=NBLOCKS).astype(jnp.bfloat16)
        per_tile = row_sums[row_ids].astype(jnp.float32)
        back_terms = jnp.einsum("tik,tsi->tsk", weights, per_tile, precision=highest) * live_mask[:, None, None]
        pedigree = jax.ops.segment_sum(back_terms, parent_ids, num_segments=NBLOCKS)
        pedigree = jnp.transpose(pedigree, (1, 0, 2)).reshape(TRAITS, ANIMALS)
        whole = animal_vec.reshape(TRAITS, NBLOCKS, BLOCK)
        own_rows = whole[:, geno_ids, :GENO_DEV].reshape(TRAITS, GENO_ROWS)
        scaled = (marker_vec * marker_scale).astype(jnp.bfloat16)
        partial_value = lax.dot_general(scaled, genotypes, (((1,), (1,)), ((), ())), preferred_element_type=jnp.float32)
        geno_sum = own_rows + partial_value
        geno_half = geno_sum.astype(jnp.bfloat16)
        marker_back = jnp.dot(geno_half, genotypes, preferred_element_type=jnp.float32)
        placed = jnp.zeros((TRAITS, NBLOCKS, BLOCK), jnp.float32).at[:, geno_ids, :GENO_DEV].add(geno_sum.reshape(TRAITS, N_ANIMALS, GENO_DEV))
        animal_out = animal_diagonal * animal_vec + pedigree + placed.reshape(TRAITS, ANIMALS)
        marker_out = marker_diagonal * marker_vec + marker_scale * marker_back
        return animal_out, marker_out

    def inner(first_u, first_m, second_u, second_m):
        return jnp.sum(first_u * second_u, axis=1) + jnp.sum(first_m * second_m, axis=1)

    animal_guess = jnp.zeros_like(animal_rhs)
    marker_guess = jnp.zeros_like(marker_rhs)
    animal_residual = animal_rhs
    marker_residual = marker_rhs
    animal_precond = animal_residual / animal_diagonal
    marker_precond = marker_residual / marker_diagonal
    animal_search = animal_precond
    marker_search = marker_precond
    rho_now = inner(animal_residual, marker_residual, animal_precond, marker_precond)
    for iteration in range(ITERS):
        animal_image, marker_image = operate(animal_search, marker_search)
        step_size = rho_now / inner(animal_search, marker_search, animal_image, marker_image)
        animal_guess = animal_guess + step_size[:, None] * animal_search
        marker_guess = marker_guess + step_size[:, None] * marker_search
        animal_residual = animal_residual - step_size[:, None] * animal_image
        marker_residual = marker_residual - step_size[:, None] * marker_image
        animal_precond = animal_residual / animal_diagonal
        marker_precond = marker_residual / marker_diagonal
        rho_next = inner(animal_residual, marker_residual, animal_precond, marker_precond)
        beta_ratio = rho_next / rho_now
        animal_search = animal_precond + beta_ratio[:, None] * animal_search
        marker_search = marker_precond + beta_ratio[:, None] * marker_search
        rho_now = rho_next
    return animal_guess, marker_guess, animal_residual, marker_residual
```

```python
from types import SimpleNamespace

import jax
import jax.numpy as jnp
from jax import lax
from jax.experimental import pallas as pl
from jax.experimental.pallas import tpu as pltpu
from jax.sharding import PartitionSpec as P

ITERS = 3
CAP = 2
NJ = 8
JB, ZB, ZS = 7, 7, 2
LANES = 128
A1, A2, B1, B2, Y, R1, R2, G1, G2, STAGES = range(10)
SZ, SX, SY, STEPS = range(4)
SUMS = 2 * ITERS - 1
ANIMALS, SNPS = "animals", "snps"
MESH = pl.DeviceIdType.MESH
F32, BF16, I32 = jnp.float32, jnp.bfloat16, jnp.int32


def iota(shape, dim):
    return lax.broadcasted_iota(I32, shape, dim)


def total(x):
    return jnp.sum(jnp.sum(x, axis=1, keepdims=True), axis=0, keepdims=True)


def kernel(nz, ny, arhs_h, mrhs_h, adiag_h, mdiag_h, mscale_h, geno_h, w_h, rows_h, owner_h, local_h, count_s,
           gblk_s, asol, msol, ares, mres, s):
    traits, markers = mrhs_h.shape
    tiles = w_h.shape[0]
    nb = adiag_h.shape[0]
    geno = geno_h.shape[0]
    slots = nz * CAP
    all_slots, dense = NJ * slots, nz * nb
    wide = ZB * LANES
    me, y = lax.axis_index(ANIMALS), lax.axis_index(SNPS)
    z, j = lax.div(me, NJ), lax.rem(me, NJ)
    in_jb = j < JB
    in_zb = (lax.rem(z, ZS) == 0) & (z < ZB * ZS)

    def to_z(zz):
        return {ANIMALS: zz * NJ + j, SNPS: y}

    def to_j(jj):
        return {ANIMALS: z * NJ + jj, SNPS: y}

    def to_y(yy):
        return {ANIMALS: me, SNPS: yy}

    def each(here, count, act):
        half = count // 2
        act(lax.rem(here + half, count))

        def step(d, c):
            act(lax.rem(here + half - d, count))
            act(lax.rem(here + half + d, count))
            return c

        lax.fori_loop(1, half, step, 0)

    def push(src, dst, send, recv, device):
        pltpu.make_async_remote_copy(src_ref=src, dst_ref=dst, send_sem=send, recv_sem=recv,
                                     device_id=device, device_id_type=MESH).start()

    def await_bytes(ref, sem):
        pltpu.make_async_copy(ref, ref, sem).wait()

    barrier = pltpu.get_barrier_semaphore()

    def greet(device):
        pl.semaphore_signal(barrier, inc=1, device_id=device, device_id_type=MESH)

    each(z, nz, lambda zz: greet(to_z(zz)))
    each(j, NJ, lambda jj: greet(to_j(jj)))
    each(y, ny, lambda yy: greet(to_y(yy)))

    pairs = ((arhs_h, s.arhs), (adiag_h, s.adiag), (mrhs_h, s.mrhs), (mdiag_h, s.mdiag.at[0]), (mscale_h, s.mscale.at[0]),
             (owner_h, s.owner), (local_h, s.local), (rows_h, s.rows), (geno_h, s.g), (w_h, s.w))
    gets = [pltpu.make_async_copy(src, dst, s.get.at[k]) for k, (src, dst) in enumerate(pairs)]
    for get in gets:
        get.start()
    gets[0].wait()
    gets[1].wait()

    blk = iota((nb, LANES), 0)
    lane = iota((nb, LANES), 1)
    sub = iota((8, LANES), 0)
    trait_col = iota((traits, 1), 0)
    lane4 = iota((traits, LANES), 1)
    a_diag = s.adiag[...]
    a_inv = 1.0 / a_diag
    r_a = jnp.zeros((nb, LANES), F32)
    for k in range(nb):
        row = jnp.where(trait_col == y, s.arhs[:, k * LANES:(k + 1) * LANES], 0.0)
        r_a = jnp.where(blk == k, jnp.sum(row, axis=0, keepdims=True), r_a)
    z_a = r_a * a_inv
    sol_a = jnp.zeros((nb, LANES), F32)
    gblk = gblk_s[0]
    cuts = [slice(b * wide, (b + 1) * wide) for b in range(JB)]
    col = jnp.zeros((traits, 1), F32)

    def plan():
        own = s.owner[...]
        names = (iota((nz * NJ, tiles), 0) == own).astype(F32)
        before = (iota((tiles, tiles), 0) < iota((tiles, tiles), 1)).astype(F32)
        earlier = jnp.dot(names.astype(BF16), before.astype(BF16), preferred_element_type=F32)
        rank = jnp.sum(names * earlier, axis=0, keepdims=True)
        slot = (lax.rem(own, NJ) * slots + lax.div(own, NJ) * CAP).astype(F32) + rank
        slot = jnp.where(iota((1, tiles), 1) < count_s[0], slot, -1.0)
        hit = (iota((all_slots, tiles), 0).astype(F32) == slot).astype(F32)
        asked = jnp.sum(hit * (s.local[...] + 1).astype(F32), axis=1, keepdims=True)
        asked = jnp.broadcast_to(asked, (all_slots, LANES))
        s.id_send[...] = asked.reshape(NJ, slots, LANES).astype(BF16)
        each(j, NJ, lambda jj: push(s.id_send.at[jj], s.id_recv.at[j], s.once_send.at[0], s.once_recv.at[0], to_j(jj)))
        s.id_recv[j] = s.id_send[j]
        s.table[...] = jnp.zeros_like(s.table)
        s.table[:, :tiles] = hit
        table = s.table[...]
        s.placed_t[...] = table.astype(BF16)
        s.placed[...] = table.T.astype(BF16)
        s.back[...] = jnp.zeros_like(s.back)

    def serve():
        await_bytes(s.id_recv.at[pl.ds(0, NJ - 1)], s.once_recv.at[0])
        ids = s.id_recv[...].astype(F32).reshape(all_slots, LANES)[:, :dense]
        source = lax.div(lax.rem(iota((all_slots, dense), 0), slots), CAP) * nb
        named = iota((all_slots, dense), 1).astype(F32) == source.astype(F32) + ids - 1.0
        pmat = ((ids > 0.5) & named).astype(F32)
        s.pmat[...] = pmat.astype(BF16)
        s.pmat_t[...] = pmat.T.astype(BF16)

    pl.semaphore_wait(barrier, nz + NJ + ny - 3)

    def start(it, stage, src, dst, device):
        push(src, dst, s.send.at[it, stage], s.recv.at[it, stage], device)

    def arrived(it, stage, ref):
        await_bytes(ref, s.recv.at[it, stage])

    def scalar_push(n, step, src, dst, device):
        push(src, dst, s.sum_send.at[n, step], s.sum_recv.at[n, step], device)

    def scalar_z(n, parts):
        row = jnp.zeros((1, LANES), F32)
        for k, part in enumerate(parts):
            row = jnp.where(lane4[:1] == k, total(part), row)
        s.sz_send[n] = row
        s.sz_recv[n, z] = row
        each(z, nz, lambda zz: scalar_push(n, SZ, s.sz_send.at[n], s.sz_recv.at[n, z], to_z(zz)))

    def scalar_x(n):
        await_bytes(s.sz_recv.at[n, pl.ds(0, nz - 1)], s.sum_recv.at[n, SZ])
        row = jnp.sum(s.sz_recv[n], axis=0)
        s.sx_send[n] = row
        s.sx_recv[n, j] = row
        each(j, NJ, lambda jj: scalar_push(n, SX, s.sx_send.at[n], s.sx_recv.at[n, j], to_j(jj)))

    def scalar_y(n, parts):
        await_bytes(s.sx_recv.at[n, pl.ds(0, NJ - 1)], s.sum_recv.at[n, SX])
        row = jnp.sum(s.sx_recv[n], axis=0)
        full = jnp.where(trait_col == y, row, 0.0)
        for k, part in enumerate(parts):
            full += jnp.where(lane4 == k, part, 0.0)
        s.sy_send[n] = full
        s.sy_recv[n, y] = full
        each(y, ny, lambda yy: scalar_push(n, SY, s.sy_send.at[n], s.sy_recv.at[n, y], to_y(yy)))

    def scalar_end(n):
        await_bytes(s.sy_recv.at[n, pl.ds(0, ny - 1)], s.sum_recv.at[n, SY])
        return jnp.sum(s.sy_recv[n], axis=0)

    def mine(col):
        return jnp.sum(jnp.where(trait_col == y, col, 0.0), axis=0, keepdims=True)

    def gather_wide(it):
        @pl.when(in_jb)
        def _():
            @pl.when(in_zb)
            def _():
                arrived(it, G1, s.g1_recv.at[it, pl.ds(0, ZB - 1)])

            @pl.when(jnp.logical_not(in_zb))
            def _():
                arrived(it, G1, s.g1_recv.at[it])

            s.g2_recv[it, j] = s.g1_recv[it]
            each(j, NJ, lambda jj: start(it, G2, s.g1_recv.at[it], s.g2_recv.at[it, j], to_j(jj)))

    def gather_end(it):
        @pl.when(in_jb)
        def _():
            arrived(it, G2, s.g2_recv.at[it, pl.ds(0, JB - 1)])

        @pl.when(jnp.logical_not(in_jb))
        def _():
            arrived(it, G2, s.g2_recv.at[it])

    def marker_image(it, b):
        cut = cuts[b]
        summed = jnp.concatenate([s.g2_recv[it, b, c] for c in range(ZB)], axis=1)
        q_m = s.mdiag[:, cut] * s.x[:, cut] + s.mscale[:, cut] * summed
        return q_m if it == 0 else q_m + beta * s.q[:, cut]

    rho = alpha = beta = None
    for it in range(ITERS):
        last = it == ITERS - 1
        norm = ITERS + it - 1

        s.a1_send[it] = z_a.astype(BF16)
        s.a1_recv[it, z] = s.a1_send[it]
        each(z, nz, lambda zz: start(it, A1, s.a1_send.at[it], s.a1_recv.at[it, z], to_z(zz)))
        if it == 0:
            for get in gets[2:-1]:
                get.wait()
            plan()
        else:
            scalar_z(norm, [r_a * z_a])
            gather_wide(it - 1)
            scalar_x(norm)
            gather_end(it - 1)

        dot_m, curv_m, rho_m = jnp.zeros((traits, geno), F32), col, col
        for b, cut in enumerate(cuts):
            if it == 0:
                m_inv = 1.0 / s.mdiag[:, cut]
                s.m_inv[:, cut] = m_inv
                r_m = s.mrhs[:, cut]
                x_m = r_m * m_inv
                s.m[:, cut] = x_m
                curv_m += jnp.sum(s.mdiag[:, cut] * x_m * x_m, axis=1, keepdims=True)
            else:
                q_m = marker_image(it - 1, b)
                s.q[:, cut] = q_m
                r_m = mres[:, cut] - alpha * q_m
                x_m = r_m * s.m_inv[:, cut]
            mres[:, cut] = r_m
            s.x[:, cut] = x_m
            rho_m += jnp.sum(r_m * x_m, axis=1, keepdims=True)
            mb = (x_m * s.mscale[:, cut]).astype(BF16)
            dot_m += lax.dot_general(mb, s.g[:, cut], (((1,), (1,)), ((), ())), preferred_element_type=F32)
        own_rows = jnp.sum(jnp.where((blk == gblk) & (lane < geno), z_a, 0.0), axis=0, keepdims=True)
        s.y_send[it] = jnp.where(sub == traits, own_rows, 0.0)
        s.y_send[it, :traits, :geno] = dot_m
        s.y_recv[it, y] = s.y_send[it]
        each(y, ny, lambda yy: start(it, Y, s.y_send.at[it], s.y_recv.at[it, y], to_y(yy)))

        if it == 0:
            serve()

        arrived(it, A1, s.a1_recv.at[it, pl.ds(0, nz - 1)])
        blocks = s.a1_recv[it].astype(F32).reshape(dense, LANES).astype(BF16)
        served = jnp.dot(s.pmat[...], blocks, preferred_element_type=F32)
        s.a2_send[it] = served.reshape(NJ, slots, LANES).astype(BF16)
        s.a2_recv[it, j] = s.a2_send[it, j]
        each(j, NJ, lambda jj: start(it, A2, s.a2_send.at[it, jj], s.a2_recv.at[it, j], to_j(jj)))

        arrived(it, Y, s.y_recv.at[it, pl.ds(0, ny - 1)])
        g = jnp.zeros((traits, LANES), F32)
        for t in range(ny):
            g += s.y_recv[it, t, :traits, :]
            g += jnp.where(trait_col == t, s.y_recv[it, t, traits:traits + 1, :], 0.0)
        gb = g[:, :geno].astype(BF16)
        for b, cut in enumerate(cuts):
            s.r1_send[it, b] = jnp.dot(gb, s.g[:, cut], preferred_element_type=F32)

        def send_r1(jj):
            @pl.when(jj < JB)
            def _():
                start(it, R1, s.r1_send.at[it, jj], s.r1_recv.at[it, j], to_j(jj))

        each(j, NJ, send_r1)
        if it > 0:
            scalar_y(norm, [rho_m])

        if it == 0:
            gets[-1].wait()
        arrived(it, A2, s.a2_recv.at[it, pl.ds(0, NJ - 1)])
        fetched = s.a2_recv[it].reshape(all_slots, LANES)
        s.fetched[...] = jnp.dot(s.placed[...], fetched, preferred_element_type=F32).reshape(LANES // 8, 8, LANES)

        def four(first):
            w = s.w[pl.ds(first, 4)]
            return jnp.concatenate([w[0:2].reshape(2 * LANES, LANES), w[2:4].reshape(2 * LANES, LANES)], axis=1)

        def forward(n, acc):
            rows = s.fetched[n]
            for h in (0, 4):
                a, b, c, d = [jnp.where(sub == s.rows[n * 8 + h + k], rows[h + k:h + k + 1], 0.0) for k in range(4)]
                left = jnp.concatenate([jnp.concatenate([a, c], axis=1), jnp.concatenate([b, d], axis=1)], axis=0)
                acc += lax.dot_general(left.astype(BF16), four(n * 8 + h), (((1,), (1,)), ((), ())),
                                       preferred_element_type=F32)
            return acc

        acc = lax.fori_loop(0, tiles // 8, forward, jnp.zeros((16, 2 * LANES), F32), unroll=2)
        v = acc[:8, :LANES] + acc[8:, LANES:]

        if it > 0:
            rho_next = scalar_end(norm)[:, 0:1]
            beta = rho_next / rho
            rho = rho_next
            beta_y = mine(beta)
            u, v_u, g_u = z_a + beta_y * u, v + beta_y * v_u, g + beta * g_u
        else:
            u, v_u, g_u = z_a, v, g
        g_row = jnp.sum(jnp.where(trait_col == y, g_u, 0.0), axis=0, keepdims=True)
        curv_a = a_diag * u * u + v_u * v_u + jnp.where(sub == 0, g_row * g_row, 0.0)
        scalar_z(it, [curv_a] if it > 0 else [curv_a, r_a * z_a])

        zero = jnp.zeros((8, LANES), F32)
        vb = v.astype(BF16).astype(F32)
        twice = jnp.concatenate([jnp.concatenate([vb, zero], axis=1), jnp.concatenate([zero, vb], axis=1)], axis=0)
        twice = twice.astype(BF16)

        def backward(n, c):
            rows = jnp.zeros((8, LANES), F32)
            for h in (0, 4):
                out = jnp.dot(twice, four(n * 8 + h), preferred_element_type=F32)
                for k in range(4):
                    up, across = k % 2, k // 2
                    part = out[8 * up:8 * up + 8, across * LANES:(across + 1) * LANES]
                    picked = jnp.sum(jnp.where(sub == s.rows[n * 8 + h + k], part, 0.0), axis=0, keepdims=True)
                    rows = jnp.where(sub == h + k, picked, rows)
            s.back[n] = rows
            return c

        lax.fori_loop(0, tiles // 8, backward, 0, unroll=2)
        back = s.back[...].reshape(LANES, LANES).astype(BF16)
        outgoing = jnp.dot(s.placed_t[...], back, preferred_element_type=F32)
        s.b1_send[it] = outgoing.reshape(NJ, slots, LANES).astype(BF16)
        s.b1_recv[it, j] = s.b1_send[it, j]
        each(j, NJ, lambda jj: start(it, B1, s.b1_send.at[it, jj], s.b1_recv.at[it, j], to_j(jj)))

        if it > 0:
            for cut in cuts:
                m = s.m[:, cut]
                msol[:, cut] = alpha * m if it == 1 else msol[:, cut] + alpha * m
                m = s.x[:, cut] + beta * m
                s.m[:, cut] = m
                curv_m += jnp.sum(s.mdiag[:, cut] * m * m, axis=1, keepdims=True)

        @pl.when(in_jb)
        def _():
            s.r1_recv[it, j] = s.r1_send[it, j]
            arrived(it, R1, s.r1_recv.at[it, pl.ds(0, NJ - 1)])
            part = jnp.sum(s.r1_recv[it], axis=0)
            for b in range(ZB):
                s.r2_send[it, b] = part[:, b * LANES:(b + 1) * LANES]

            def send_r2(b, c):
                @pl.when(b * ZS != z)
                def _():
                    start(it, R2, s.r2_send.at[it, b], s.r2_recv.at[it, z], to_z(b * ZS))

                return c

            lax.fori_loop(0, ZB, send_r2, 0)

        scalar_x(it)

        arrived(it, B1, s.b1_recv.at[it, pl.ds(0, NJ - 1)])
        returned = s.b1_recv[it].reshape(all_slots, LANES)
        summed = jnp.dot(s.pmat_t[...], returned, preferred_element_type=F32)
        s.b2_send[it] = summed.reshape(nz, nb, LANES).astype(BF16)
        s.b2_recv[it, z] = s.b2_send[it, z]
        each(z, nz, lambda zz: start(it, B2, s.b2_send.at[it, zz], s.b2_recv.at[it, z], to_z(zz)))

        @pl.when(in_jb & in_zb)
        def _():
            s.r2_recv[it, z] = s.r2_send[it, lax.div(z, ZS)]
            arrived(it, R2, s.r2_recv.at[it, pl.ds(0, nz - 1)])
            part = jnp.sum(s.r2_recv[it], axis=0)
            s.g1_send[it] = part
            s.g1_recv[it, lax.div(z, ZS)] = part
            each(z, nz, lambda zz: start(it, G1, s.g1_send.at[it], s.g1_recv.at[it, lax.div(z, ZS)], to_z(zz)))

        scalar_y(it, [curv_m] if it > 0 else [curv_m, rho_m])

        arrived(it, B2, s.b2_recv.at[it, pl.ds(0, nz - 1)])
        ped = jnp.sum(s.b2_recv[it].astype(F32), axis=0)
        g_row = jnp.sum(jnp.where(trait_col == y, g, 0.0), axis=0, keepdims=True)
        image = a_diag * z_a + ped + jnp.where(blk == gblk, g_row, 0.0)
        q_a = image if it == 0 else image + beta_y * q_a
        sums = scalar_end(it)
        if it == 0:
            rho = sums[:, 1:2]
        alpha = rho / sums[:, 0:1]
        alpha_y = mine(alpha)
        sol_a = sol_a + alpha_y * u
        r_a = r_a - alpha_y * q_a
        z_a = r_a * a_inv

    s.f_send[0] = sol_a
    s.f_send[1] = r_a
    s.f_recv[y] = s.f_send[...]
    each(y, ny, lambda yy: push(s.f_send, s.f_recv.at[y], s.once_send.at[1], s.once_recv.at[1], to_y(yy)))
    gather_wide(it)
    for cut in cuts:
        msol[:, cut] = msol[:, cut] + alpha * s.m[:, cut]
    gather_end(it)
    for b, cut in enumerate(cuts):
        mres[:, cut] = mres[:, cut] - alpha * marker_image(it, b)
    await_bytes(s.f_recv.at[pl.ds(0, ny - 1)], s.once_recv.at[1])
    for t in range(traits):
        for k in range(nb):
            asol[t:t + 1, k * LANES:(k + 1) * LANES] = s.f_recv[t, 0, k:k + 1, :]
            ares[t:t + 1, k * LANES:(k + 1) * LANES] = s.f_recv[t, 1, k:k + 1, :]

    await_bytes(s.id_recv.at[pl.ds(0, NJ - 1)], s.once_send.at[0])
    await_bytes(s.f_recv.at[pl.ds(0, ny - 1)], s.once_send.at[1])
    for n in range(SUMS):
        for step, ref, count in ((SZ, s.sz_recv, nz - 1), (SX, s.sx_recv, NJ - 1), (SY, s.sy_recv, ny - 1)):
            await_bytes(ref.at[n, pl.ds(0, count)], s.sum_send.at[n, step])
    for it in range(ITERS):
        def gone(stage, ref, count, it=it):
            await_bytes(ref.at[it, pl.ds(0, count)], s.send.at[it, stage])

        for stage, ref, count in ((A1, s.a1_recv, nz - 1), (A2, s.a2_recv, NJ - 1), (B1, s.b1_recv, NJ - 1),
                                  (B2, s.b2_recv, nz - 1), (Y, s.y_recv, ny - 1)):
            gone(stage, ref, count)

        @pl.when(in_jb)
        def _():
            gone(R1, s.r1_recv, JB - 1)
            gone(G2, s.g2_recv, NJ - 1)

            @pl.when(in_zb)
            def _():
                gone(R2, s.r2_recv, ZB - 1)
                gone(G1, s.r2_recv, nz - 1)

            @pl.when(jnp.logical_not(in_zb))
            def _():
                gone(R2, s.r2_recv, ZB)

        @pl.when(jnp.logical_not(in_jb))
        def _():
            gone(R1, s.r1_recv, JB)


def body(animal_rhs, marker_rhs, animal_diagonal, marker_diagonal, marker_scale, genotypes, tile_weights,
         tile_rows, tile_owner, tile_local, tile_count, genotyped_block):
    traits, animals = animal_rhs.shape
    markers = marker_rhs.shape[1]
    tiles = tile_weights.shape[0]
    nz, ny = lax.axis_size(ANIMALS) // NJ, lax.axis_size(SNPS)
    nb, slots = animals // LANES, nz * CAP
    every = NJ * slots
    wide = ZB * LANES

    def f32(*shape):
        return pltpu.VMEM(shape, F32)

    def b16(*shape):
        return pltpu.VMEM(shape, BF16)

    dma = pltpu.SemaphoreType.DMA
    scratch = dict(
        arhs=f32(traits, animals), adiag=f32(nb, LANES), mrhs=f32(traits, markers), mdiag=f32(1, markers),
        mscale=f32(1, markers), owner=pltpu.VMEM((1, tiles), I32), local=pltpu.VMEM((1, tiles), I32),
        rows=pltpu.SMEM((tiles,), I32),
        w=b16(*tile_weights.shape), g=b16(*genotypes.shape),
        placed=b16(LANES, every), placed_t=b16(every, LANES), table=f32(every, LANES),
        pmat=b16(every, nz * nb), pmat_t=b16(nz * nb, every),
        fetched=f32(LANES // 8, 8, LANES), back=f32(LANES // 8, 8, LANES),
        m=f32(traits, markers), q=f32(traits, markers), x=f32(traits, markers),
        m_inv=f32(1, markers),
        id_send=b16(NJ, slots, LANES), id_recv=b16(NJ, slots, LANES),
        a1_send=b16(ITERS, nb, LANES), a1_recv=b16(ITERS, nz, nb, LANES),
        a2_send=b16(ITERS, NJ, slots, LANES), a2_recv=b16(ITERS, NJ, slots, LANES),
        b1_send=b16(ITERS, NJ, slots, LANES), b1_recv=b16(ITERS, NJ, slots, LANES),
        b2_send=b16(ITERS, nz, nb, LANES), b2_recv=b16(ITERS, nz, nb, LANES),
        y_send=f32(ITERS, 8, LANES), y_recv=f32(ITERS, ny, 8, LANES),
        r1_send=f32(ITERS, JB, traits, wide), r1_recv=f32(ITERS, NJ, traits, wide),
        r2_send=f32(ITERS, ZB, traits, LANES), r2_recv=f32(ITERS, nz, traits, LANES),
        g1_send=f32(ITERS, traits, LANES), g1_recv=f32(ITERS, ZB, traits, LANES),
        g2_recv=f32(ITERS, JB, ZB, traits, LANES),
        sz_send=f32(SUMS, 1, LANES), sz_recv=f32(SUMS, nz, 1, LANES),
        sx_send=f32(SUMS, 1, LANES), sx_recv=f32(SUMS, NJ, 1, LANES),
        sy_send=f32(SUMS, traits, LANES), sy_recv=f32(SUMS, ny, traits, LANES),
        f_send=f32(2, nb, LANES), f_recv=f32(ny, 2, nb, LANES),
        get=dma((10,)), once_send=dma((2,)), once_recv=dma((2,)),
        send=dma((ITERS, STAGES)), recv=dma((ITERS, STAGES)),
        sum_send=dma((SUMS, STEPS)), sum_recv=dma((SUMS, STEPS)),
    )

    def run(*refs):
        first = len(refs) - len(scratch)
        kernel(nz, ny, *refs[:first], SimpleNamespace(**dict(zip(scratch, refs[first:]))))

    outs = pl.pallas_call(
        run,
        out_shape=[jax.ShapeDtypeStruct(a.shape, F32) for a in (animal_rhs, marker_rhs, animal_rhs, marker_rhs)],
        in_specs=[pl.BlockSpec(memory_space=pl.ANY)] * 10 + [pl.BlockSpec(memory_space=pltpu.SMEM)] * 2,
        out_specs=[pl.BlockSpec(memory_space=pltpu.VMEM)] * 4,
        scratch_shapes=list(scratch.values()),
        compiler_params=pltpu.CompilerParams(collective_id=0, has_side_effects=True, vmem_limit_bytes=60 * 2**20),
    )(animal_rhs, marker_rhs, animal_diagonal.reshape(nb, LANES), marker_diagonal,
      marker_scale, genotypes, tile_weights, tile_rows, tile_owner.reshape(1, tiles),
      tile_local.reshape(1, tiles), tile_count, genotyped_block)

    def leave(*refs):
        copies = [pltpu.make_async_copy(refs[k], refs[4 + k], refs[8].at[k]) for k in range(4)]
        for copy in copies:
            copy.start()
        for copy in copies:
            copy.wait()

    return pl.pallas_call(
        leave,
        out_shape=[jax.ShapeDtypeStruct(a.shape, F32) for a in outs],
        in_specs=[pl.BlockSpec(memory_space=pl.ANY)] * 4,
        out_specs=[pl.BlockSpec(memory_space=pl.ANY)] * 4,
        scratch_shapes=[dma((4,))],
        compiler_params=pltpu.CompilerParams(vmem_limit_bytes=60 * 2**20),
    )(*outs)


def solution(mesh):
    placed = (P(None, ANIMALS), P(None, SNPS), P(ANIMALS), P(SNPS), P(SNPS), P(ANIMALS, SNPS),
              P(ANIMALS, None, None), P(ANIMALS), P(ANIMALS, None), P(ANIMALS), P(ANIMALS), P(ANIMALS))
    return jax.shard_map(
        body, mesh=mesh, in_specs=placed,
        out_specs=(P(None, ANIMALS), P(None, SNPS), P(None, ANIMALS), P(None, SNPS)), check_vma=False)
```

```python
from types import SimpleNamespace

import jax
import jax.numpy as jnp
from jax import lax
from jax.experimental import pallas as pl
from jax.experimental.pallas import tpu as pltpu
from jax.sharding import PartitionSpec as P

ITERS = 3
CAP = 2
NJ = 8
JB, ZB, ZS = 7, 7, 2
LANES = 128
A1, A2, B1, B2, Y, R1, R2, G1, G2, STAGES = range(10)
SZ, SX, SY, STEPS = range(4)
SUMS = 2 * ITERS - 1
ANIMALS, SNPS = "animals", "snps"
MESH = pl.DeviceIdType.MESH
F32, BF16, I32 = jnp.float32, jnp.bfloat16, jnp.int32


def iota(shape, dim):
    return lax.broadcasted_iota(I32, shape, dim)


def total(x):
    return jnp.sum(jnp.sum(x, axis=1, keepdims=True), axis=0, keepdims=True)


def kernel(nz, ny, arhs_h, mrhs_h, adiag_h, mdiag_h, mscale_h, geno_h, w_h, rows_h, owner_h, local_h, count_s,
           gblk_s, asol, msol, ares, mres, s):
    traits, markers = mrhs_h.shape
    tiles = w_h.shape[0]
    nb = adiag_h.shape[0]
    geno = geno_h.shape[0]
    slots = nz * CAP
    all_slots, dense = NJ * slots, nz * nb
    wide = ZB * LANES
    me, y = lax.axis_index(ANIMALS), lax.axis_index(SNPS)
    z, j = lax.div(me, NJ), lax.rem(me, NJ)
    in_jb = j < JB
    in_zb = (lax.rem(z, ZS) == 0) & (z < ZB * ZS)

    def to_z(zz):
        return {ANIMALS: zz * NJ + j, SNPS: y}

    def to_j(jj):
        return {ANIMALS: z * NJ + jj, SNPS: y}

    def to_y(yy):
        return {ANIMALS: me, SNPS: yy}

    def each(here, count, act):
        half = count // 2
        act(lax.rem(here + half, count))

        def step(d, c):
            act(lax.rem(here + half - d, count))
            act(lax.rem(here + half + d, count))
            return c

        lax.fori_loop(1, half, step, 0)

    def push(src, dst, send, recv, device):
        pltpu.make_async_remote_copy(src_ref=src, dst_ref=dst, send_sem=send, recv_sem=recv,
                                     device_id=device, device_id_type=MESH).start()

    def await_bytes(ref, sem):
        pltpu.make_async_copy(ref, ref, sem).wait()

    barrier = pltpu.get_barrier_semaphore()

    def greet(device):
        pl.semaphore_signal(barrier, inc=1, device_id=device, device_id_type=MESH)

    each(z, nz, lambda zz: greet(to_z(zz)))
    each(j, NJ, lambda jj: greet(to_j(jj)))
    each(y, ny, lambda yy: greet(to_y(yy)))

    pairs = ((arhs_h, s.arhs), (adiag_h, s.adiag), (mrhs_h, s.mrhs), (mdiag_h, s.mdiag.at[0]), (mscale_h, s.mscale.at[0]),
             (owner_h, s.owner), (local_h, s.local), (rows_h, s.rows), (geno_h, s.g), (w_h, s.w))
    gets = [pltpu.make_async_copy(src, dst, s.get.at[k]) for k, (src, dst) in enumerate(pairs)]
    for get in gets:
        get.start()
    gets[0].wait()
    gets[1].wait()

    blk = iota((nb, LANES), 0)
    lane = iota((nb, LANES), 1)
    sub = iota((8, LANES), 0)
    trait_col = iota((traits, 1), 0)
    lane4 = iota((traits, LANES), 1)
    a_diag = s.adiag[...]
    a_inv = 1.0 / a_diag
    r_a = jnp.zeros((nb, LANES), F32)
    for k in range(nb):
        row = jnp.where(trait_col == y, s.arhs[:, k * LANES:(k + 1) * LANES], 0.0)
        r_a = jnp.where(blk == k, jnp.sum(row, axis=0, keepdims=True), r_a)
    z_a = r_a * a_inv
    sol_a = jnp.zeros((nb, LANES), F32)
    gblk = gblk_s[0]
    cuts = [slice(b * wide, (b + 1) * wide) for b in range(JB)]
    col = jnp.zeros((traits, 1), F32)

    def plan():
        own = s.owner[...]
        names = (iota((nz * NJ, tiles), 0) == own).astype(F32)
        before = (iota((tiles, tiles), 0) < iota((tiles, tiles), 1)).astype(F32)
        earlier = jnp.dot(names.astype(BF16), before.astype(BF16), preferred_element_type=F32)
        rank = jnp.sum(names * earlier, axis=0, keepdims=True)
        slot = (lax.rem(own, NJ) * slots + lax.div(own, NJ) * CAP).astype(F32) + rank
        slot = jnp.where(iota((1, tiles), 1) < count_s[0], slot, -1.0)
        hit = (iota((all_slots, tiles), 0).astype(F32) == slot).astype(F32)
        asked = jnp.sum(hit * (s.local[...] + 1).astype(F32), axis=1, keepdims=True)
        asked = jnp.broadcast_to(asked, (all_slots, LANES))
        s.id_send[...] = asked.reshape(NJ, slots, LANES).astype(BF16)
        each(j, NJ, lambda jj: push(s.id_send.at[jj], s.id_recv.at[j], s.once_send.at[0], s.once_recv.at[0], to_j(jj)))
        s.id_recv[j] = s.id_send[j]
        s.table[...] = jnp.zeros_like(s.table)
        s.table[:, :tiles] = hit
        table = s.table[...]
        s.placed_t[...] = table.astype(BF16)
        s.placed[...] = table.T.astype(BF16)
        s.back[...] = jnp.zeros_like(s.back)

    def serve():
        await_bytes(s.id_recv.at[pl.ds(0, NJ - 1)], s.once_recv.at[0])
        ids = s.id_recv[...].astype(F32).reshape(all_slots, LANES)[:, :dense]
        source = lax.div(lax.rem(iota((all_slots, dense), 0), slots), CAP) * nb
        named = iota((all_slots, dense), 1).astype(F32) == source.astype(F32) + ids - 1.0
        pmat = ((ids > 0.5) & named).astype(F32)
        s.pmat[...] = pmat.astype(BF16)
        s.pmat_t[...] = pmat.T.astype(BF16)

    pl.semaphore_wait(barrier, nz + NJ + ny - 3)

    def start(it, stage, src, dst, device):
        push(src, dst, s.send.at[it, stage], s.recv.at[it, stage], device)

    def arrived(it, stage, ref):
        await_bytes(ref, s.recv.at[it, stage])

    def scalar_push(n, step, src, dst, device):
        push(src, dst, s.sum_send.at[n, step], s.sum_recv.at[n, step], device)

    def scalar_z(n, parts):
        row = jnp.zeros((1, LANES), F32)
        for k, part in enumerate(parts):
            row = jnp.where(lane4[:1] == k, total(part), row)
        s.sz_send[n] = row
        s.sz_recv[n, z] = row
        each(z, nz, lambda zz: scalar_push(n, SZ, s.sz_send.at[n], s.sz_recv.at[n, z], to_z(zz)))

    def scalar_x(n):
        await_bytes(s.sz_recv.at[n, pl.ds(0, nz - 1)], s.sum_recv.at[n, SZ])
        row = jnp.sum(s.sz_recv[n], axis=0)
        s.sx_send[n] = row
        s.sx_recv[n, j] = row
        each(j, NJ, lambda jj: scalar_push(n, SX, s.sx_send.at[n], s.sx_recv.at[n, j], to_j(jj)))

    def scalar_y(n, parts):
        await_bytes(s.sx_recv.at[n, pl.ds(0, NJ - 1)], s.sum_recv.at[n, SX])
        row = jnp.sum(s.sx_recv[n], axis=0)
        full = jnp.where(trait_col == y, row, 0.0)
        for k, part in enumerate(parts):
            full += jnp.where(lane4 == k, part, 0.0)
        s.sy_send[n] = full
        s.sy_recv[n, y] = full
        each(y, ny, lambda yy: scalar_push(n, SY, s.sy_send.at[n], s.sy_recv.at[n, y], to_y(yy)))

    def scalar_end(n):
        await_bytes(s.sy_recv.at[n, pl.ds(0, ny - 1)], s.sum_recv.at[n, SY])
        return jnp.sum(s.sy_recv[n], axis=0)

    def mine(col):
        return jnp.sum(jnp.where(trait_col == y, col, 0.0), axis=0, keepdims=True)

    def gather_wide(it):
        @pl.when(in_jb)
        def _():
            @pl.when(in_zb)
            def _():
                arrived(it, G1, s.g1_recv.at[it, pl.ds(0, ZB - 1)])

            @pl.when(jnp.logical_not(in_zb))
            def _():
                arrived(it, G1, s.g1_recv.at[it])

            s.g2_recv[it, j] = s.g1_recv[it]
            each(j, NJ, lambda jj: start(it, G2, s.g1_recv.at[it], s.g2_recv.at[it, j], to_j(jj)))

    def gather_end(it):
        @pl.when(in_jb)
        def _():
            arrived(it, G2, s.g2_recv.at[it, pl.ds(0, JB - 1)])

        @pl.when(jnp.logical_not(in_jb))
        def _():
            arrived(it, G2, s.g2_recv.at[it])

    def marker_image(it, b):
        cut = cuts[b]
        summed = jnp.concatenate([s.g2_recv[it, b, c] for c in range(ZB)], axis=1)
        q_m = s.mdiag[:, cut] * s.x[:, cut] + s.mscale[:, cut] * summed
        return q_m if it == 0 else q_m + beta * s.q[:, cut]

    rho = alpha = beta = None
    for it in range(ITERS):
        last = it == ITERS - 1
        norm = ITERS + it - 1

        s.a1_send[it] = z_a.astype(BF16)
        s.a1_recv[it, z] = s.a1_send[it]
        each(z, nz, lambda zz: start(it, A1, s.a1_send.at[it], s.a1_recv.at[it, z], to_z(zz)))
        if it == 0:
            for get in gets[2:-1]:
                get.wait()
            plan()
            serve()
        else:
            scalar_z(norm, [r_a * z_a])
            gather_wide(it - 1)

        arrived(it, A1, s.a1_recv.at[it, pl.ds(0, nz - 1)])
        blocks = s.a1_recv[it].astype(F32).reshape(dense, LANES).astype(BF16)
        served = jnp.dot(s.pmat[...], blocks, preferred_element_type=F32)
        s.a2_send[it] = served.reshape(NJ, slots, LANES).astype(BF16)
        s.a2_recv[it, j] = s.a2_send[it, j]
        each(j, NJ, lambda jj: start(it, A2, s.a2_send.at[it, jj], s.a2_recv.at[it, j], to_j(jj)))

        if it > 0:
            scalar_x(norm)
            gather_end(it - 1)

        dot_m, curv_m, rho_m = jnp.zeros((traits, geno), F32), col, col
        for b, cut in enumerate(cuts):
            if it == 0:
                m_inv = 1.0 / s.mdiag[:, cut]
                s.m_inv[:, cut] = m_inv
                r_m = s.mrhs[:, cut]
                x_m = r_m * m_inv
                s.m[:, cut] = x_m
                curv_m += jnp.sum(s.mdiag[:, cut] * x_m * x_m, axis=1, keepdims=True)
            else:
                q_m = marker_image(it - 1, b)
                s.q[:, cut] = q_m
                r_m = mres[:, cut] - alpha * q_m
                x_m = r_m * s.m_inv[:, cut]
            mres[:, cut] = r_m
            s.x[:, cut] = x_m
            rho_m += jnp.sum(r_m * x_m, axis=1, keepdims=True)
            mb = (x_m * s.mscale[:, cut]).astype(BF16)
            dot_m += lax.dot_general(mb, s.g[:, cut], (((1,), (1,)), ((), ())), preferred_element_type=F32)
        own_rows = jnp.sum(jnp.where((blk == gblk) & (lane < geno), z_a, 0.0), axis=0, keepdims=True)
        s.y_send[it] = jnp.where(sub == traits, own_rows, 0.0)
        s.y_send[it, :traits, :geno] = dot_m
        s.y_recv[it, y] = s.y_send[it]
        each(y, ny, lambda yy: start(it, Y, s.y_send.at[it], s.y_recv.at[it, y], to_y(yy)))

        if it > 0:
            scalar_y(norm, [rho_m])

        if it == 0:
            gets[-1].wait()
        arrived(it, A2, s.a2_recv.at[it, pl.ds(0, NJ - 1)])
        fetched = s.a2_recv[it].reshape(all_slots, LANES)
        s.fetched[...] = jnp.dot(s.placed[...], fetched, preferred_element_type=F32).reshape(LANES // 8, 8, LANES)

        def four(first):
            w = s.w[pl.ds(first, 4)]
            return jnp.concatenate([w[0:2].reshape(2 * LANES, LANES), w[2:4].reshape(2 * LANES, LANES)], axis=1)

        def forward(n, acc):
            rows = s.fetched[n]
            for h in (0, 4):
                a, b, c, d = [jnp.where(sub == s.rows[n * 8 + h + k], rows[h + k:h + k + 1], 0.0) for k in range(4)]
                left = jnp.concatenate([jnp.concatenate([a, c], axis=1), jnp.concatenate([b, d], axis=1)], axis=0)
                acc += lax.dot_general(left.astype(BF16), four(n * 8 + h), (((1,), (1,)), ((), ())),
                                       preferred_element_type=F32)
            return acc

        acc = lax.fori_loop(0, tiles // 8, forward, jnp.zeros((16, 2 * LANES), F32), unroll=7)
        v = acc[:8, :LANES] + acc[8:, LANES:]

        arrived(it, Y, s.y_recv.at[it, pl.ds(0, ny - 1)])
        g = jnp.zeros((traits, LANES), F32)
        for t in range(ny):
            g += s.y_recv[it, t, :traits, :]
            g += jnp.where(trait_col == t, s.y_recv[it, t, traits:traits + 1, :], 0.0)
        gb = g[:, :geno].astype(BF16)
        for b, cut in enumerate(cuts):
            s.r1_send[it, b] = jnp.dot(gb, s.g[:, cut], preferred_element_type=F32)

        def send_r1(jj):
            @pl.when(jj < JB)
            def _():
                start(it, R1, s.r1_send.at[it, jj], s.r1_recv.at[it, j], to_j(jj))

        each(j, NJ, send_r1)
        if it > 0:
            rho_next = scalar_end(norm)[:, 0:1]
            beta = rho_next / rho
            rho = rho_next
            beta_y = mine(beta)
            u, v_u, g_u = z_a + beta_y * u, v + beta_y * v_u, g + beta * g_u
        else:
            u, v_u, g_u = z_a, v, g
        g_row = jnp.sum(jnp.where(trait_col == y, g_u, 0.0), axis=0, keepdims=True)
        curv_a = a_diag * u * u + v_u * v_u + jnp.where(sub == 0, g_row * g_row, 0.0)
        scalar_z(it, [curv_a] if it > 0 else [curv_a, r_a * z_a])

        zero = jnp.zeros((8, LANES), F32)
        vb = v.astype(BF16).astype(F32)
        twice = jnp.concatenate([jnp.concatenate([vb, zero], axis=1), jnp.concatenate([zero, vb], axis=1)], axis=0)
        twice = twice.astype(BF16)

        def backward(n, c):
            rows = jnp.zeros((8, LANES), F32)
            for h in (0, 4):
                out = jnp.dot(twice, four(n * 8 + h), preferred_element_type=F32)
                for k in range(4):
                    up, across = k % 2, k // 2
                    part = out[8 * up:8 * up + 8, across * LANES:(across + 1) * LANES]
                    picked = jnp.sum(jnp.where(sub == s.rows[n * 8 + h + k], part, 0.0), axis=0, keepdims=True)
                    rows = jnp.where(sub == h + k, picked, rows)
            s.back[n] = rows
            return c

        lax.fori_loop(0, tiles // 8, backward, 0, unroll=7)
        back = s.back[...].reshape(LANES, LANES).astype(BF16)
        outgoing = jnp.dot(s.placed_t[...], back, preferred_element_type=F32)
        s.b1_send[it] = outgoing.reshape(NJ, slots, LANES).astype(BF16)
        s.b1_recv[it, j] = s.b1_send[it, j]
        each(j, NJ, lambda jj: start(it, B1, s.b1_send.at[it, jj], s.b1_recv.at[it, j], to_j(jj)))

        if it > 0:
            for cut in cuts:
                m = s.m[:, cut]
                msol[:, cut] = alpha * m if it == 1 else msol[:, cut] + alpha * m
                m = s.x[:, cut] + beta * m
                s.m[:, cut] = m
                curv_m += jnp.sum(s.mdiag[:, cut] * m * m, axis=1, keepdims=True)

        @pl.when(in_jb)
        def _():
            s.r1_recv[it, j] = s.r1_send[it, j]
            arrived(it, R1, s.r1_recv.at[it, pl.ds(0, NJ - 1)])
            part = jnp.sum(s.r1_recv[it], axis=0)
            for b in range(ZB):
                s.r2_send[it, b] = part[:, b * LANES:(b + 1) * LANES]

            def send_r2(b, c):
                @pl.when(b * ZS != z)
                def _():
                    start(it, R2, s.r2_send.at[it, b], s.r2_recv.at[it, z], to_z(b * ZS))

                return c

            lax.fori_loop(0, ZB, send_r2, 0)

        scalar_x(it)

        arrived(it, B1, s.b1_recv.at[it, pl.ds(0, NJ - 1)])
        returned = s.b1_recv[it].reshape(all_slots, LANES)
        summed = jnp.dot(s.pmat_t[...], returned, preferred_element_type=F32)
        s.b2_send[it] = summed.reshape(nz, nb, LANES).astype(BF16)
        s.b2_recv[it, z] = s.b2_send[it, z]
        each(z, nz, lambda zz: start(it, B2, s.b2_send.at[it, zz], s.b2_recv.at[it, z], to_z(zz)))

        @pl.when(in_jb & in_zb)
        def _():
            s.r2_recv[it, z] = s.r2_send[it, lax.div(z, ZS)]
            arrived(it, R2, s.r2_recv.at[it, pl.ds(0, nz - 1)])
            part = jnp.sum(s.r2_recv[it], axis=0)
            s.g1_send[it] = part
            s.g1_recv[it, lax.div(z, ZS)] = part
            each(z, nz, lambda zz: start(it, G1, s.g1_send.at[it], s.g1_recv.at[it, lax.div(z, ZS)], to_z(zz)))

        scalar_y(it, [curv_m] if it > 0 else [curv_m, rho_m])

        arrived(it, B2, s.b2_recv.at[it, pl.ds(0, nz - 1)])
        ped = jnp.sum(s.b2_recv[it].astype(F32), axis=0)
        g_row = jnp.sum(jnp.where(trait_col == y, g, 0.0), axis=0, keepdims=True)
        image = a_diag * z_a + ped + jnp.where(blk == gblk, g_row, 0.0)
        q_a = image if it == 0 else image + beta_y * q_a
        sums = scalar_end(it)
        if it == 0:
            rho = sums[:, 1:2]
        alpha = rho / sums[:, 0:1]
        alpha_y = mine(alpha)
        sol_a = sol_a + alpha_y * u
        r_a = r_a - alpha_y * q_a
        z_a = r_a * a_inv

    s.f_send[0] = sol_a
    s.f_send[1] = r_a
    s.f_recv[y] = s.f_send[...]
    each(y, ny, lambda yy: push(s.f_send, s.f_recv.at[y], s.once_send.at[1], s.once_recv.at[1], to_y(yy)))
    gather_wide(it)
    for cut in cuts:
        msol[:, cut] = msol[:, cut] + alpha * s.m[:, cut]
    gather_end(it)
    for b, cut in enumerate(cuts):
        mres[:, cut] = mres[:, cut] - alpha * marker_image(it, b)
    await_bytes(s.f_recv.at[pl.ds(0, ny - 1)], s.once_recv.at[1])
    for t in range(traits):
        for k in range(nb):
            asol[t:t + 1, k * LANES:(k + 1) * LANES] = s.f_recv[t, 0, k:k + 1, :]
            ares[t:t + 1, k * LANES:(k + 1) * LANES] = s.f_recv[t, 1, k:k + 1, :]

    await_bytes(s.id_recv.at[pl.ds(0, NJ - 1)], s.once_send.at[0])
    await_bytes(s.f_recv.at[pl.ds(0, ny - 1)], s.once_send.at[1])
    for n in range(SUMS):
        for step, ref, count in ((SZ, s.sz_recv, nz - 1), (SX, s.sx_recv, NJ - 1), (SY, s.sy_recv, ny - 1)):
            await_bytes(ref.at[n, pl.ds(0, count)], s.sum_send.at[n, step])
    for it in range(ITERS):
        def gone(stage, ref, count, it=it):
            await_bytes(ref.at[it, pl.ds(0, count)], s.send.at[it, stage])

        for stage, ref, count in ((A1, s.a1_recv, nz - 1), (A2, s.a2_recv, NJ - 1), (B1, s.b1_recv, NJ - 1),
                                  (B2, s.b2_recv, nz - 1), (Y, s.y_recv, ny - 1)):
            gone(stage, ref, count)

        @pl.when(in_jb)
        def _():
            gone(R1, s.r1_recv, JB - 1)
            gone(G2, s.g2_recv, NJ - 1)

            @pl.when(in_zb)
            def _():
                gone(R2, s.r2_recv, ZB - 1)
                gone(G1, s.r2_recv, nz - 1)

            @pl.when(jnp.logical_not(in_zb))
            def _():
                gone(R2, s.r2_recv, ZB)

        @pl.when(jnp.logical_not(in_jb))
        def _():
            gone(R1, s.r1_recv, JB)


def body(animal_rhs, marker_rhs, animal_diagonal, marker_diagonal, marker_scale, genotypes, tile_weights,
         tile_rows, tile_owner, tile_local, tile_count, genotyped_block):
    traits, animals = animal_rhs.shape
    markers = marker_rhs.shape[1]
    tiles = tile_weights.shape[0]
    nz, ny = lax.axis_size(ANIMALS) // NJ, lax.axis_size(SNPS)
    nb, slots = animals // LANES, nz * CAP
    every = NJ * slots
    wide = ZB * LANES

    def f32(*shape):
        return pltpu.VMEM(shape, F32)

    def b16(*shape):
        return pltpu.VMEM(shape, BF16)

    dma = pltpu.SemaphoreType.DMA
    scratch = dict(
        arhs=f32(traits, animals), adiag=f32(nb, LANES), mrhs=f32(traits, markers), mdiag=f32(1, markers),
        mscale=f32(1, markers), owner=pltpu.VMEM((1, tiles), I32), local=pltpu.VMEM((1, tiles), I32),
        rows=pltpu.SMEM((tiles,), I32),
        w=b16(*tile_weights.shape), g=b16(*genotypes.shape),
        placed=b16(LANES, every), placed_t=b16(every, LANES), table=f32(every, LANES),
        pmat=b16(every, nz * nb), pmat_t=b16(nz * nb, every),
        fetched=f32(LANES // 8, 8, LANES), back=f32(LANES // 8, 8, LANES),
        m=f32(traits, markers), q=f32(traits, markers), x=f32(traits, markers),
        m_inv=f32(1, markers),
        id_send=b16(NJ, slots, LANES), id_recv=b16(NJ, slots, LANES),
        a1_send=b16(ITERS, nb, LANES), a1_recv=b16(ITERS, nz, nb, LANES),
        a2_send=b16(ITERS, NJ, slots, LANES), a2_recv=b16(ITERS, NJ, slots, LANES),
        b1_send=b16(ITERS, NJ, slots, LANES), b1_recv=b16(ITERS, NJ, slots, LANES),
        b2_send=b16(ITERS, nz, nb, LANES), b2_recv=b16(ITERS, nz, nb, LANES),
        y_send=f32(ITERS, 8, LANES), y_recv=f32(ITERS, ny, 8, LANES),
        r1_send=f32(ITERS, JB, traits, wide), r1_recv=f32(ITERS, NJ, traits, wide),
        r2_send=f32(ITERS, ZB, traits, LANES), r2_recv=f32(ITERS, nz, traits, LANES),
        g1_send=f32(ITERS, traits, LANES), g1_recv=f32(ITERS, ZB, traits, LANES),
        g2_recv=f32(ITERS, JB, ZB, traits, LANES),
        sz_send=f32(SUMS, 1, LANES), sz_recv=f32(SUMS, nz, 1, LANES),
        sx_send=f32(SUMS, 1, LANES), sx_recv=f32(SUMS, NJ, 1, LANES),
        sy_send=f32(SUMS, traits, LANES), sy_recv=f32(SUMS, ny, traits, LANES),
        f_send=f32(2, nb, LANES), f_recv=f32(ny, 2, nb, LANES),
        get=dma((10,)), once_send=dma((2,)), once_recv=dma((2,)),
        send=dma((ITERS, STAGES)), recv=dma((ITERS, STAGES)),
        sum_send=dma((SUMS, STEPS)), sum_recv=dma((SUMS, STEPS)),
    )

    def run(*refs):
        first = len(refs) - len(scratch)
        kernel(nz, ny, *refs[:first], SimpleNamespace(**dict(zip(scratch, refs[first:]))))

    outs = pl.pallas_call(
        run,
        out_shape=[jax.ShapeDtypeStruct(a.shape, F32) for a in (animal_rhs, marker_rhs, animal_rhs, marker_rhs)],
        in_specs=[pl.BlockSpec(memory_space=pl.ANY)] * 10 + [pl.BlockSpec(memory_space=pltpu.SMEM)] * 2,
        out_specs=[pl.BlockSpec(memory_space=pltpu.VMEM)] * 4,
        scratch_shapes=list(scratch.values()),
        compiler_params=pltpu.CompilerParams(collective_id=0, has_side_effects=True, vmem_limit_bytes=60 * 2**20),
    )(animal_rhs, marker_rhs, animal_diagonal.reshape(nb, LANES), marker_diagonal,
      marker_scale, genotypes, tile_weights, tile_rows, tile_owner.reshape(1, tiles),
      tile_local.reshape(1, tiles), tile_count, genotyped_block)

    def leave(*refs):
        sources, results, stages, sems = refs[:4], refs[4:8], refs[8:12], refs[12]
        reads = [pltpu.make_async_copy(a, b, sems.at[k]) for k, (a, b) in enumerate(zip(sources, stages))]
        writes = [pltpu.make_async_copy(a, b, sems.at[4 + k]) for k, (a, b) in enumerate(zip(stages, results))]
        for read in reads:
            read.start()
        for read, write in zip(reads, writes):
            read.wait()
            write.start()
        for write in writes:
            write.wait()

    return pl.pallas_call(
        leave,
        out_shape=[jax.ShapeDtypeStruct(a.shape, F32) for a in outs],
        in_specs=[pl.BlockSpec(memory_space=pl.ANY)] * 4,
        out_specs=[pl.BlockSpec(memory_space=pl.ANY)] * 4,
        scratch_shapes=[pltpu.VMEM(a.shape, F32) for a in outs] + [dma((8,))],
        compiler_params=pltpu.CompilerParams(vmem_limit_bytes=60 * 2**20),
    )(*outs)


def solution(mesh):
    placed = (P(None, ANIMALS), P(None, SNPS), P(ANIMALS), P(SNPS), P(SNPS), P(ANIMALS, SNPS),
              P(ANIMALS, None, None), P(ANIMALS), P(ANIMALS, None), P(ANIMALS), P(ANIMALS), P(ANIMALS))
    return jax.shard_map(
        body, mesh=mesh, in_specs=placed,
        out_specs=(P(None, ANIMALS), P(None, SNPS), P(None, ANIMALS), P(None, SNPS)), check_vma=False)
```

```python
from types import SimpleNamespace

import jax
import jax.numpy as jnp
from jax import lax
from jax.experimental import pallas as pl
from jax.experimental.pallas import tpu as pltpu
from jax.sharding import PartitionSpec as P

ITERS = 3
CAP = 2
NJ = 8
JB, ZB, ZS = 7, 7, 2
LANES = 128
A1, A2, B1, B2, Y, R1, R2, G1, G2, STAGES = range(10)
SZ, SX, SY, STEPS = range(4)
SUMS = 2 * ITERS
ANIMALS, SNPS = "animals", "snps"
MESH = pl.DeviceIdType.MESH
F32, BF16, I32 = jnp.float32, jnp.bfloat16, jnp.int32


def iota(shape, dim):
    return lax.broadcasted_iota(I32, shape, dim)


def total(x):
    return jnp.sum(jnp.sum(x, axis=1, keepdims=True), axis=0, keepdims=True)


def kernel(nz, ny, arhs_h, mrhs_h, adiag_h, mdiag_h, mscale_h, geno_h, w_h, rows_h, owner_h, local_h, count_s,
           gblk_s, asol, msol, ares, mres, s):
    traits, markers = mrhs_h.shape
    tiles = w_h.shape[0]
    nb = adiag_h.shape[0]
    geno = geno_h.shape[0]
    slots = nz * CAP
    all_slots, dense = NJ * slots, nz * nb
    wide = ZB * LANES
    me, y = lax.axis_index(ANIMALS), lax.axis_index(SNPS)
    z, j = lax.div(me, NJ), lax.rem(me, NJ)
    in_jb = j < JB
    in_zb = (lax.rem(z, ZS) == 0) & (z < ZB * ZS)

    def to_z(zz):
        return {ANIMALS: zz * NJ + j, SNPS: y}

    def to_j(jj):
        return {ANIMALS: z * NJ + jj, SNPS: y}

    def to_y(yy):
        return {ANIMALS: me, SNPS: yy}

    def others(here, count):
        half = count // 2
        order = [half] + [half + d for k in range(1, half) for d in (-k, k)]
        return [lax.rem(here + d, count) for d in order]

    peers_z, peers_j, peers_y = others(z, nz), others(j, NJ), others(y, ny)

    def each(peers, act):
        for peer in peers:
            act(peer)

    def push(src, dst, send, recv, device):
        pltpu.make_async_remote_copy(src_ref=src, dst_ref=dst, send_sem=send, recv_sem=recv,
                                     device_id=device, device_id_type=MESH).start()

    def await_bytes(ref, sem):
        pltpu.make_async_copy(ref, ref, sem).wait()

    barrier = pltpu.get_barrier_semaphore()

    def greet(device):
        pl.semaphore_signal(barrier, inc=1, device_id=device, device_id_type=MESH)

    each(peers_z, lambda zz: greet(to_z(zz)))
    each(peers_j, lambda jj: greet(to_j(jj)))
    each(peers_y, lambda yy: greet(to_y(yy)))

    pairs = ((arhs_h, s.arhs), (adiag_h, s.adiag), (mrhs_h, s.mrhs), (mdiag_h, s.mdiag.at[0]), (mscale_h, s.mscale.at[0]),
             (owner_h, s.owner), (local_h, s.local), (rows_h, s.rows), (geno_h, s.g), (w_h, s.w))
    gets = [pltpu.make_async_copy(src, dst, s.get.at[k]) for k, (src, dst) in enumerate(pairs)]
    for get in gets:
        get.start()
    gets[0].wait()
    gets[1].wait()

    blk = iota((nb, LANES), 0)
    lane = iota((nb, LANES), 1)
    sub = iota((8, LANES), 0)
    trait_col = iota((traits, 1), 0)
    lane4 = iota((traits, LANES), 1)
    a_diag = s.adiag[...]
    a_inv = 1.0 / a_diag
    r_a = jnp.zeros((nb, LANES), F32)
    for k in range(nb):
        row = jnp.where(trait_col == y, s.arhs[:, k * LANES:(k + 1) * LANES], 0.0)
        r_a = jnp.where(blk == k, jnp.sum(row, axis=0, keepdims=True), r_a)
    gblk = gblk_s[0]
    cuts = [slice(b * wide, (b + 1) * wide) for b in range(JB)]
    col = jnp.zeros((traits, 1), F32)

    def plan():
        own = s.owner[...]
        names = (iota((nz * NJ, tiles), 0) == own).astype(F32)
        before = (iota((tiles, tiles), 0) < iota((tiles, tiles), 1)).astype(F32)
        earlier = jnp.dot(names.astype(BF16), before.astype(BF16), preferred_element_type=F32)
        rank = jnp.sum(names * earlier, axis=0, keepdims=True)
        slot = (lax.rem(own, NJ) * slots + lax.div(own, NJ) * CAP).astype(F32) + rank
        slot = jnp.where(iota((1, tiles), 1) < count_s[0], slot, -1.0)
        hit = (iota((all_slots, tiles), 0).astype(F32) == slot).astype(F32)
        asked = jnp.sum(hit * (s.local[...] + 1).astype(F32), axis=1, keepdims=True)
        asked = jnp.broadcast_to(asked, (all_slots, LANES))
        s.id_send[...] = asked.reshape(NJ, slots, LANES).astype(BF16)
        each(peers_j, lambda jj: push(s.id_send.at[jj], s.id_recv.at[j], s.once_send.at[0], s.once_recv.at[0], to_j(jj)))
        s.id_recv[j] = s.id_send[j]
        s.table[...] = jnp.zeros_like(s.table)
        s.table[:, :tiles] = hit
        table = s.table[...]
        s.placed_t[...] = table.astype(BF16)
        s.placed[...] = table.T.astype(BF16)
        s.back[...] = jnp.zeros_like(s.back)

    def serve():
        await_bytes(s.id_recv.at[pl.ds(0, NJ - 1)], s.once_recv.at[0])
        ids = s.id_recv[...].astype(F32).reshape(all_slots, LANES)[:, :dense]
        source = lax.div(lax.rem(iota((all_slots, dense), 0), slots), CAP) * nb
        named = iota((all_slots, dense), 1).astype(F32) == source.astype(F32) + ids - 1.0
        pmat = ((ids > 0.5) & named).astype(F32)
        s.pmat[...] = pmat.astype(BF16)
        s.pmat_t[...] = pmat.T.astype(BF16)

    def begin():
        for cut in cuts:
            s.m_inv[:, cut] = 1.0 / s.mdiag[:, cut]
            mres[:, cut] = s.mrhs[:, cut]
            for ref in (s.x, s.q, s.m, msol):
                ref[:, cut] = jnp.zeros((traits, wide), F32)
        s.g2_recv[0] = jnp.zeros(s.g2_recv.shape[1:], F32)

    pl.semaphore_wait(barrier, nz + NJ + ny - 3)

    def start(it, stage, src, dst, device):
        push(src, dst, s.send.at[it, stage], s.recv.at[it, stage], device)

    def arrived(it, stage, ref):
        await_bytes(ref, s.recv.at[it, stage])

    def scalar_push(n, step, src, dst, device):
        push(src, dst, s.sum_send.at[n, step], s.sum_recv.at[n, step], device)

    def scalar_z(n, parts):
        row = jnp.zeros((1, LANES), F32)
        for k, part in enumerate(parts):
            row = jnp.where(lane4[:1] == k, total(part), row)
        s.sz_send[n] = row
        s.sz_recv[n, z] = row
        each(peers_z, lambda zz: scalar_push(n, SZ, s.sz_send.at[n], s.sz_recv.at[n, z], to_z(zz)))

    def scalar_x(n):
        await_bytes(s.sz_recv.at[n, pl.ds(0, nz - 1)], s.sum_recv.at[n, SZ])
        row = jnp.sum(s.sz_recv[n], axis=0)
        s.sx_send[n] = row
        s.sx_recv[n, j] = row
        each(peers_j, lambda jj: scalar_push(n, SX, s.sx_send.at[n], s.sx_recv.at[n, j], to_j(jj)))

    def scalar_y(n, parts):
        await_bytes(s.sx_recv.at[n, pl.ds(0, NJ - 1)], s.sum_recv.at[n, SX])
        row = jnp.sum(s.sx_recv[n], axis=0)
        full = jnp.where(trait_col == y, row, 0.0)
        for k, part in enumerate(parts):
            full += jnp.where(lane4 == k, part, 0.0)
        s.sy_send[n] = full
        s.sy_recv[n, y] = full
        each(peers_y, lambda yy: scalar_push(n, SY, s.sy_send.at[n], s.sy_recv.at[n, y], to_y(yy)))

    def scalar_end(n):
        await_bytes(s.sy_recv.at[n, pl.ds(0, ny - 1)], s.sum_recv.at[n, SY])
        return jnp.sum(s.sy_recv[n], axis=0)

    def mine(col):
        return jnp.sum(jnp.where(trait_col == y, col, 0.0), axis=0, keepdims=True)

    def gather_wide(it):
        @pl.when(in_jb)
        def _():
            @pl.when(in_zb)
            def _():
                arrived(it, G1, s.g1_recv.at[it, pl.ds(0, ZB - 1)])

            @pl.when(jnp.logical_not(in_zb))
            def _():
                arrived(it, G1, s.g1_recv.at[it])

            s.g2_recv[it + 1, j] = s.g1_recv[it]
            each(peers_j, lambda jj: start(it, G2, s.g1_recv.at[it], s.g2_recv.at[it + 1, j], to_j(jj)))

    def gather_end(it):
        @pl.when(in_jb)
        def _():
            arrived(it, G2, s.g2_recv.at[it + 1, pl.ds(0, JB - 1)])

        @pl.when(jnp.logical_not(in_jb))
        def _():
            arrived(it, G2, s.g2_recv.at[it + 1])

    def marker_image(n, b, beta):
        cut = cuts[b]
        summed = jnp.concatenate([s.g2_recv[n, b, c] for c in range(ZB)], axis=1)
        return s.mdiag[:, cut] * s.x[:, cut] + s.mscale[:, cut] * summed + beta * s.q[:, cut]

    def iterate(it, held):
        z_a, r_a, q_a, u, sol_a, v_u, g_u, alpha, beta, rho = held
        norm = ITERS + it

        s.a1_send[it] = z_a.astype(BF16)
        s.a1_recv[it, z] = s.a1_send[it]
        each(peers_z, lambda zz: start(it, A1, s.a1_send.at[it], s.a1_recv.at[it, z], to_z(zz)))
        scalar_z(norm, [r_a * z_a])

        @pl.when(it == 0)
        def _():
            for get in gets[2:-1]:
                get.wait()
            plan()
            begin()
            serve()

        @pl.when(it > 0)
        def _():
            gather_wide(it - 1)

        arrived(it, A1, s.a1_recv.at[it, pl.ds(0, nz - 1)])
        blocks = s.a1_recv[it].astype(F32).reshape(dense, LANES).astype(BF16)
        served = jnp.dot(s.pmat[...], blocks, preferred_element_type=F32)
        s.a2_send[it] = served.reshape(NJ, slots, LANES).astype(BF16)
        s.a2_recv[it, j] = s.a2_send[it, j]
        each(peers_j, lambda jj: start(it, A2, s.a2_send.at[it, jj], s.a2_recv.at[it, j], to_j(jj)))

        scalar_x(norm)

        @pl.when(it > 0)
        def _():
            gather_end(it - 1)

        dot_m, curv_m, rho_m = jnp.zeros((traits, geno), F32), col, col
        for b, cut in enumerate(cuts):
            q_m = marker_image(it, b, beta)
            r_m = mres[:, cut] - alpha * q_m
            x_m = r_m * s.m_inv[:, cut]
            s.q[:, cut] = q_m
            mres[:, cut] = r_m
            s.x[:, cut] = x_m
            rho_m += jnp.sum(r_m * x_m, axis=1, keepdims=True)
            mb = (x_m * s.mscale[:, cut]).astype(BF16)
            dot_m += lax.dot_general(mb, s.g[:, cut], (((1,), (1,)), ((), ())), preferred_element_type=F32)
        own_rows = jnp.sum(jnp.where((blk == gblk) & (lane < geno), z_a, 0.0), axis=0, keepdims=True)
        s.y_send[it] = jnp.where(sub == traits, own_rows, 0.0)
        s.y_send[it, :traits, :geno] = dot_m
        s.y_recv[it, y] = s.y_send[it]
        each(peers_y, lambda yy: start(it, Y, s.y_send.at[it], s.y_recv.at[it, y], to_y(yy)))

        scalar_y(norm, [rho_m])

        @pl.when(it == 0)
        def _():
            gets[-1].wait()

        arrived(it, A2, s.a2_recv.at[it, pl.ds(0, NJ - 1)])
        fetched = s.a2_recv[it].reshape(all_slots, LANES)
        s.fetched[...] = jnp.dot(s.placed[...], fetched, preferred_element_type=F32).reshape(LANES // 8, 8, LANES)

        def four(first):
            w = s.w[pl.ds(first, 4)]
            return jnp.concatenate([w[0:2].reshape(2 * LANES, LANES), w[2:4].reshape(2 * LANES, LANES)], axis=1)

        def forward(n, acc):
            rows = s.fetched[n]
            for h in (0, 4):
                a, b, c, d = [jnp.where(sub == s.rows[n * 8 + h + k], rows[h + k:h + k + 1], 0.0) for k in range(4)]
                left = jnp.concatenate([jnp.concatenate([a, c], axis=1), jnp.concatenate([b, d], axis=1)], axis=0)
                acc += lax.dot_general(left.astype(BF16), four(n * 8 + h), (((1,), (1,)), ((), ())),
                                       preferred_element_type=F32)
            return acc

        acc = lax.fori_loop(0, tiles // 8, forward, jnp.zeros((16, 2 * LANES), F32), unroll=True)
        v = acc[:8, :LANES] + acc[8:, LANES:]

        arrived(it, Y, s.y_recv.at[it, pl.ds(0, ny - 1)])
        g = jnp.zeros((traits, LANES), F32)
        for t in range(ny):
            g += s.y_recv[it, t, :traits, :]
            g += jnp.where(trait_col == t, s.y_recv[it, t, traits:traits + 1, :], 0.0)
        gb = g[:, :geno].astype(BF16)
        for b, cut in enumerate(cuts):
            s.r1_send[it, b] = jnp.dot(gb, s.g[:, cut], preferred_element_type=F32)

        def send_r1(jj):
            @pl.when(jj < JB)
            def _():
                start(it, R1, s.r1_send.at[it, jj], s.r1_recv.at[it, j], to_j(jj))

        each(peers_j, send_r1)
        rho_next = scalar_end(norm)[:, 0:1]
        beta = jnp.where(it == 0, 0.0, rho_next / rho)
        beta_y = mine(beta)
        u, v_u, g_u = z_a + beta_y * u, v + beta_y * v_u, g + beta * g_u
        g_row = jnp.sum(jnp.where(trait_col == y, g_u, 0.0), axis=0, keepdims=True)
        scalar_z(it, [a_diag * u * u + v_u * v_u + jnp.where(sub == 0, g_row * g_row, 0.0)])

        zero = jnp.zeros((8, LANES), F32)
        vb = v.astype(BF16).astype(F32)
        twice = jnp.concatenate([jnp.concatenate([vb, zero], axis=1), jnp.concatenate([zero, vb], axis=1)], axis=0)
        twice = twice.astype(BF16)

        def backward(n, c):
            rows = jnp.zeros((8, LANES), F32)
            for h in (0, 4):
                out = jnp.dot(twice, four(n * 8 + h), preferred_element_type=F32)
                for k in range(4):
                    up, across = k % 2, k // 2
                    part = out[8 * up:8 * up + 8, across * LANES:(across + 1) * LANES]
                    picked = jnp.sum(jnp.where(sub == s.rows[n * 8 + h + k], part, 0.0), axis=0, keepdims=True)
                    rows = jnp.where(sub == h + k, picked, rows)
            s.back[n] = rows
            return c

        lax.fori_loop(0, tiles // 8, backward, 0, unroll=True)
        back = s.back[...].reshape(LANES, LANES).astype(BF16)
        outgoing = jnp.dot(s.placed_t[...], back, preferred_element_type=F32)
        s.b1_send[it] = outgoing.reshape(NJ, slots, LANES).astype(BF16)
        s.b1_recv[it, j] = s.b1_send[it, j]
        each(peers_j, lambda jj: start(it, B1, s.b1_send.at[it, jj], s.b1_recv.at[it, j], to_j(jj)))

        for cut in cuts:
            m = s.m[:, cut]
            msol[:, cut] = msol[:, cut] + alpha * m
            m = s.x[:, cut] + beta * m
            s.m[:, cut] = m
            curv_m += jnp.sum(s.mdiag[:, cut] * m * m, axis=1, keepdims=True)

        @pl.when(in_jb)
        def _():
            s.r1_recv[it, j] = s.r1_send[it, j]
            arrived(it, R1, s.r1_recv.at[it, pl.ds(0, NJ - 1)])
            part = jnp.sum(s.r1_recv[it], axis=0)
            for b in range(ZB):
                s.r2_send[it, b] = part[:, b * LANES:(b + 1) * LANES]

            for b in range(ZB):
                @pl.when(b * ZS != z)
                def _(b=b):
                    start(it, R2, s.r2_send.at[it, b], s.r2_recv.at[it, z], to_z(b * ZS))

        scalar_x(it)

        arrived(it, B1, s.b1_recv.at[it, pl.ds(0, NJ - 1)])
        returned = s.b1_recv[it].reshape(all_slots, LANES)
        summed = jnp.dot(s.pmat_t[...], returned, preferred_element_type=F32)
        s.b2_send[it] = summed.reshape(nz, nb, LANES).astype(BF16)
        s.b2_recv[it, z] = s.b2_send[it, z]
        each(peers_z, lambda zz: start(it, B2, s.b2_send.at[it, zz], s.b2_recv.at[it, z], to_z(zz)))

        @pl.when(in_jb & in_zb)
        def _():
            s.r2_recv[it, z] = s.r2_send[it, lax.div(z, ZS)]
            arrived(it, R2, s.r2_recv.at[it, pl.ds(0, nz - 1)])
            part = jnp.sum(s.r2_recv[it], axis=0)
            s.g1_send[it] = part
            s.g1_recv[it, lax.div(z, ZS)] = part
            each(peers_z, lambda zz: start(it, G1, s.g1_send.at[it], s.g1_recv.at[it, lax.div(z, ZS)], to_z(zz)))

        scalar_y(it, [curv_m])

        arrived(it, B2, s.b2_recv.at[it, pl.ds(0, nz - 1)])
        ped = jnp.sum(s.b2_recv[it].astype(F32), axis=0)
        g_row = jnp.sum(jnp.where(trait_col == y, g, 0.0), axis=0, keepdims=True)
        image = a_diag * z_a + ped + jnp.where(blk == gblk, g_row, 0.0)
        q_a = image + beta_y * q_a
        alpha = rho_next / scalar_end(it)[:, 0:1]
        alpha_y = mine(alpha)
        sol_a = sol_a + alpha_y * u
        r_a = r_a - alpha_y * q_a
        return r_a * a_inv, r_a, q_a, u, sol_a, v_u, g_u, alpha, beta, rho_next

    none = jnp.zeros((nb, LANES), F32)
    held = lax.fori_loop(0, ITERS, iterate, (r_a * a_inv, r_a, none, none, none, none, jnp.zeros((traits, LANES), F32),
                                             col, col, jnp.ones((traits, 1), F32)))
    _, r_a, _, _, sol_a, _, _, alpha, beta, _ = held
    last = ITERS - 1
    s.f_send[0] = sol_a
    s.f_send[1] = r_a
    s.f_recv[y] = s.f_send[...]
    each(peers_y, lambda yy: push(s.f_send, s.f_recv.at[y], s.once_send.at[1], s.once_recv.at[1], to_y(yy)))
    gather_wide(last)
    for cut in cuts:
        msol[:, cut] = msol[:, cut] + alpha * s.m[:, cut]
    gather_end(last)
    for b, cut in enumerate(cuts):
        mres[:, cut] = mres[:, cut] - alpha * marker_image(ITERS, b, beta)
    await_bytes(s.f_recv.at[pl.ds(0, ny - 1)], s.once_recv.at[1])
    for t in range(traits):
        for k in range(nb):
            asol[t:t + 1, k * LANES:(k + 1) * LANES] = s.f_recv[t, 0, k:k + 1, :]
            ares[t:t + 1, k * LANES:(k + 1) * LANES] = s.f_recv[t, 1, k:k + 1, :]

    await_bytes(s.id_recv.at[pl.ds(0, NJ - 1)], s.once_send.at[0])
    await_bytes(s.f_recv.at[pl.ds(0, ny - 1)], s.once_send.at[1])
    for n in range(SUMS):
        for step, ref, count in ((SZ, s.sz_recv, nz - 1), (SX, s.sx_recv, NJ - 1), (SY, s.sy_recv, ny - 1)):
            await_bytes(ref.at[n, pl.ds(0, count)], s.sum_send.at[n, step])
    for it in range(ITERS):
        def gone(stage, ref, count, it=it):
            await_bytes(ref.at[it, pl.ds(0, count)], s.send.at[it, stage])

        for stage, ref, count in ((A1, s.a1_recv, nz - 1), (A2, s.a2_recv, NJ - 1), (B1, s.b1_recv, NJ - 1),
                                  (B2, s.b2_recv, nz - 1), (Y, s.y_recv, ny - 1)):
            gone(stage, ref, count)

        @pl.when(in_jb)
        def _():
            gone(R1, s.r1_recv, JB - 1)
            gone(G2, s.g2_recv, NJ - 1)

            @pl.when(in_zb)
            def _():
                gone(R2, s.r2_recv, ZB - 1)
                gone(G1, s.r2_recv, nz - 1)

            @pl.when(jnp.logical_not(in_zb))
            def _():
                gone(R2, s.r2_recv, ZB)

        @pl.when(jnp.logical_not(in_jb))
        def _():
            gone(R1, s.r1_recv, JB)


def body(animal_rhs, marker_rhs, animal_diagonal, marker_diagonal, marker_scale, genotypes, tile_weights,
         tile_rows, tile_owner, tile_local, tile_count, genotyped_block):
    traits, animals = animal_rhs.shape
    markers = marker_rhs.shape[1]
    tiles = tile_weights.shape[0]
    nz, ny = lax.axis_size(ANIMALS) // NJ, lax.axis_size(SNPS)
    nb, slots = animals // LANES, nz * CAP
    every = NJ * slots
    wide = ZB * LANES

    def f32(*shape):
        return pltpu.VMEM(shape, F32)

    def b16(*shape):
        return pltpu.VMEM(shape, BF16)

    dma = pltpu.SemaphoreType.DMA
    scratch = dict(
        arhs=f32(traits, animals), adiag=f32(nb, LANES), mrhs=f32(traits, markers), mdiag=f32(1, markers),
        mscale=f32(1, markers), owner=pltpu.VMEM((1, tiles), I32), local=pltpu.VMEM((1, tiles), I32),
        rows=pltpu.SMEM((tiles,), I32),
        w=b16(*tile_weights.shape), g=b16(*genotypes.shape),
        placed=b16(LANES, every), placed_t=b16(every, LANES), table=f32(every, LANES),
        pmat=b16(every, nz * nb), pmat_t=b16(nz * nb, every),
        fetched=f32(LANES // 8, 8, LANES), back=f32(LANES // 8, 8, LANES),
        m=f32(traits, markers), q=f32(traits, markers), x=f32(traits, markers),
        m_inv=f32(1, markers),
        id_send=b16(NJ, slots, LANES), id_recv=b16(NJ, slots, LANES),
        a1_send=b16(ITERS, nb, LANES), a1_recv=b16(ITERS, nz, nb, LANES),
        a2_send=b16(ITERS, NJ, slots, LANES), a2_recv=b16(ITERS, NJ, slots, LANES),
        b1_send=b16(ITERS, NJ, slots, LANES), b1_recv=b16(ITERS, NJ, slots, LANES),
        b2_send=b16(ITERS, nz, nb, LANES), b2_recv=b16(ITERS, nz, nb, LANES),
        y_send=f32(ITERS, 8, LANES), y_recv=f32(ITERS, ny, 8, LANES),
        r1_send=f32(ITERS, JB, traits, wide), r1_recv=f32(ITERS, NJ, traits, wide),
        r2_send=f32(ITERS, ZB, traits, LANES), r2_recv=f32(ITERS, nz, traits, LANES),
        g1_send=f32(ITERS, traits, LANES), g1_recv=f32(ITERS, ZB, traits, LANES),
        g2_recv=f32(ITERS + 1, JB, ZB, traits, LANES),
        sz_send=f32(SUMS, 1, LANES), sz_recv=f32(SUMS, nz, 1, LANES),
        sx_send=f32(SUMS, 1, LANES), sx_recv=f32(SUMS, NJ, 1, LANES),
        sy_send=f32(SUMS, traits, LANES), sy_recv=f32(SUMS, ny, traits, LANES),
        f_send=f32(2, nb, LANES), f_recv=f32(ny, 2, nb, LANES),
        get=dma((10,)), once_send=dma((2,)), once_recv=dma((2,)),
        send=dma((ITERS, STAGES)), recv=dma((ITERS, STAGES)),
        sum_send=dma((SUMS, STEPS)), sum_recv=dma((SUMS, STEPS)),
    )

    def run(*refs):
        first = len(refs) - len(scratch)
        kernel(nz, ny, *refs[:first], SimpleNamespace(**dict(zip(scratch, refs[first:]))))

    outs = pl.pallas_call(
        run,
        out_shape=[jax.ShapeDtypeStruct(a.shape, F32) for a in (animal_rhs, marker_rhs, animal_rhs, marker_rhs)],
        in_specs=[pl.BlockSpec(memory_space=pl.ANY)] * 10 + [pl.BlockSpec(memory_space=pltpu.SMEM)] * 2,
        out_specs=[pl.BlockSpec(memory_space=pltpu.VMEM)] * 4,
        scratch_shapes=list(scratch.values()),
        compiler_params=pltpu.CompilerParams(collective_id=0, has_side_effects=True, vmem_limit_bytes=60 * 2**20),
    )(animal_rhs, marker_rhs, animal_diagonal.reshape(nb, LANES), marker_diagonal,
      marker_scale, genotypes, tile_weights, tile_rows, tile_owner.reshape(1, tiles),
      tile_local.reshape(1, tiles), tile_count, genotyped_block)

    def leave(*refs):
        sources, results, stages, sems = refs[:4], refs[4:8], refs[8:12], refs[12]
        reads = [pltpu.make_async_copy(a, b, sems.at[k]) for k, (a, b) in enumerate(zip(sources, stages))]
        writes = [pltpu.make_async_copy(a, b, sems.at[4 + k]) for k, (a, b) in enumerate(zip(stages, results))]
        for read in reads:
            read.start()
        for read, write in zip(reads, writes):
            read.wait()
            write.start()
        for write in writes:
            write.wait()

    return pl.pallas_call(
        leave,
        out_shape=[jax.ShapeDtypeStruct(a.shape, F32) for a in outs],
        in_specs=[pl.BlockSpec(memory_space=pl.ANY)] * 4,
        out_specs=[pl.BlockSpec(memory_space=pl.ANY)] * 4,
        scratch_shapes=[pltpu.VMEM(a.shape, F32) for a in outs] + [dma((8,))],
        compiler_params=pltpu.CompilerParams(vmem_limit_bytes=60 * 2**20),
    )(*outs)


def solution(mesh):
    placed = (P(None, ANIMALS), P(None, SNPS), P(ANIMALS), P(SNPS), P(SNPS), P(ANIMALS, SNPS),
              P(ANIMALS, None, None), P(ANIMALS), P(ANIMALS, None), P(ANIMALS), P(ANIMALS), P(ANIMALS))
    return jax.shard_map(
        body, mesh=mesh, in_specs=placed,
        out_specs=(P(None, ANIMALS), P(None, SNPS), P(None, ANIMALS), P(None, SNPS)), check_vma=False)
```

```python
from types import SimpleNamespace

import jax
import jax.numpy as jnp
from jax import lax
from jax.experimental import pallas as pl
from jax.experimental.pallas import tpu as pltpu
from jax.sharding import PartitionSpec as P

ITERS = 3
CAP = 2
NJ = 8
JB, ZB, ZS = 7, 7, 2
LANES = 128
A1, A2, B1, B2, Y, R1, R2, G1, G2, STAGES = range(10)
SZ, SX, SY, STEPS = range(4)
SUMS = 2 * ITERS
ANIMALS, SNPS = "animals", "snps"
MESH = pl.DeviceIdType.MESH
F32, BF16, I32 = jnp.float32, jnp.bfloat16, jnp.int32


def iota(shape, dim):
    return lax.broadcasted_iota(I32, shape, dim)


def total(x):
    return jnp.sum(jnp.sum(x, axis=1, keepdims=True), axis=0, keepdims=True)


def kernel(nz, ny, arhs_h, mrhs_h, adiag_h, mdiag_h, mscale_h, geno_h, w_h, rows_h, owner_h, local_h, count_s,
           gblk_s, asol, msol, ares, mres, s):
    traits, markers = mrhs_h.shape
    tiles = w_h.shape[0]
    nb = adiag_h.shape[0]
    geno = geno_h.shape[0]
    slots = nz * CAP
    all_slots, dense = NJ * slots, nz * nb
    wide = ZB * LANES
    me, y = lax.axis_index(ANIMALS), lax.axis_index(SNPS)
    z, j = lax.div(me, NJ), lax.rem(me, NJ)
    in_jb = j < JB
    in_zb = (lax.rem(z, ZS) == 0) & (z < ZB * ZS)

    def to_z(zz):
        return {ANIMALS: zz * NJ + j, SNPS: y}

    def to_j(jj):
        return {ANIMALS: z * NJ + jj, SNPS: y}

    def to_y(yy):
        return {ANIMALS: me, SNPS: yy}

    def others(here, count):
        half = count // 2
        order = [half] + [half + d for k in range(1, half) for d in (-k, k)]
        return [lax.rem(here + d, count) for d in order]

    peers_z, peers_j, peers_y = others(z, nz), others(j, NJ), others(y, ny)

    def each(peers, act):
        for peer in peers:
            act(peer)

    def push(src, dst, send, recv, device):
        pltpu.make_async_remote_copy(src_ref=src, dst_ref=dst, send_sem=send, recv_sem=recv,
                                     device_id=device, device_id_type=MESH).start()

    def await_bytes(ref, sem):
        pltpu.make_async_copy(ref, ref, sem).wait()

    barrier = pltpu.get_barrier_semaphore()

    def greet(device):
        pl.semaphore_signal(barrier, inc=1, device_id=device, device_id_type=MESH)

    each(peers_z, lambda zz: greet(to_z(zz)))
    each(peers_j, lambda jj: greet(to_j(jj)))
    each(peers_y, lambda yy: greet(to_y(yy)))

    pairs = ((arhs_h, s.arhs), (adiag_h, s.adiag), (mrhs_h, s.mrhs), (mdiag_h, s.mdiag.at[0]), (mscale_h, s.mscale.at[0]),
             (owner_h, s.owner), (local_h, s.local), (rows_h, s.rows),
             (rows_h, s.row_names.at[0]), (geno_h, s.g), (w_h, s.w))
    gets = [pltpu.make_async_copy(src, dst, s.get.at[k]) for k, (src, dst) in enumerate(pairs)]
    for get in gets:
        get.start()
    gets[0].wait()
    gets[1].wait()

    blk = iota((nb, LANES), 0)
    lane = iota((nb, LANES), 1)
    sub = iota((8, LANES), 0)
    trait_col = iota((traits, 1), 0)
    lane4 = iota((traits, LANES), 1)
    a_diag = s.adiag[...]
    a_inv = 1.0 / a_diag
    r_a = jnp.zeros((nb, LANES), F32)
    for k in range(nb):
        row = jnp.where(trait_col == y, s.arhs[:, k * LANES:(k + 1) * LANES], 0.0)
        r_a = jnp.where(blk == k, jnp.sum(row, axis=0, keepdims=True), r_a)
    gblk = gblk_s[0]
    cuts = [slice(b * wide, (b + 1) * wide) for b in range(JB)]
    col = jnp.zeros((traits, 1), F32)

    def plan():
        own = s.owner[...]
        names = (iota((nz * NJ, tiles), 0) == own).astype(F32)
        before = (iota((tiles, tiles), 0) < iota((tiles, tiles), 1)).astype(F32)
        earlier = jnp.dot(names.astype(BF16), before.astype(BF16), preferred_element_type=F32)
        rank = jnp.sum(names * earlier, axis=0, keepdims=True)
        slot = (lax.rem(own, NJ) * slots + lax.div(own, NJ) * CAP).astype(F32) + rank
        slot = jnp.where(iota((1, tiles), 1) < count_s[0], slot, -1.0)
        hit = (iota((all_slots, tiles), 0).astype(F32) == slot).astype(F32)
        asked = jnp.sum(hit * (s.local[...] + 1).astype(F32), axis=1, keepdims=True)
        asked = jnp.broadcast_to(asked, (all_slots, LANES))
        s.id_send[...] = asked.reshape(NJ, slots, LANES).astype(BF16)
        each(peers_j, lambda jj: push(s.id_send.at[jj], s.id_recv.at[j], s.once_send.at[0], s.once_recv.at[0], to_j(jj)))
        s.id_recv[j] = s.id_send[j]
        s.row_hot[...] = jnp.zeros_like(s.row_hot)
        s.row_hot[:, :tiles] = (iota((8, tiles), 0) == s.row_names[...]).astype(F32)
        s.table[...] = jnp.zeros_like(s.table)
        s.table[:, :tiles] = hit
        table = s.table[...]
        s.placed_t[...] = table.astype(BF16)
        s.placed[...] = table.T.astype(BF16)
        s.back[...] = jnp.zeros_like(s.back)

    def serve():
        await_bytes(s.id_recv.at[pl.ds(0, NJ - 1)], s.once_recv.at[0])
        ids = s.id_recv[...].astype(F32).reshape(all_slots, LANES)[:, :dense]
        source = lax.div(lax.rem(iota((all_slots, dense), 0), slots), CAP) * nb
        named = iota((all_slots, dense), 1).astype(F32) == source.astype(F32) + ids - 1.0
        pmat = ((ids > 0.5) & named).astype(F32)
        s.pmat[...] = pmat.astype(BF16)
        s.pmat_t[...] = pmat.T.astype(BF16)

    def begin():
        for cut in cuts:
            s.m_inv[:, cut] = 1.0 / s.mdiag[:, cut]
            mres[:, cut] = s.mrhs[:, cut]
            for ref in (s.x, s.q, s.m, msol):
                ref[:, cut] = jnp.zeros((traits, wide), F32)
        s.g2_recv[0] = jnp.zeros(s.g2_recv.shape[1:], BF16)

    pl.semaphore_wait(barrier, nz + NJ + ny - 3)

    def start(it, stage, src, dst, device):
        push(src, dst, s.send.at[it, stage], s.recv.at[it, stage], device)

    def arrived(it, stage, ref):
        await_bytes(ref, s.recv.at[it, stage])

    def scalar_push(n, step, src, dst, device):
        push(src, dst, s.sum_send.at[n, step], s.sum_recv.at[n, step], device)

    def scalar_z(n, parts):
        row = jnp.zeros((1, LANES), F32)
        for k, part in enumerate(parts):
            row = jnp.where(lane4[:1] == k, total(part), row)
        s.sz_send[n] = row
        s.sz_recv[n, z] = row
        each(peers_z, lambda zz: scalar_push(n, SZ, s.sz_send.at[n], s.sz_recv.at[n, z], to_z(zz)))

    def scalar_x(n):
        await_bytes(s.sz_recv.at[n, pl.ds(0, nz - 1)], s.sum_recv.at[n, SZ])
        row = jnp.sum(s.sz_recv[n], axis=0)
        s.sx_send[n] = row
        s.sx_recv[n, j] = row
        each(peers_j, lambda jj: scalar_push(n, SX, s.sx_send.at[n], s.sx_recv.at[n, j], to_j(jj)))

    def scalar_y(n, parts):
        await_bytes(s.sx_recv.at[n, pl.ds(0, NJ - 1)], s.sum_recv.at[n, SX])
        row = jnp.sum(s.sx_recv[n], axis=0)
        full = jnp.where(trait_col == y, row, 0.0)
        for k, part in enumerate(parts):
            full += jnp.where(lane4 == k, part, 0.0)
        s.sy_send[n] = full
        s.sy_recv[n, y] = full
        each(peers_y, lambda yy: scalar_push(n, SY, s.sy_send.at[n], s.sy_recv.at[n, y], to_y(yy)))

    def scalar_end(n):
        await_bytes(s.sy_recv.at[n, pl.ds(0, ny - 1)], s.sum_recv.at[n, SY])
        return jnp.sum(s.sy_recv[n], axis=0)

    def mine(col):
        return jnp.sum(jnp.where(trait_col == y, col, 0.0), axis=0, keepdims=True)

    def gather_wide(it):
        @pl.when(in_jb)
        def _():
            @pl.when(in_zb)
            def _():
                arrived(it, G1, s.g1_recv.at[it, pl.ds(0, ZB - 1)])

            @pl.when(jnp.logical_not(in_zb))
            def _():
                arrived(it, G1, s.g1_recv.at[it])

            s.g2_recv[it + 1, j] = s.g1_recv[it]
            each(peers_j, lambda jj: start(it, G2, s.g1_recv.at[it], s.g2_recv.at[it + 1, j], to_j(jj)))

    def gather_end(it):
        @pl.when(in_jb)
        def _():
            arrived(it, G2, s.g2_recv.at[it + 1, pl.ds(0, JB - 1)])

        @pl.when(jnp.logical_not(in_jb))
        def _():
            arrived(it, G2, s.g2_recv.at[it + 1])

    def marker_image(n, b, beta):
        cut = cuts[b]
        summed = jnp.concatenate([s.g2_recv[n, b, c].astype(F32) for c in range(ZB)], axis=1)
        return s.mdiag[:, cut] * s.x[:, cut] + s.mscale[:, cut] * summed + beta * s.q[:, cut]

    def iterate(it, held):
        z_a, r_a, q_a, u, sol_a, v_u, g_u, alpha, beta, rho = held
        norm = ITERS + it

        s.a1_send[it] = z_a.astype(BF16)
        s.a1_recv[it, z] = s.a1_send[it]
        each(peers_z, lambda zz: start(it, A1, s.a1_send.at[it], s.a1_recv.at[it, z], to_z(zz)))
        scalar_z(norm, [r_a * z_a])

        @pl.when(it == 0)
        def _():
            for get in gets[2:-1]:
                get.wait()
            plan()
            begin()
            serve()

        @pl.when(it > 0)
        def _():
            gather_wide(it - 1)

        arrived(it, A1, s.a1_recv.at[it, pl.ds(0, nz - 1)])
        blocks = s.a1_recv[it].astype(F32).reshape(dense, LANES).astype(BF16)
        served = jnp.dot(s.pmat[...], blocks, preferred_element_type=F32)
        s.a2_send[it] = served.reshape(NJ, slots, LANES).astype(BF16)
        s.a2_recv[it, j] = s.a2_send[it, j]
        each(peers_j, lambda jj: start(it, A2, s.a2_send.at[it, jj], s.a2_recv.at[it, j], to_j(jj)))

        scalar_x(norm)

        @pl.when(it > 0)
        def _():
            gather_end(it - 1)

        dot_m, curv_m, rho_m = jnp.zeros((traits, geno), F32), col, col
        for b, cut in enumerate(cuts):
            q_m = marker_image(it, b, beta)
            r_m = mres[:, cut] - alpha * q_m
            x_m = r_m * s.m_inv[:, cut]
            s.q[:, cut] = q_m
            mres[:, cut] = r_m
            s.x[:, cut] = x_m
            rho_m += jnp.sum(r_m * x_m, axis=1, keepdims=True)
            mb = (x_m * s.mscale[:, cut]).astype(BF16)
            dot_m += lax.dot_general(mb, s.g[:, cut], (((1,), (1,)), ((), ())), preferred_element_type=F32)
        own_rows = jnp.sum(jnp.where((blk == gblk) & (lane < geno), z_a, 0.0), axis=0, keepdims=True)
        s.y_send[it] = jnp.where(sub == traits, own_rows, 0.0)
        s.y_send[it, :traits, :geno] = dot_m
        s.y_recv[it, y] = s.y_send[it]
        each(peers_y, lambda yy: start(it, Y, s.y_send.at[it], s.y_recv.at[it, y], to_y(yy)))

        scalar_y(norm, [rho_m])

        @pl.when(it == 0)
        def _():
            gets[-1].wait()

        arrived(it, A2, s.a2_recv.at[it, pl.ds(0, NJ - 1)])
        fetched = jnp.dot(s.placed[...], s.a2_recv[it].reshape(all_slots, LANES), preferred_element_type=F32)
        blocks = fetched.T
        zero = jnp.zeros_like(blocks)
        both = jnp.concatenate([jnp.concatenate([blocks, zero], axis=1), jnp.concatenate([zero, blocks], axis=1)], axis=0)
        both = both.astype(BF16)

        def forward(n, acc):
            w = s.w[pl.ds(n * 8, 8)]
            left = jnp.concatenate([w[:4].reshape(4 * LANES, LANES), w[4:].reshape(4 * LANES, LANES)], axis=1)
            out = jnp.dot(left, both, preferred_element_type=F32)
            for k in range(8):
                down, across = k % 4 * LANES, k // 4 * LANES
                acc = jnp.where(column == n * 8 + k, out[down:down + LANES, across:across + LANES], acc)
            return acc

        column = iota((LANES, LANES), 1)
        acc = lax.fori_loop(0, tiles // 8, forward, zero, unroll=2)
        v = jnp.dot(s.row_hot[...], acc.T, preferred_element_type=F32, precision=lax.Precision.HIGHEST)

        arrived(it, Y, s.y_recv.at[it, pl.ds(0, ny - 1)])
        g = jnp.zeros((traits, LANES), F32)
        for t in range(ny):
            g += s.y_recv[it, t, :traits, :]
            g += jnp.where(trait_col == t, s.y_recv[it, t, traits:traits + 1, :], 0.0)
        gb = g[:, :geno].astype(BF16)
        for b, cut in enumerate(cuts):
            s.r1_send[it, b] = jnp.dot(gb, s.g[:, cut], preferred_element_type=F32).astype(BF16)

        def send_r1(jj):
            @pl.when(jj < JB)
            def _():
                start(it, R1, s.r1_send.at[it, jj], s.r1_recv.at[it, j], to_j(jj))

        each(peers_j, send_r1)
        rho_next = scalar_end(norm)[:, 0:1]
        beta = jnp.where(it == 0, 0.0, rho_next / rho)
        beta_y = mine(beta)
        u, v_u, g_u = z_a + beta_y * u, v + beta_y * v_u, g + beta * g_u
        g_row = jnp.sum(jnp.where(trait_col == y, g_u, 0.0), axis=0, keepdims=True)
        scalar_z(it, [a_diag * u * u + v_u * v_u + jnp.where(sub == 0, g_row * g_row, 0.0)])

        zero = jnp.zeros((8, LANES), F32)
        vb = v.astype(BF16).astype(F32)
        twice = jnp.concatenate([jnp.concatenate([vb, zero], axis=1), jnp.concatenate([zero, vb], axis=1)], axis=0)
        twice = twice.astype(BF16)

        def four(first):
            w = s.w[pl.ds(first, 4)]
            return jnp.concatenate([w[0:2].reshape(2 * LANES, LANES), w[2:4].reshape(2 * LANES, LANES)], axis=1)

        def backward(n, c):
            rows = jnp.zeros((8, LANES), F32)
            for h in (0, 4):
                out = jnp.dot(twice, four(n * 8 + h), preferred_element_type=F32)
                for k in range(4):
                    up, across = k % 2, k // 2
                    part = out[8 * up:8 * up + 8, across * LANES:(across + 1) * LANES]
                    picked = jnp.sum(jnp.where(sub == s.rows[n * 8 + h + k], part, 0.0), axis=0, keepdims=True)
                    rows = jnp.where(sub == h + k, picked, rows)
            s.back[n] = rows
            return c

        lax.fori_loop(0, tiles // 8, backward, 0, unroll=True)
        back = s.back[...].reshape(LANES, LANES).astype(BF16)
        outgoing = jnp.dot(s.placed_t[...], back, preferred_element_type=F32)
        s.b1_send[it] = outgoing.reshape(NJ, slots, LANES).astype(BF16)
        s.b1_recv[it, j] = s.b1_send[it, j]
        each(peers_j, lambda jj: start(it, B1, s.b1_send.at[it, jj], s.b1_recv.at[it, j], to_j(jj)))

        for cut in cuts:
            m = s.m[:, cut]
            msol[:, cut] = msol[:, cut] + alpha * m
            m = s.x[:, cut] + beta * m
            s.m[:, cut] = m
            curv_m += jnp.sum(s.mdiag[:, cut] * m * m, axis=1, keepdims=True)

        @pl.when(in_jb)
        def _():
            s.r1_recv[it, j] = s.r1_send[it, j]
            arrived(it, R1, s.r1_recv.at[it, pl.ds(0, NJ - 1)])
            part = jnp.sum(s.r1_recv[it].astype(F32), axis=0)
            for b in range(ZB):
                s.r2_send[it, b] = part[:, b * LANES:(b + 1) * LANES]

            for b in range(ZB):
                @pl.when(b * ZS != z)
                def _(b=b):
                    start(it, R2, s.r2_send.at[it, b], s.r2_recv.at[it, z], to_z(b * ZS))

        scalar_x(it)

        arrived(it, B1, s.b1_recv.at[it, pl.ds(0, NJ - 1)])
        returned = s.b1_recv[it].reshape(all_slots, LANES)
        summed = jnp.dot(s.pmat_t[...], returned, preferred_element_type=F32)
        s.b2_send[it] = summed.reshape(nz, nb, LANES).astype(BF16)
        s.b2_recv[it, z] = s.b2_send[it, z]
        each(peers_z, lambda zz: start(it, B2, s.b2_send.at[it, zz], s.b2_recv.at[it, z], to_z(zz)))

        @pl.when(in_jb & in_zb)
        def _():
            s.r2_recv[it, z] = s.r2_send[it, lax.div(z, ZS)]
            arrived(it, R2, s.r2_recv.at[it, pl.ds(0, nz - 1)])
            part = jnp.sum(s.r2_recv[it], axis=0).astype(BF16)
            s.g1_send[it] = part
            s.g1_recv[it, lax.div(z, ZS)] = part
            each(peers_z, lambda zz: start(it, G1, s.g1_send.at[it], s.g1_recv.at[it, lax.div(z, ZS)], to_z(zz)))

        scalar_y(it, [curv_m])

        arrived(it, B2, s.b2_recv.at[it, pl.ds(0, nz - 1)])
        ped = jnp.sum(s.b2_recv[it].astype(F32), axis=0)
        g_row = jnp.sum(jnp.where(trait_col == y, g, 0.0), axis=0, keepdims=True)
        image = a_diag * z_a + ped + jnp.where(blk == gblk, g_row, 0.0)
        q_a = image + beta_y * q_a
        alpha = rho_next / scalar_end(it)[:, 0:1]
        alpha_y = mine(alpha)
        sol_a = sol_a + alpha_y * u
        r_a = r_a - alpha_y * q_a
        return r_a * a_inv, r_a, q_a, u, sol_a, v_u, g_u, alpha, beta, rho_next

    none = jnp.zeros((nb, LANES), F32)
    held = lax.fori_loop(0, ITERS, iterate, (r_a * a_inv, r_a, none, none, none, none, jnp.zeros((traits, LANES), F32),
                                             col, col, jnp.ones((traits, 1), F32)), unroll=True)
    _, r_a, _, _, sol_a, _, _, alpha, beta, _ = held
    last = ITERS - 1
    s.f_send[0] = sol_a
    s.f_send[1] = r_a
    s.f_recv[y] = s.f_send[...]
    each(peers_y, lambda yy: push(s.f_send, s.f_recv.at[y], s.once_send.at[1], s.once_recv.at[1], to_y(yy)))
    gather_wide(last)
    for cut in cuts:
        msol[:, cut] = msol[:, cut] + alpha * s.m[:, cut]
    gather_end(last)
    for b, cut in enumerate(cuts):
        mres[:, cut] = mres[:, cut] - alpha * marker_image(ITERS, b, beta)
    await_bytes(s.f_recv.at[pl.ds(0, ny - 1)], s.once_recv.at[1])
    for t in range(traits):
        for k in range(nb):
            asol[t:t + 1, k * LANES:(k + 1) * LANES] = s.f_recv[t, 0, k:k + 1, :]
            ares[t:t + 1, k * LANES:(k + 1) * LANES] = s.f_recv[t, 1, k:k + 1, :]

    await_bytes(s.id_recv.at[pl.ds(0, NJ - 1)], s.once_send.at[0])
    await_bytes(s.f_recv.at[pl.ds(0, ny - 1)], s.once_send.at[1])
    for n in range(SUMS):
        for step, ref, count in ((SZ, s.sz_recv, nz - 1), (SX, s.sx_recv, NJ - 1), (SY, s.sy_recv, ny - 1)):
            await_bytes(ref.at[n, pl.ds(0, count)], s.sum_send.at[n, step])
    for it in range(ITERS):
        def gone(stage, ref, count, it=it):
            await_bytes(ref.at[it, pl.ds(0, count)], s.send.at[it, stage])

        for stage, ref, count in ((A1, s.a1_recv, nz - 1), (A2, s.a2_recv, NJ - 1), (B1, s.b1_recv, NJ - 1),
                                  (B2, s.b2_recv, nz - 1), (Y, s.y_recv, ny - 1)):
            gone(stage, ref, count)

        @pl.when(in_jb)
        def _():
            gone(R1, s.r1_recv, JB - 1)
            gone(G2, s.g2_recv, NJ - 1)

            @pl.when(in_zb)
            def _():
                gone(R2, s.r2_recv, ZB - 1)
                gone(G1, s.g1_gone, nz - 1)

            @pl.when(jnp.logical_not(in_zb))
            def _():
                gone(R2, s.r2_recv, ZB)

        @pl.when(jnp.logical_not(in_jb))
        def _():
            gone(R1, s.r1_recv, JB)


def body(animal_rhs, marker_rhs, animal_diagonal, marker_diagonal, marker_scale, genotypes, tile_weights,
         tile_rows, tile_owner, tile_local, tile_count, genotyped_block):
    traits, animals = animal_rhs.shape
    markers = marker_rhs.shape[1]
    tiles = tile_weights.shape[0]
    nz, ny = lax.axis_size(ANIMALS) // NJ, lax.axis_size(SNPS)
    nb, slots = animals // LANES, nz * CAP
    every = NJ * slots
    wide = ZB * LANES

    def f32(*shape):
        return pltpu.VMEM(shape, F32)

    def b16(*shape):
        return pltpu.VMEM(shape, BF16)

    dma = pltpu.SemaphoreType.DMA
    scratch = dict(
        arhs=f32(traits, animals), adiag=f32(nb, LANES), mrhs=f32(traits, markers), mdiag=f32(1, markers),
        mscale=f32(1, markers), owner=pltpu.VMEM((1, tiles), I32), local=pltpu.VMEM((1, tiles), I32),
        rows=pltpu.SMEM((tiles,), I32),
        w=b16(*tile_weights.shape), g=b16(*genotypes.shape),
        placed=b16(LANES, every), placed_t=b16(every, LANES), table=f32(every, LANES),
        pmat=b16(every, nz * nb), pmat_t=b16(nz * nb, every),
        row_names=pltpu.VMEM((1, tiles), I32), row_hot=f32(8, LANES), back=f32(LANES // 8, 8, LANES),
        m=f32(traits, markers), q=f32(traits, markers), x=f32(traits, markers),
        m_inv=f32(1, markers),
        id_send=b16(NJ, slots, LANES), id_recv=b16(NJ, slots, LANES),
        a1_send=b16(ITERS, nb, LANES), a1_recv=b16(ITERS, nz, nb, LANES),
        a2_send=b16(ITERS, NJ, slots, LANES), a2_recv=b16(ITERS, NJ, slots, LANES),
        b1_send=b16(ITERS, NJ, slots, LANES), b1_recv=b16(ITERS, NJ, slots, LANES),
        b2_send=b16(ITERS, nz, nb, LANES), b2_recv=b16(ITERS, nz, nb, LANES),
        y_send=f32(ITERS, 8, LANES), y_recv=f32(ITERS, ny, 8, LANES),
        r1_send=b16(ITERS, JB, traits, wide), r1_recv=b16(ITERS, NJ, traits, wide),
        r2_send=f32(ITERS, ZB, traits, LANES), r2_recv=f32(ITERS, nz, traits, LANES),
        g1_send=b16(ITERS, traits, LANES), g1_recv=b16(ITERS, ZB, traits, LANES),
        g2_recv=b16(ITERS + 1, JB, ZB, traits, LANES),
        sz_send=f32(SUMS, 1, LANES), sz_recv=f32(SUMS, nz, 1, LANES),
        sx_send=f32(SUMS, 1, LANES), sx_recv=f32(SUMS, NJ, 1, LANES),
        sy_send=f32(SUMS, traits, LANES), sy_recv=f32(SUMS, ny, traits, LANES),
        g1_gone=b16(ITERS, nz, traits, LANES), f_send=f32(2, nb, LANES), f_recv=f32(ny, 2, nb, LANES),
        get=dma((11,)), once_send=dma((2,)), once_recv=dma((2,)),
        send=dma((ITERS, STAGES)), recv=dma((ITERS, STAGES)),
        sum_send=dma((SUMS, STEPS)), sum_recv=dma((SUMS, STEPS)),
    )

    def run(*refs):
        first = len(refs) - len(scratch)
        kernel(nz, ny, *refs[:first], SimpleNamespace(**dict(zip(scratch, refs[first:]))))

    outs = pl.pallas_call(
        run,
        out_shape=[jax.ShapeDtypeStruct(a.shape, F32) for a in (animal_rhs, marker_rhs, animal_rhs, marker_rhs)],
        in_specs=[pl.BlockSpec(memory_space=pl.ANY)] * 10 + [pl.BlockSpec(memory_space=pltpu.SMEM)] * 2,
        out_specs=[pl.BlockSpec(memory_space=pltpu.VMEM)] * 4,
        scratch_shapes=list(scratch.values()),
        compiler_params=pltpu.CompilerParams(collective_id=0, has_side_effects=True, vmem_limit_bytes=60 * 2**20),
    )(animal_rhs, marker_rhs, animal_diagonal.reshape(nb, LANES), marker_diagonal,
      marker_scale, genotypes, tile_weights, tile_rows, tile_owner.reshape(1, tiles),
      tile_local.reshape(1, tiles), tile_count, genotyped_block)

    def leave(*refs):
        sources, results, stages, sems = refs[:4], refs[4:8], refs[8:12], refs[12]
        reads = [pltpu.make_async_copy(a, b, sems.at[k]) for k, (a, b) in enumerate(zip(sources, stages))]
        writes = [pltpu.make_async_copy(a, b, sems.at[4 + k]) for k, (a, b) in enumerate(zip(stages, results))]
        for read in reads:
            read.start()
        for read, write in zip(reads, writes):
            read.wait()
            write.start()
        for write in writes:
            write.wait()

    return pl.pallas_call(
        leave,
        out_shape=[jax.ShapeDtypeStruct(a.shape, F32) for a in outs],
        in_specs=[pl.BlockSpec(memory_space=pl.ANY)] * 4,
        out_specs=[pl.BlockSpec(memory_space=pl.ANY)] * 4,
        scratch_shapes=[pltpu.VMEM(a.shape, F32) for a in outs] + [dma((8,))],
        compiler_params=pltpu.CompilerParams(vmem_limit_bytes=60 * 2**20),
    )(*outs)


def solution(mesh):
    placed = (P(None, ANIMALS), P(None, SNPS), P(ANIMALS), P(SNPS), P(SNPS), P(ANIMALS, SNPS),
              P(ANIMALS, None, None), P(ANIMALS), P(ANIMALS, None), P(ANIMALS), P(ANIMALS), P(ANIMALS))
    return jax.shard_map(
        body, mesh=mesh, in_specs=placed,
        out_specs=(P(None, ANIMALS), P(None, SNPS), P(None, ANIMALS), P(None, SNPS)), check_vma=False)
```

```python
from types import SimpleNamespace

import jax
import jax.numpy as jnp
from jax import lax
from jax.experimental import pallas as pl
from jax.experimental.pallas import tpu as pltpu
from jax.sharding import PartitionSpec as P

ITERS = 3
CAP = 2
NJ = 8
JB, ZB, ZS = 7, 7, 2
LANES = 128
A1, A2, B1, B2, Y, R1, R2, G1, G2, STAGES = range(10)
SZ, SX, SY, STEPS = range(4)
ANIMALS, SNPS = "animals", "snps"
MESH = pl.DeviceIdType.MESH
F32, BF16, I32 = jnp.float32, jnp.bfloat16, jnp.int32


def iota(shape, dim):
    return lax.broadcasted_iota(I32, shape, dim)


def total(x):
    return jnp.sum(jnp.sum(x, axis=1, keepdims=True), axis=0, keepdims=True)


def kernel(nz, ny, arhs_h, mrhs_h, adiag_h, mdiag_h, mscale_h, geno_h, w_h, rows_h, owner_h, local_h, count_s,
           gblk_s, asol, msol, ares, mres, s):
    traits, markers = mrhs_h.shape
    tiles = w_h.shape[0]
    nb = adiag_h.shape[0]
    geno = geno_h.shape[0]
    slots = nz * CAP
    all_slots, dense = NJ * slots, nz * nb
    wide = ZB * LANES
    me, y = lax.axis_index(ANIMALS), lax.axis_index(SNPS)
    z, j = lax.div(me, NJ), lax.rem(me, NJ)
    in_jb = j < JB
    in_zb = (lax.rem(z, ZS) == 0) & (z < ZB * ZS)

    def to_z(zz):
        return {ANIMALS: zz * NJ + j, SNPS: y}

    def to_j(jj):
        return {ANIMALS: z * NJ + jj, SNPS: y}

    def to_y(yy):
        return {ANIMALS: me, SNPS: yy}

    def others(here, count):
        half = count // 2
        order = [half] + [half + d for k in range(1, half) for d in (-k, k)]
        return [lax.rem(here + d, count) for d in order]

    peers_z, peers_j, peers_y = others(z, nz), others(j, NJ), others(y, ny)

    def each(peers, act):
        for peer in peers:
            act(peer)

    def push(src, dst, send, recv, device):
        pltpu.make_async_remote_copy(src_ref=src, dst_ref=dst, send_sem=send, recv_sem=recv,
                                     device_id=device, device_id_type=MESH).start()

    def await_bytes(ref, sem):
        pltpu.make_async_copy(ref, ref, sem).wait()

    barrier = pltpu.get_barrier_semaphore()

    def greet(device):
        pl.semaphore_signal(barrier, inc=1, device_id=device, device_id_type=MESH)

    each(peers_z, lambda zz: greet(to_z(zz)))
    each(peers_j, lambda jj: greet(to_j(jj)))
    each(peers_y, lambda yy: greet(to_y(yy)))

    pairs = ((arhs_h, s.arhs), (adiag_h, s.adiag), (mrhs_h, s.mrhs), (mdiag_h, s.mdiag.at[0]), (mscale_h, s.mscale.at[0]),
             (owner_h, s.owner), (local_h, s.local), (rows_h, s.rows), (geno_h, s.g), (w_h, s.w))
    gets = [pltpu.make_async_copy(src, dst, s.get.at[k]) for k, (src, dst) in enumerate(pairs)]
    for get in gets:
        get.start()
    gets[0].wait()
    gets[1].wait()

    blk = iota((nb, LANES), 0)
    lane = iota((nb, LANES), 1)
    sub = iota((8, LANES), 0)
    trait_col = iota((traits, 1), 0)
    lane4 = iota((traits, LANES), 1)
    a_diag = s.adiag[...]
    a_inv = 1.0 / a_diag
    r_a = jnp.zeros((nb, LANES), F32)
    for k in range(nb):
        row = jnp.where(trait_col == y, s.arhs[:, k * LANES:(k + 1) * LANES], 0.0)
        r_a = jnp.where(blk == k, jnp.sum(row, axis=0, keepdims=True), r_a)
    gblk = gblk_s[0]
    cuts = [slice(b * wide, (b + 1) * wide) for b in range(JB)]
    col = jnp.zeros((traits, 1), F32)

    def plan():
        own = s.owner[...]
        names = (iota((nz * NJ, tiles), 0) == own).astype(F32)
        before = (iota((tiles, tiles), 0) < iota((tiles, tiles), 1)).astype(F32)
        earlier = jnp.dot(names.astype(BF16), before.astype(BF16), preferred_element_type=F32)
        rank = jnp.sum(names * earlier, axis=0, keepdims=True)
        slot = (lax.rem(own, NJ) * slots + lax.div(own, NJ) * CAP).astype(F32) + rank
        slot = jnp.where(iota((1, tiles), 1) < count_s[0], slot, -1.0)
        hit = (iota((all_slots, tiles), 0).astype(F32) == slot).astype(F32)
        asked = jnp.sum(hit * (s.local[...] + 1).astype(F32), axis=1, keepdims=True)
        asked = jnp.broadcast_to(asked, (all_slots, LANES))
        s.id_send[...] = asked.reshape(NJ, slots, LANES).astype(BF16)
        each(peers_j, lambda jj: push(s.id_send.at[jj], s.id_recv.at[j], s.once_send.at[0], s.once_recv.at[0], to_j(jj)))
        s.id_recv[j] = s.id_send[j]
        s.table[...] = jnp.zeros_like(s.table)
        s.table[:, :tiles] = hit
        table = s.table[...]
        s.placed_t[...] = table.astype(BF16)
        s.placed[...] = table.T.astype(BF16)
        s.back[...] = jnp.zeros_like(s.back)

    def serve():
        await_bytes(s.id_recv.at[pl.ds(0, NJ - 1)], s.once_recv.at[0])
        ids = s.id_recv[...].astype(F32).reshape(all_slots, LANES)[:, :dense]
        source = lax.div(lax.rem(iota((all_slots, dense), 0), slots), CAP) * nb
        named = iota((all_slots, dense), 1).astype(F32) == source.astype(F32) + ids - 1.0
        pmat = ((ids > 0.5) & named).astype(F32)
        s.pmat[...] = pmat.astype(BF16)
        s.pmat_t[...] = pmat.T.astype(BF16)

    def begin():
        for cut in cuts:
            s.m_inv[:, cut] = 1.0 / s.mdiag[:, cut]
            mres[:, cut] = s.mrhs[:, cut]
            for ref in (s.x, s.q, s.m, msol):
                ref[:, cut] = jnp.zeros((traits, wide), F32)
        s.g2_recv[0] = jnp.zeros(s.g2_recv.shape[1:], BF16)

    pl.semaphore_wait(barrier, nz + NJ + ny - 3)

    def start(it, stage, src, dst, device):
        push(src, dst, s.send.at[it, stage], s.recv.at[it, stage], device)

    def arrived(it, stage, ref):
        await_bytes(ref, s.recv.at[it, stage])

    def scalar_push(n, step, src, dst, device):
        push(src, dst, s.sum_send.at[n, step], s.sum_recv.at[n, step], device)

    def scalar_z(n, parts):
        row = jnp.zeros((1, LANES), F32)
        for k, part in enumerate(parts):
            row = jnp.where(lane4[:1] == k, total(part), row)
        s.sz_send[n] = row
        s.sz_recv[n, z] = row
        each(peers_z, lambda zz: scalar_push(n, SZ, s.sz_send.at[n], s.sz_recv.at[n, z], to_z(zz)))

    def scalar_x(n):
        await_bytes(s.sz_recv.at[n, pl.ds(0, nz - 1)], s.sum_recv.at[n, SZ])
        row = jnp.sum(s.sz_recv[n], axis=0)
        s.sx_send[n] = row
        s.sx_recv[n, j] = row
        each(peers_j, lambda jj: scalar_push(n, SX, s.sx_send.at[n], s.sx_recv.at[n, j], to_j(jj)))

    def scalar_y(n, parts):
        await_bytes(s.sx_recv.at[n, pl.ds(0, NJ - 1)], s.sum_recv.at[n, SX])
        row = jnp.sum(s.sx_recv[n], axis=0)
        full = jnp.where(trait_col == y, row, 0.0)
        for k, part in enumerate(parts):
            full += jnp.where(lane4 == k, part, 0.0)
        s.sy_send[n] = full
        s.sy_recv[n, y] = full
        each(peers_y, lambda yy: scalar_push(n, SY, s.sy_send.at[n], s.sy_recv.at[n, y], to_y(yy)))

    def scalar_end(n):
        await_bytes(s.sy_recv.at[n, pl.ds(0, ny - 1)], s.sum_recv.at[n, SY])
        return jnp.sum(s.sy_recv[n], axis=0)

    def mine(col):
        return jnp.sum(jnp.where(trait_col == y, col, 0.0), axis=0, keepdims=True)

    def gather_wide(it):
        @pl.when(in_jb)
        def _():
            @pl.when(in_zb)
            def _():
                arrived(it, G1, s.g1_recv.at[it, pl.ds(0, ZB - 1)])

            @pl.when(jnp.logical_not(in_zb))
            def _():
                arrived(it, G1, s.g1_recv.at[it])

            s.g2_recv[it + 1, j] = s.g1_recv[it]
            each(peers_j, lambda jj: start(it, G2, s.g1_recv.at[it], s.g2_recv.at[it + 1, j], to_j(jj)))

    def gather_end(it):
        @pl.when(in_jb)
        def _():
            arrived(it, G2, s.g2_recv.at[it + 1, pl.ds(0, JB - 1)])

        @pl.when(jnp.logical_not(in_jb))
        def _():
            arrived(it, G2, s.g2_recv.at[it + 1])

    def marker_step(n, b, alpha, beta):
        cut = cuts[b]
        m = s.x[:, cut] + beta * s.m[:, cut]
        s.m[:, cut] = m
        msol[:, cut] = msol[:, cut] + alpha * m
        summed = jnp.concatenate([s.g2_recv[n, b, c].astype(F32) for c in range(ZB)], axis=1)
        q_m = s.mdiag[:, cut] * s.x[:, cut] + s.mscale[:, cut] * summed + beta * s.q[:, cut]
        s.q[:, cut] = q_m
        r_m = mres[:, cut] - alpha * q_m
        mres[:, cut] = r_m
        return cut, q_m, r_m

    def iterate(it, held):
        z_a, r_a, q_a, u, sol_a, alpha, beta, rho, curv = held

        s.a1_send[it] = z_a.astype(BF16)
        s.a1_recv[it, z] = s.a1_send[it]
        each(peers_z, lambda zz: start(it, A1, s.a1_send.at[it], s.a1_recv.at[it, z], to_z(zz)))

        @pl.when(it == 0)
        def _():
            for get in gets[2:-1]:
                get.wait()
            plan()
            begin()
            serve()

        @pl.when(it > 0)
        def _():
            gather_wide(it - 1)

        arrived(it, A1, s.a1_recv.at[it, pl.ds(0, nz - 1)])
        blocks = s.a1_recv[it].astype(F32).reshape(dense, LANES).astype(BF16)
        served = jnp.dot(s.pmat[...], blocks, preferred_element_type=F32)
        s.a2_send[it] = served.reshape(NJ, slots, LANES).astype(BF16)
        s.a2_recv[it, j] = s.a2_send[it, j]
        each(peers_j, lambda jj: start(it, A2, s.a2_send.at[it, jj], s.a2_recv.at[it, j], to_j(jj)))

        @pl.when(it > 0)
        def _():
            gather_end(it - 1)

        dot_m, rho_m, eta_m, delta_m = jnp.zeros((traits, geno), F32), col, col, col
        for b in range(JB):
            cut, q_m, r_m = marker_step(it, b, alpha, beta)
            x_m = r_m * s.m_inv[:, cut]
            s.x[:, cut] = x_m
            rho_m += jnp.sum(r_m * x_m, axis=1, keepdims=True)
            eta_m += jnp.sum(q_m * x_m, axis=1, keepdims=True)
            delta_m += jnp.sum(s.mdiag[:, cut] * x_m * x_m, axis=1, keepdims=True)
            mb = (x_m * s.mscale[:, cut]).astype(BF16)
            dot_m += lax.dot_general(mb, s.g[:, cut], (((1,), (1,)), ((), ())), preferred_element_type=F32)
        own_rows = jnp.sum(jnp.where((blk == gblk) & (lane < geno), z_a, 0.0), axis=0, keepdims=True)
        s.y_send[it] = jnp.where(sub == traits, own_rows, 0.0)
        s.y_send[it, :traits, :geno] = dot_m
        s.y_recv[it, y] = s.y_send[it]
        each(peers_y, lambda yy: start(it, Y, s.y_send.at[it], s.y_recv.at[it, y], to_y(yy)))


        @pl.when(it == 0)
        def _():
            gets[-1].wait()

        arrived(it, A2, s.a2_recv.at[it, pl.ds(0, NJ - 1)])
        fetched = s.a2_recv[it].reshape(all_slots, LANES)
        s.fetched[...] = jnp.dot(s.placed[...], fetched, preferred_element_type=F32).reshape(LANES // 8, 8, LANES)

        def four(first):
            w = s.w[pl.ds(first, 4)]
            return jnp.concatenate([w[0:2].reshape(2 * LANES, LANES), w[2:4].reshape(2 * LANES, LANES)], axis=1)

        def forward(n, acc):
            rows = s.fetched[n]
            for h in (0, 4):
                a, b, c, d = [jnp.where(sub == s.rows[n * 8 + h + k], rows[h + k:h + k + 1], 0.0) for k in range(4)]
                left = jnp.concatenate([jnp.concatenate([a, c], axis=1), jnp.concatenate([b, d], axis=1)], axis=0)
                acc += lax.dot_general(left.astype(BF16), four(n * 8 + h), (((1,), (1,)), ((), ())),
                                       preferred_element_type=F32)
            return acc

        acc = lax.fori_loop(0, tiles // 8, forward, jnp.zeros((16, 2 * LANES), F32), unroll=7)
        v = acc[:8, :LANES] + acc[8:, LANES:]

        arrived(it, Y, s.y_recv.at[it, pl.ds(0, ny - 1)])
        g = jnp.zeros((traits, LANES), F32)
        for t in range(ny):
            g += s.y_recv[it, t, :traits, :]
            g += jnp.where(trait_col == t, s.y_recv[it, t, traits:traits + 1, :], 0.0)
        gb = g[:, :geno].astype(BF16)
        for b, cut in enumerate(cuts):
            s.r1_send[it, b] = jnp.dot(gb, s.g[:, cut], preferred_element_type=F32).astype(BF16)

        def send_r1(jj):
            @pl.when(jj < JB)
            def _():
                start(it, R1, s.r1_send.at[it, jj], s.r1_recv.at[it, j], to_j(jj))

        each(peers_j, send_r1)
        g_row = jnp.sum(jnp.where(trait_col == y, g, 0.0), axis=0, keepdims=True)
        delta_a = a_diag * z_a * z_a + v * v + jnp.where(sub == 0, g_row * g_row, 0.0)
        scalar_z(it, [r_a * z_a, z_a * q_a, delta_a])

        zero = jnp.zeros((8, LANES), F32)
        vb = v.astype(BF16).astype(F32)
        twice = jnp.concatenate([jnp.concatenate([vb, zero], axis=1), jnp.concatenate([zero, vb], axis=1)], axis=0)
        twice = twice.astype(BF16)

        def backward(n, c):
            rows = jnp.zeros((8, LANES), F32)
            for h in (0, 4):
                out = jnp.dot(twice, four(n * 8 + h), preferred_element_type=F32)
                for k in range(4):
                    up, across = k % 2, k // 2
                    part = out[8 * up:8 * up + 8, across * LANES:(across + 1) * LANES]
                    picked = jnp.sum(jnp.where(sub == s.rows[n * 8 + h + k], part, 0.0), axis=0, keepdims=True)
                    rows = jnp.where(sub == h + k, picked, rows)
            s.back[n] = rows
            return c

        lax.fori_loop(0, tiles // 8, backward, 0, unroll=7)
        back = s.back[...].reshape(LANES, LANES).astype(BF16)
        outgoing = jnp.dot(s.placed_t[...], back, preferred_element_type=F32)
        s.b1_send[it] = outgoing.reshape(NJ, slots, LANES).astype(BF16)
        s.b1_recv[it, j] = s.b1_send[it, j]
        each(peers_j, lambda jj: start(it, B1, s.b1_send.at[it, jj], s.b1_recv.at[it, j], to_j(jj)))

        @pl.when(in_jb)
        def _():
            s.r1_recv[it, j] = s.r1_send[it, j]
            arrived(it, R1, s.r1_recv.at[it, pl.ds(0, NJ - 1)])
            part = jnp.sum(s.r1_recv[it].astype(F32), axis=0)
            for b in range(ZB):
                s.r2_send[it, b] = part[:, b * LANES:(b + 1) * LANES]

            for b in range(ZB):
                @pl.when(b * ZS != z)
                def _(b=b):
                    start(it, R2, s.r2_send.at[it, b], s.r2_recv.at[it, z], to_z(b * ZS))

        scalar_x(it)

        arrived(it, B1, s.b1_recv.at[it, pl.ds(0, NJ - 1)])
        returned = s.b1_recv[it].reshape(all_slots, LANES)
        summed = jnp.dot(s.pmat_t[...], returned, preferred_element_type=F32)
        s.b2_send[it] = summed.reshape(nz, nb, LANES).astype(BF16)
        s.b2_recv[it, z] = s.b2_send[it, z]
        each(peers_z, lambda zz: start(it, B2, s.b2_send.at[it, zz], s.b2_recv.at[it, z], to_z(zz)))

        @pl.when(in_jb & in_zb)
        def _():
            s.r2_recv[it, z] = s.r2_send[it, lax.div(z, ZS)]
            arrived(it, R2, s.r2_recv.at[it, pl.ds(0, nz - 1)])
            part = jnp.sum(s.r2_recv[it], axis=0).astype(BF16)
            s.g1_send[it] = part
            s.g1_recv[it, lax.div(z, ZS)] = part
            each(peers_z, lambda zz: start(it, G1, s.g1_send.at[it], s.g1_recv.at[it, lax.div(z, ZS)], to_z(zz)))

        scalar_y(it, [rho_m, eta_m, delta_m])

        arrived(it, B2, s.b2_recv.at[it, pl.ds(0, nz - 1)])
        ped = jnp.sum(s.b2_recv[it].astype(F32), axis=0)
        image = a_diag * z_a + ped + jnp.where(blk == gblk, g_row, 0.0)
        sums = scalar_end(it)
        rho_next = sums[:, 0:1]
        beta = jnp.where(it == 0, 0.0, rho_next / rho)
        curv = sums[:, 2:3] + 2.0 * beta * sums[:, 1:2] + beta * beta * curv
        alpha = rho_next / curv
        alpha_y, beta_y = mine(alpha), mine(beta)
        u = z_a + beta_y * u
        q_a = image + beta_y * q_a
        sol_a = sol_a + alpha_y * u
        r_a = r_a - alpha_y * q_a
        return r_a * a_inv, r_a, q_a, u, sol_a, alpha, beta, rho_next, curv

    none = jnp.zeros((nb, LANES), F32)
    held = lax.fori_loop(0, ITERS, iterate, (r_a * a_inv, r_a, none, none, none, col, col, jnp.ones((traits, 1), F32), col),
                         unroll=True)
    _, r_a, _, _, sol_a, alpha, beta, _, _ = held
    last = ITERS - 1
    s.f_send[0] = sol_a
    s.f_send[1] = r_a
    s.f_recv[y] = s.f_send[...]
    each(peers_y, lambda yy: push(s.f_send, s.f_recv.at[y], s.once_send.at[1], s.once_recv.at[1], to_y(yy)))
    gather_wide(last)
    gather_end(last)
    for b in range(JB):
        marker_step(ITERS, b, alpha, beta)
    await_bytes(s.f_recv.at[pl.ds(0, ny - 1)], s.once_recv.at[1])
    for t in range(traits):
        for k in range(nb):
            asol[t:t + 1, k * LANES:(k + 1) * LANES] = s.f_recv[t, 0, k:k + 1, :]
            ares[t:t + 1, k * LANES:(k + 1) * LANES] = s.f_recv[t, 1, k:k + 1, :]

    await_bytes(s.id_recv.at[pl.ds(0, NJ - 1)], s.once_send.at[0])
    await_bytes(s.f_recv.at[pl.ds(0, ny - 1)], s.once_send.at[1])
    for n in range(ITERS):
        for step, ref, count in ((SZ, s.sz_recv, nz - 1), (SX, s.sx_recv, NJ - 1), (SY, s.sy_recv, ny - 1)):
            await_bytes(ref.at[n, pl.ds(0, count)], s.sum_send.at[n, step])
    for it in range(ITERS):
        def gone(stage, ref, count, it=it):
            await_bytes(ref.at[it, pl.ds(0, count)], s.send.at[it, stage])

        for stage, ref, count in ((A1, s.a1_recv, nz - 1), (A2, s.a2_recv, NJ - 1), (B1, s.b1_recv, NJ - 1),
                                  (B2, s.b2_recv, nz - 1), (Y, s.y_recv, ny - 1)):
            gone(stage, ref, count)

        @pl.when(in_jb)
        def _():
            gone(R1, s.r1_recv, JB - 1)
            gone(G2, s.g2_recv, NJ - 1)

            @pl.when(in_zb)
            def _():
                gone(R2, s.r2_recv, ZB - 1)
                gone(G1, s.g1_gone, nz - 1)

            @pl.when(jnp.logical_not(in_zb))
            def _():
                gone(R2, s.r2_recv, ZB)

        @pl.when(jnp.logical_not(in_jb))
        def _():
            gone(R1, s.r1_recv, JB)


def body(animal_rhs, marker_rhs, animal_diagonal, marker_diagonal, marker_scale, genotypes, tile_weights,
         tile_rows, tile_owner, tile_local, tile_count, genotyped_block):
    traits, animals = animal_rhs.shape
    markers = marker_rhs.shape[1]
    tiles = tile_weights.shape[0]
    nz, ny = lax.axis_size(ANIMALS) // NJ, lax.axis_size(SNPS)
    nb, slots = animals // LANES, nz * CAP
    every = NJ * slots
    wide = ZB * LANES

    def f32(*shape):
        return pltpu.VMEM(shape, F32)

    def b16(*shape):
        return pltpu.VMEM(shape, BF16)

    dma = pltpu.SemaphoreType.DMA
    scratch = dict(
        arhs=f32(traits, animals), adiag=f32(nb, LANES), mrhs=f32(traits, markers), mdiag=f32(1, markers),
        mscale=f32(1, markers), owner=pltpu.VMEM((1, tiles), I32), local=pltpu.VMEM((1, tiles), I32),
        rows=pltpu.SMEM((tiles,), I32),
        w=b16(*tile_weights.shape), g=b16(*genotypes.shape),
        placed=b16(LANES, every), placed_t=b16(every, LANES), table=f32(every, LANES),
        pmat=b16(every, nz * nb), pmat_t=b16(nz * nb, every),
        fetched=f32(LANES // 8, 8, LANES), back=f32(LANES // 8, 8, LANES),
        m=f32(traits, markers), q=f32(traits, markers), x=f32(traits, markers),
        m_inv=f32(1, markers),
        id_send=b16(NJ, slots, LANES), id_recv=b16(NJ, slots, LANES),
        a1_send=b16(ITERS, nb, LANES), a1_recv=b16(ITERS, nz, nb, LANES),
        a2_send=b16(ITERS, NJ, slots, LANES), a2_recv=b16(ITERS, NJ, slots, LANES),
        b1_send=b16(ITERS, NJ, slots, LANES), b1_recv=b16(ITERS, NJ, slots, LANES),
        b2_send=b16(ITERS, nz, nb, LANES), b2_recv=b16(ITERS, nz, nb, LANES),
        y_send=f32(ITERS, 8, LANES), y_recv=f32(ITERS, ny, 8, LANES),
        r1_send=b16(ITERS, JB, traits, wide), r1_recv=b16(ITERS, NJ, traits, wide),
        r2_send=f32(ITERS, ZB, traits, LANES), r2_recv=f32(ITERS, nz, traits, LANES),
        g1_send=b16(ITERS, traits, LANES), g1_recv=b16(ITERS, ZB, traits, LANES),
        g2_recv=b16(ITERS + 1, JB, ZB, traits, LANES),
        sz_send=f32(ITERS, 1, LANES), sz_recv=f32(ITERS, nz, 1, LANES),
        sx_send=f32(ITERS, 1, LANES), sx_recv=f32(ITERS, NJ, 1, LANES),
        sy_send=f32(ITERS, traits, LANES), sy_recv=f32(ITERS, ny, traits, LANES),
        g1_gone=b16(ITERS, nz, traits, LANES), f_send=f32(2, nb, LANES), f_recv=f32(ny, 2, nb, LANES),
        get=dma((10,)), once_send=dma((2,)), once_recv=dma((2,)),
        send=dma((ITERS, STAGES)), recv=dma((ITERS, STAGES)),
        sum_send=dma((ITERS, STEPS)), sum_recv=dma((ITERS, STEPS)),
    )

    def run(*refs):
        first = len(refs) - len(scratch)
        kernel(nz, ny, *refs[:first], SimpleNamespace(**dict(zip(scratch, refs[first:]))))

    outs = pl.pallas_call(
        run,
        out_shape=[jax.ShapeDtypeStruct(a.shape, F32) for a in (animal_rhs, marker_rhs, animal_rhs, marker_rhs)],
        in_specs=[pl.BlockSpec(memory_space=pl.ANY)] * 10 + [pl.BlockSpec(memory_space=pltpu.SMEM)] * 2,
        out_specs=[pl.BlockSpec(memory_space=pltpu.VMEM)] * 4,
        scratch_shapes=list(scratch.values()),
        compiler_params=pltpu.CompilerParams(collective_id=0, has_side_effects=True, vmem_limit_bytes=60 * 2**20),
    )(animal_rhs, marker_rhs, animal_diagonal.reshape(nb, LANES), marker_diagonal,
      marker_scale, genotypes, tile_weights, tile_rows, tile_owner.reshape(1, tiles),
      tile_local.reshape(1, tiles), tile_count, genotyped_block)

    def leave(*refs):
        sources, results, stages, sems = refs[:4], refs[4:8], refs[8:12], refs[12]
        reads = [pltpu.make_async_copy(a, b, sems.at[k]) for k, (a, b) in enumerate(zip(sources, stages))]
        writes = [pltpu.make_async_copy(a, b, sems.at[4 + k]) for k, (a, b) in enumerate(zip(stages, results))]
        for read in reads:
            read.start()
        for read, write in zip(reads, writes):
            read.wait()
            write.start()
        for write in writes:
            write.wait()

    return pl.pallas_call(
        leave,
        out_shape=[jax.ShapeDtypeStruct(a.shape, F32) for a in outs],
        in_specs=[pl.BlockSpec(memory_space=pl.ANY)] * 4,
        out_specs=[pl.BlockSpec(memory_space=pl.ANY)] * 4,
        scratch_shapes=[pltpu.VMEM(a.shape, F32) for a in outs] + [dma((8,))],
        compiler_params=pltpu.CompilerParams(vmem_limit_bytes=60 * 2**20),
    )(*outs)


def solution(mesh):
    placed = (P(None, ANIMALS), P(None, SNPS), P(ANIMALS), P(SNPS), P(SNPS), P(ANIMALS, SNPS),
              P(ANIMALS, None, None), P(ANIMALS), P(ANIMALS, None), P(ANIMALS), P(ANIMALS), P(ANIMALS))
    return jax.shard_map(
        body, mesh=mesh, in_specs=placed,
        out_specs=(P(None, ANIMALS), P(None, SNPS), P(None, ANIMALS), P(None, SNPS)), check_vma=False)
```

```python
from types import SimpleNamespace

import jax
import jax.numpy as jnp
from jax import lax
from jax.experimental import pallas as pl
from jax.experimental.pallas import tpu as pltpu
from jax.sharding import PartitionSpec as P

ITERS = 3
CAP = 2
NJ = 8
JB, ZB, ZS = 7, 7, 2
LANES = 128
A1, A2, B1, B2, Y, R1, R2, G1, G2, STAGES = range(10)
SZ, SX, SY, STEPS = range(4)
ANIMALS, SNPS = "animals", "snps"
MESH = pl.DeviceIdType.MESH
F32, BF16, I32 = jnp.float32, jnp.bfloat16, jnp.int32


def iota(shape, dim):
    return lax.broadcasted_iota(I32, shape, dim)


def total(x):
    return jnp.sum(jnp.sum(x, axis=1, keepdims=True), axis=0, keepdims=True)


def kernel(nz, ny, arhs_h, mrhs_h, adiag_h, mdiag_h, mscale_h, geno_h, w_h, rows_h, owner_h, local_h, count_s,
           gblk_s, asol, msol, ares, mres, s):
    traits, markers = mrhs_h.shape
    tiles = w_h.shape[0]
    nb = adiag_h.shape[0]
    geno = geno_h.shape[0]
    slots = nz * CAP
    all_slots, dense = NJ * slots, nz * nb
    wide = ZB * LANES
    me, y = lax.axis_index(ANIMALS), lax.axis_index(SNPS)
    z, j = lax.div(me, NJ), lax.rem(me, NJ)
    in_jb = j < JB
    in_zb = (lax.rem(z, ZS) == 0) & (z < ZB * ZS)

    def to_z(zz):
        return {ANIMALS: zz * NJ + j, SNPS: y}

    def to_j(jj):
        return {ANIMALS: z * NJ + jj, SNPS: y}

    def to_y(yy):
        return {ANIMALS: me, SNPS: yy}

    def others(here, count):
        half = count // 2
        order = [half] + [half + d for k in range(1, half) for d in (-k, k)]
        return [lax.rem(here + d, count) for d in order]

    peers_z, peers_j, peers_y = others(z, nz), others(j, NJ), others(y, ny)

    def each(peers, act):
        for peer in peers:
            act(peer)

    def push(src, dst, send, recv, device):
        pltpu.make_async_remote_copy(src_ref=src, dst_ref=dst, send_sem=send, recv_sem=recv,
                                     device_id=device, device_id_type=MESH).start()

    def await_bytes(ref, sem):
        pltpu.make_async_copy(ref, ref, sem).wait()

    barrier = pltpu.get_barrier_semaphore()

    def greet(device):
        pl.semaphore_signal(barrier, inc=1, device_id=device, device_id_type=MESH)

    each(peers_z, lambda zz: greet(to_z(zz)))
    each(peers_j, lambda jj: greet(to_j(jj)))
    each(peers_y, lambda yy: greet(to_y(yy)))

    pairs = ((arhs_h, s.arhs), (adiag_h, s.adiag), (mrhs_h, s.mrhs), (mdiag_h, s.mdiag.at[0]), (mscale_h, s.mscale.at[0]),
             (owner_h, s.owner), (local_h, s.local), (rows_h, s.rows), (geno_h, s.g), (w_h, s.w))
    gets = [pltpu.make_async_copy(src, dst, s.get.at[k]) for k, (src, dst) in enumerate(pairs)]
    for get in gets:
        get.start()
    gets[0].wait()
    gets[1].wait()

    blk = iota((nb, LANES), 0)
    lane = iota((nb, LANES), 1)
    sub = iota((8, LANES), 0)
    trait_col = iota((traits, 1), 0)
    lane4 = iota((traits, LANES), 1)
    a_diag = s.adiag[...]
    a_inv = 1.0 / a_diag
    r_a = jnp.zeros((nb, LANES), F32)
    for k in range(nb):
        row = jnp.where(trait_col == y, s.arhs[:, k * LANES:(k + 1) * LANES], 0.0)
        r_a = jnp.where(blk == k, jnp.sum(row, axis=0, keepdims=True), r_a)
    gblk = gblk_s[0]
    cuts = [slice(b * wide, (b + 1) * wide) for b in range(JB)]
    col = jnp.zeros((traits, 1), F32)

    def plan():
        own = s.owner[...]
        names = (iota((nz * NJ, tiles), 0) == own).astype(F32)
        before = (iota((tiles, tiles), 0) < iota((tiles, tiles), 1)).astype(F32)
        earlier = jnp.dot(names.astype(BF16), before.astype(BF16), preferred_element_type=F32)
        rank = jnp.sum(names * earlier, axis=0, keepdims=True)
        slot = (lax.rem(own, NJ) * slots + lax.div(own, NJ) * CAP).astype(F32) + rank
        slot = jnp.where(iota((1, tiles), 1) < count_s[0], slot, -1.0)
        hit = (iota((all_slots, tiles), 0).astype(F32) == slot).astype(F32)
        asked = jnp.sum(hit * (s.local[...] + 1).astype(F32), axis=1, keepdims=True)
        asked = jnp.broadcast_to(asked, (all_slots, LANES))
        s.id_send[...] = asked.reshape(NJ, slots, LANES).astype(BF16)
        each(peers_j, lambda jj: push(s.id_send.at[jj], s.id_recv.at[j], s.once_send.at[0], s.once_recv.at[0], to_j(jj)))
        s.id_recv[j] = s.id_send[j]
        s.table[...] = jnp.zeros_like(s.table)
        s.table[:, :tiles] = hit
        table = s.table[...]
        s.placed_t[...] = table.astype(BF16)
        s.placed[...] = table.T.astype(BF16)
        s.back[...] = jnp.zeros_like(s.back)

    def serve():
        await_bytes(s.id_recv.at[pl.ds(0, NJ - 1)], s.once_recv.at[0])
        ids = s.id_recv[...].astype(F32).reshape(all_slots, LANES)[:, :dense]
        source = lax.div(lax.rem(iota((all_slots, dense), 0), slots), CAP) * nb
        named = iota((all_slots, dense), 1).astype(F32) == source.astype(F32) + ids - 1.0
        pmat = ((ids > 0.5) & named).astype(F32)
        s.pmat[...] = pmat.astype(BF16)
        s.pmat_t[...] = pmat.T.astype(BF16)

    def begin():
        for cut in cuts:
            s.m_inv[:, cut] = 1.0 / s.mdiag[:, cut]
            mres[:, cut] = s.mrhs[:, cut]
            for ref in (s.x, s.q, s.m, msol):
                ref[:, cut] = jnp.zeros((traits, wide), F32)
        s.g2_recv[0] = jnp.zeros(s.g2_recv.shape[1:], BF16)

    pl.semaphore_wait(barrier, nz + NJ + ny - 3)

    def start(it, stage, src, dst, device):
        push(src, dst, s.send.at[it, stage], s.recv.at[it, stage], device)

    def arrived(it, stage, ref):
        await_bytes(ref, s.recv.at[it, stage])

    def scalar_push(n, step, src, dst, device):
        push(src, dst, s.sum_send.at[n, step], s.sum_recv.at[n, step], device)

    def scalar_z(n, parts):
        row = jnp.zeros((1, LANES), F32)
        for k, part in enumerate(parts):
            row = jnp.where(lane4[:1] == k, part, row)
        s.sz_send[n] = row
        s.sz_recv[n, z] = row
        each(peers_z, lambda zz: scalar_push(n, SZ, s.sz_send.at[n], s.sz_recv.at[n, z], to_z(zz)))

    def scalar_x(n):
        await_bytes(s.sz_recv.at[n, pl.ds(0, nz - 1)], s.sum_recv.at[n, SZ])
        row = jnp.sum(s.sz_recv[n], axis=0)
        s.sx_send[n] = row
        s.sx_recv[n, j] = row
        each(peers_j, lambda jj: scalar_push(n, SX, s.sx_send.at[n], s.sx_recv.at[n, j], to_j(jj)))

    def scalar_y(n, parts):
        await_bytes(s.sx_recv.at[n, pl.ds(0, NJ - 1)], s.sum_recv.at[n, SX])
        row = jnp.sum(s.sx_recv[n], axis=0)
        full = jnp.where(trait_col == y, row, 0.0)
        for k, part in enumerate(parts):
            full += jnp.where(lane4 == k, part, 0.0)
        s.sy_send[n] = full
        s.sy_recv[n, y] = full
        each(peers_y, lambda yy: scalar_push(n, SY, s.sy_send.at[n], s.sy_recv.at[n, y], to_y(yy)))

    def scalar_end(n):
        await_bytes(s.sy_recv.at[n, pl.ds(0, ny - 1)], s.sum_recv.at[n, SY])
        return jnp.sum(s.sy_recv[n], axis=0)

    def mine(col):
        return jnp.sum(jnp.where(trait_col == y, col, 0.0), axis=0, keepdims=True)

    def gather_wide(it):
        @pl.when(in_jb)
        def _():
            @pl.when(in_zb)
            def _():
                arrived(it, G1, s.g1_recv.at[it, pl.ds(0, ZB - 1)])

            @pl.when(jnp.logical_not(in_zb))
            def _():
                arrived(it, G1, s.g1_recv.at[it])

            s.g2_recv[it + 1, j] = s.g1_recv[it]
            each(peers_j, lambda jj: start(it, G2, s.g1_recv.at[it], s.g2_recv.at[it + 1, j], to_j(jj)))

    def gather_end(it):
        @pl.when(in_jb)
        def _():
            arrived(it, G2, s.g2_recv.at[it + 1, pl.ds(0, JB - 1)])

        @pl.when(jnp.logical_not(in_jb))
        def _():
            arrived(it, G2, s.g2_recv.at[it + 1])

    def marker_step(n, b, alpha, beta):
        cut = cuts[b]
        m = s.x[:, cut] + beta * s.m[:, cut]
        s.m[:, cut] = m
        msol[:, cut] = msol[:, cut] + alpha * m
        summed = jnp.concatenate([s.g2_recv[n, b, c].astype(F32) for c in range(ZB)], axis=1)
        q_m = s.mdiag[:, cut] * s.x[:, cut] + s.mscale[:, cut] * summed + beta * s.q[:, cut]
        s.q[:, cut] = q_m
        r_m = mres[:, cut] - alpha * q_m
        mres[:, cut] = r_m
        return cut, q_m, r_m

    def iterate(it, held):
        z_a, r_a, q_a, u, sol_a, alpha, beta, rho, curv = held

        s.a1_send[it] = z_a.astype(BF16)
        s.a1_recv[it, z] = s.a1_send[it]
        each(peers_z, lambda zz: start(it, A1, s.a1_send.at[it], s.a1_recv.at[it, z], to_z(zz)))

        @pl.when(it == 0)
        def _():
            for get in gets[2:-1]:
                get.wait()
            plan()
            begin()
            serve()

        @pl.when(it > 0)
        def _():
            gather_wide(it - 1)

        arrived(it, A1, s.a1_recv.at[it, pl.ds(0, nz - 1)])
        blocks = s.a1_recv[it].astype(F32).reshape(dense, LANES).astype(BF16)
        served = jnp.dot(s.pmat[...], blocks, preferred_element_type=F32)
        s.a2_send[it] = served.reshape(NJ, slots, LANES).astype(BF16)
        s.a2_recv[it, j] = s.a2_send[it, j]
        each(peers_j, lambda jj: start(it, A2, s.a2_send.at[it, jj], s.a2_recv.at[it, j], to_j(jj)))

        @pl.when(it > 0)
        def _():
            gather_end(it - 1)

        dot_m, rho_m, eta_m, delta_m = jnp.zeros((traits, geno), F32), col, col, col
        for b in range(JB):
            cut, q_m, r_m = marker_step(it, b, alpha, beta)
            x_m = r_m * s.m_inv[:, cut]
            s.x[:, cut] = x_m
            rho_m += jnp.sum(r_m * x_m, axis=1, keepdims=True)
            eta_m += jnp.sum(q_m * x_m, axis=1, keepdims=True)
            delta_m += jnp.sum(s.mdiag[:, cut] * x_m * x_m, axis=1, keepdims=True)
            mb = (x_m * s.mscale[:, cut]).astype(BF16)
            dot_m += lax.dot_general(mb, s.g[:, cut], (((1,), (1,)), ((), ())), preferred_element_type=F32)
        own_rows = jnp.sum(jnp.where((blk == gblk) & (lane < geno), z_a, 0.0), axis=0, keepdims=True)
        s.y_send[it] = jnp.where(sub == traits, own_rows, 0.0)
        s.y_send[it, :traits, :geno] = dot_m
        s.y_recv[it, y] = s.y_send[it]
        each(peers_y, lambda yy: start(it, Y, s.y_send.at[it], s.y_recv.at[it, y], to_y(yy)))


        arrived(it, Y, s.y_recv.at[it, pl.ds(0, ny - 1)])
        g = jnp.zeros((traits, LANES), F32)
        for t in range(ny):
            g += s.y_recv[it, t, :traits, :]
            g += jnp.where(trait_col == t, s.y_recv[it, t, traits:traits + 1, :], 0.0)
        gb = g[:, :geno].astype(BF16)
        for b, cut in enumerate(cuts):
            s.r1_send[it, b] = jnp.dot(gb, s.g[:, cut], preferred_element_type=F32).astype(BF16)

        def send_r1(jj):
            @pl.when(jj < JB)
            def _():
                start(it, R1, s.r1_send.at[it, jj], s.r1_recv.at[it, j], to_j(jj))

        each(peers_j, send_r1)
        g_row = jnp.sum(jnp.where(trait_col == y, g, 0.0), axis=0, keepdims=True)
        known = [total(r_a * z_a), total(z_a * q_a), total(a_diag * z_a * z_a) + total(g_row * g_row)]

        @pl.when(it == 0)
        def _():
            gets[-1].wait()

        arrived(it, A2, s.a2_recv.at[it, pl.ds(0, NJ - 1)])
        fetched = s.a2_recv[it].reshape(all_slots, LANES)
        s.fetched[...] = jnp.dot(s.placed[...], fetched, preferred_element_type=F32).reshape(LANES // 8, 8, LANES)

        def four(first):
            w = s.w[pl.ds(first, 4)]
            return jnp.concatenate([w[0:2].reshape(2 * LANES, LANES), w[2:4].reshape(2 * LANES, LANES)], axis=1)

        def forward(n, acc):
            rows = s.fetched[n]
            for h in (0, 4):
                a, b, c, d = [jnp.where(sub == s.rows[n * 8 + h + k], rows[h + k:h + k + 1], 0.0) for k in range(4)]
                left = jnp.concatenate([jnp.concatenate([a, c], axis=1), jnp.concatenate([b, d], axis=1)], axis=0)
                acc += lax.dot_general(left.astype(BF16), four(n * 8 + h), (((1,), (1,)), ((), ())),
                                       preferred_element_type=F32)
            return acc

        acc = lax.fori_loop(0, tiles // 8, forward, jnp.zeros((16, 2 * LANES), F32), unroll=7)
        v = acc[:8, :LANES] + acc[8:, LANES:]

        scalar_z(it, known[:2] + [known[2] + total(v * v)])

        zero = jnp.zeros((8, LANES), F32)
        vb = v.astype(BF16).astype(F32)
        twice = jnp.concatenate([jnp.concatenate([vb, zero], axis=1), jnp.concatenate([zero, vb], axis=1)], axis=0)
        twice = twice.astype(BF16)

        def backward(n, c):
            rows = jnp.zeros((8, LANES), F32)
            for h in (0, 4):
                out = jnp.dot(twice, four(n * 8 + h), preferred_element_type=F32)
                for k in range(4):
                    up, across = k % 2, k // 2
                    part = out[8 * up:8 * up + 8, across * LANES:(across + 1) * LANES]
                    picked = jnp.sum(jnp.where(sub == s.rows[n * 8 + h + k], part, 0.0), axis=0, keepdims=True)
                    rows = jnp.where(sub == h + k, picked, rows)
            s.back[n] = rows
            return c

        lax.fori_loop(0, tiles // 8, backward, 0, unroll=7)
        back = s.back[...].reshape(LANES, LANES).astype(BF16)
        outgoing = jnp.dot(s.placed_t[...], back, preferred_element_type=F32)
        s.b1_send[it] = outgoing.reshape(NJ, slots, LANES).astype(BF16)
        s.b1_recv[it, j] = s.b1_send[it, j]
        each(peers_j, lambda jj: start(it, B1, s.b1_send.at[it, jj], s.b1_recv.at[it, j], to_j(jj)))

        @pl.when(in_jb)
        def _():
            s.r1_recv[it, j] = s.r1_send[it, j]
            arrived(it, R1, s.r1_recv.at[it, pl.ds(0, NJ - 1)])
            part = jnp.sum(s.r1_recv[it].astype(F32), axis=0)
            for b in range(ZB):
                s.r2_send[it, b] = part[:, b * LANES:(b + 1) * LANES]

            for b in range(ZB):
                @pl.when(b * ZS != z)
                def _(b=b):
                    start(it, R2, s.r2_send.at[it, b], s.r2_recv.at[it, z], to_z(b * ZS))

        scalar_x(it)

        arrived(it, B1, s.b1_recv.at[it, pl.ds(0, NJ - 1)])
        returned = s.b1_recv[it].reshape(all_slots, LANES)
        summed = jnp.dot(s.pmat_t[...], returned, preferred_element_type=F32)
        s.b2_send[it] = summed.reshape(nz, nb, LANES).astype(BF16)
        s.b2_recv[it, z] = s.b2_send[it, z]
        each(peers_z, lambda zz: start(it, B2, s.b2_send.at[it, zz], s.b2_recv.at[it, z], to_z(zz)))

        @pl.when(in_jb & in_zb)
        def _():
            s.r2_recv[it, z] = s.r2_send[it, lax.div(z, ZS)]
            arrived(it, R2, s.r2_recv.at[it, pl.ds(0, nz - 1)])
            part = jnp.sum(s.r2_recv[it], axis=0).astype(BF16)
            s.g1_send[it] = part
            s.g1_recv[it, lax.div(z, ZS)] = part
            each(peers_z, lambda zz: start(it, G1, s.g1_send.at[it], s.g1_recv.at[it, lax.div(z, ZS)], to_z(zz)))

        scalar_y(it, [rho_m, eta_m, delta_m])

        arrived(it, B2, s.b2_recv.at[it, pl.ds(0, nz - 1)])
        ped = jnp.sum(s.b2_recv[it].astype(F32), axis=0)
        image = a_diag * z_a + ped + jnp.where(blk == gblk, g_row, 0.0)
        sums = scalar_end(it)
        rho_next = sums[:, 0:1]
        beta = jnp.where(it == 0, 0.0, rho_next / rho)
        curv = sums[:, 2:3] + 2.0 * beta * sums[:, 1:2] + beta * beta * curv
        alpha = rho_next / curv
        alpha_y, beta_y = mine(alpha), mine(beta)
        u = z_a + beta_y * u
        q_a = image + beta_y * q_a
        sol_a = sol_a + alpha_y * u
        r_a = r_a - alpha_y * q_a
        return r_a * a_inv, r_a, q_a, u, sol_a, alpha, beta, rho_next, curv

    none = jnp.zeros((nb, LANES), F32)
    held = lax.fori_loop(0, ITERS, iterate, (r_a * a_inv, r_a, none, none, none, col, col, jnp.ones((traits, 1), F32), col),
                         unroll=True)
    _, r_a, _, _, sol_a, alpha, beta, _, _ = held
    last = ITERS - 1
    s.f_send[0] = sol_a
    s.f_send[1] = r_a
    s.f_recv[y] = s.f_send[...]
    each(peers_y, lambda yy: push(s.f_send, s.f_recv.at[y], s.once_send.at[1], s.once_recv.at[1], to_y(yy)))
    gather_wide(last)
    gather_end(last)
    for b in range(JB):
        marker_step(ITERS, b, alpha, beta)
    await_bytes(s.f_recv.at[pl.ds(0, ny - 1)], s.once_recv.at[1])
    for t in range(traits):
        for k in range(nb):
            asol[t:t + 1, k * LANES:(k + 1) * LANES] = s.f_recv[t, 0, k:k + 1, :]
            ares[t:t + 1, k * LANES:(k + 1) * LANES] = s.f_recv[t, 1, k:k + 1, :]

    await_bytes(s.id_recv.at[pl.ds(0, NJ - 1)], s.once_send.at[0])
    await_bytes(s.f_recv.at[pl.ds(0, ny - 1)], s.once_send.at[1])
    for n in range(ITERS):
        for step, ref, count in ((SZ, s.sz_recv, nz - 1), (SX, s.sx_recv, NJ - 1), (SY, s.sy_recv, ny - 1)):
            await_bytes(ref.at[n, pl.ds(0, count)], s.sum_send.at[n, step])
    for it in range(ITERS):
        def gone(stage, ref, count, it=it):
            await_bytes(ref.at[it, pl.ds(0, count)], s.send.at[it, stage])

        for stage, ref, count in ((A1, s.a1_recv, nz - 1), (A2, s.a2_recv, NJ - 1), (B1, s.b1_recv, NJ - 1),
                                  (B2, s.b2_recv, nz - 1), (Y, s.y_recv, ny - 1)):
            gone(stage, ref, count)

        @pl.when(in_jb)
        def _():
            gone(R1, s.r1_recv, JB - 1)
            gone(G2, s.g2_recv, NJ - 1)

            @pl.when(in_zb)
            def _():
                gone(R2, s.r2_recv, ZB - 1)
                gone(G1, s.g1_gone, nz - 1)

            @pl.when(jnp.logical_not(in_zb))
            def _():
                gone(R2, s.r2_recv, ZB)

        @pl.when(jnp.logical_not(in_jb))
        def _():
            gone(R1, s.r1_recv, JB)


def body(animal_rhs, marker_rhs, animal_diagonal, marker_diagonal, marker_scale, genotypes, tile_weights,
         tile_rows, tile_owner, tile_local, tile_count, genotyped_block):
    traits, animals = animal_rhs.shape
    markers = marker_rhs.shape[1]
    tiles = tile_weights.shape[0]
    nz, ny = lax.axis_size(ANIMALS) // NJ, lax.axis_size(SNPS)
    nb, slots = animals // LANES, nz * CAP
    every = NJ * slots
    wide = ZB * LANES

    def f32(*shape):
        return pltpu.VMEM(shape, F32)

    def b16(*shape):
        return pltpu.VMEM(shape, BF16)

    dma = pltpu.SemaphoreType.DMA
    scratch = dict(
        arhs=f32(traits, animals), adiag=f32(nb, LANES), mrhs=f32(traits, markers), mdiag=f32(1, markers),
        mscale=f32(1, markers), owner=pltpu.VMEM((1, tiles), I32), local=pltpu.VMEM((1, tiles), I32),
        rows=pltpu.SMEM((tiles,), I32),
        w=b16(*tile_weights.shape), g=b16(*genotypes.shape),
        placed=b16(LANES, every), placed_t=b16(every, LANES), table=f32(every, LANES),
        pmat=b16(every, nz * nb), pmat_t=b16(nz * nb, every),
        fetched=f32(LANES // 8, 8, LANES), back=f32(LANES // 8, 8, LANES),
        m=f32(traits, markers), q=f32(traits, markers), x=f32(traits, markers),
        m_inv=f32(1, markers),
        id_send=b16(NJ, slots, LANES), id_recv=b16(NJ, slots, LANES),
        a1_send=b16(ITERS, nb, LANES), a1_recv=b16(ITERS, nz, nb, LANES),
        a2_send=b16(ITERS, NJ, slots, LANES), a2_recv=b16(ITERS, NJ, slots, LANES),
        b1_send=b16(ITERS, NJ, slots, LANES), b1_recv=b16(ITERS, NJ, slots, LANES),
        b2_send=b16(ITERS, nz, nb, LANES), b2_recv=b16(ITERS, nz, nb, LANES),
        y_send=f32(ITERS, 8, LANES), y_recv=f32(ITERS, ny, 8, LANES),
        r1_send=b16(ITERS, JB, traits, wide), r1_recv=b16(ITERS, NJ, traits, wide),
        r2_send=f32(ITERS, ZB, traits, LANES), r2_recv=f32(ITERS, nz, traits, LANES),
        g1_send=b16(ITERS, traits, LANES), g1_recv=b16(ITERS, ZB, traits, LANES),
        g2_recv=b16(ITERS + 1, JB, ZB, traits, LANES),
        sz_send=f32(ITERS, 1, LANES), sz_recv=f32(ITERS, nz, 1, LANES),
        sx_send=f32(ITERS, 1, LANES), sx_recv=f32(ITERS, NJ, 1, LANES),
        sy_send=f32(ITERS, traits, LANES), sy_recv=f32(ITERS, ny, traits, LANES),
        g1_gone=b16(ITERS, nz, traits, LANES), f_send=f32(2, nb, LANES), f_recv=f32(ny, 2, nb, LANES),
        get=dma((10,)), once_send=dma((2,)), once_recv=dma((2,)),
        send=dma((ITERS, STAGES)), recv=dma((ITERS, STAGES)),
        sum_send=dma((ITERS, STEPS)), sum_recv=dma((ITERS, STEPS)),
    )

    def run(*refs):
        first = len(refs) - len(scratch)
        kernel(nz, ny, *refs[:first], SimpleNamespace(**dict(zip(scratch, refs[first:]))))

    outs = pl.pallas_call(
        run,
        out_shape=[jax.ShapeDtypeStruct(a.shape, F32) for a in (animal_rhs, marker_rhs, animal_rhs, marker_rhs)],
        in_specs=[pl.BlockSpec(memory_space=pl.ANY)] * 10 + [pl.BlockSpec(memory_space=pltpu.SMEM)] * 2,
        out_specs=[pl.BlockSpec(memory_space=pltpu.VMEM)] * 4,
        scratch_shapes=list(scratch.values()),
        compiler_params=pltpu.CompilerParams(collective_id=0, has_side_effects=True, vmem_limit_bytes=60 * 2**20),
    )(animal_rhs, marker_rhs, animal_diagonal.reshape(nb, LANES), marker_diagonal,
      marker_scale, genotypes, tile_weights, tile_rows, tile_owner.reshape(1, tiles),
      tile_local.reshape(1, tiles), tile_count, genotyped_block)

    def leave(*refs):
        sources, results, stages, sems = refs[:4], refs[4:8], refs[8:12], refs[12]
        reads = [pltpu.make_async_copy(a, b, sems.at[k]) for k, (a, b) in enumerate(zip(sources, stages))]
        writes = [pltpu.make_async_copy(a, b, sems.at[4 + k]) for k, (a, b) in enumerate(zip(stages, results))]
        for read in reads:
            read.start()
        for read, write in zip(reads, writes):
            read.wait()
            write.start()
        for write in writes:
            write.wait()

    return pl.pallas_call(
        leave,
        out_shape=[jax.ShapeDtypeStruct(a.shape, F32) for a in outs],
        in_specs=[pl.BlockSpec(memory_space=pl.ANY)] * 4,
        out_specs=[pl.BlockSpec(memory_space=pl.ANY)] * 4,
        scratch_shapes=[pltpu.VMEM(a.shape, F32) for a in outs] + [dma((8,))],
        compiler_params=pltpu.CompilerParams(vmem_limit_bytes=60 * 2**20),
    )(*outs)


def solution(mesh):
    placed = (P(None, ANIMALS), P(None, SNPS), P(ANIMALS), P(SNPS), P(SNPS), P(ANIMALS, SNPS),
              P(ANIMALS, None, None), P(ANIMALS), P(ANIMALS, None), P(ANIMALS), P(ANIMALS), P(ANIMALS))
    return jax.shard_map(
        body, mesh=mesh, in_specs=placed,
        out_specs=(P(None, ANIMALS), P(None, SNPS), P(None, ANIMALS), P(None, SNPS)), check_vma=False)
```

```python
from types import SimpleNamespace

import jax
import jax.numpy as jnp
from jax import lax
from jax.experimental import pallas as pl
from jax.experimental.pallas import tpu as pltpu
from jax.sharding import PartitionSpec as P

ITERS = 3
CAP = 2
NJ = 8
JB, ZB, ZS = 7, 7, 2
LANES = 128
A1, A2, B1, B2, Y, R1, R2, G1, G2, STAGES = range(10)
SZ, SX, SY, STEPS = range(4)
ANIMALS, SNPS = "animals", "snps"
MESH = pl.DeviceIdType.MESH
F32, BF16, I32 = jnp.float32, jnp.bfloat16, jnp.int32


def iota(shape, dim):
    return lax.broadcasted_iota(I32, shape, dim)


def total(x):
    return jnp.sum(jnp.sum(x, axis=1, keepdims=True), axis=0, keepdims=True)


def kernel(nz, ny, arhs_h, mrhs_h, adiag_h, mdiag_h, mscale_h, geno_h, w_h, rows_h, owner_h, local_h, count_s,
           gblk_s, asol, msol, ares, mres, s):
    traits, markers = mrhs_h.shape
    tiles = w_h.shape[0]
    nb = adiag_h.shape[0]
    geno = geno_h.shape[0]
    slots = nz * CAP
    all_slots, dense = NJ * slots, nz * nb
    wide = ZB * LANES
    me, y = lax.axis_index(ANIMALS), lax.axis_index(SNPS)
    z, j = lax.div(me, NJ), lax.rem(me, NJ)
    in_jb = j < JB
    in_zb = (lax.rem(z, ZS) == 0) & (z < ZB * ZS)

    def to_z(zz):
        return {ANIMALS: zz * NJ + j, SNPS: y}

    def to_j(jj):
        return {ANIMALS: z * NJ + jj, SNPS: y}

    def to_y(yy):
        return {ANIMALS: me, SNPS: yy}

    def others(here, count):
        half = count // 2
        order = [half] + [half + d for k in range(1, half) for d in (-k, k)]
        return [lax.rem(here + d, count) for d in order]

    peers_z, peers_j, peers_y = others(z, nz), others(j, NJ), others(y, ny)

    def each(peers, act):
        for peer in peers:
            act(peer)

    def push(src, dst, send, recv, device):
        pltpu.make_async_remote_copy(src_ref=src, dst_ref=dst, send_sem=send, recv_sem=recv,
                                     device_id=device, device_id_type=MESH).start()

    def await_bytes(ref, sem):
        pltpu.make_async_copy(ref, ref, sem).wait()

    barrier = pltpu.get_barrier_semaphore()

    def greet(device):
        pl.semaphore_signal(barrier, inc=1, device_id=device, device_id_type=MESH)

    each(peers_z, lambda zz: greet(to_z(zz)))
    each(peers_j, lambda jj: greet(to_j(jj)))
    each(peers_y, lambda yy: greet(to_y(yy)))

    pairs = ((arhs_h, s.arhs), (adiag_h, s.adiag), (mrhs_h, s.mrhs), (mdiag_h, s.mdiag.at[0]), (mscale_h, s.mscale.at[0]),
             (owner_h, s.owner), (local_h, s.local), (rows_h, s.rows),
             (rows_h, s.row_names.at[0]), (geno_h, s.g), (w_h, s.w))
    gets = [pltpu.make_async_copy(src, dst, s.get.at[k]) for k, (src, dst) in enumerate(pairs)]
    for get in gets:
        get.start()
    gets[0].wait()
    gets[1].wait()

    blk = iota((nb, LANES), 0)
    lane = iota((nb, LANES), 1)
    sub = iota((8, LANES), 0)
    trait_col = iota((traits, 1), 0)
    lane4 = iota((traits, LANES), 1)
    a_diag = s.adiag[...]
    a_inv = 1.0 / a_diag
    r_a = jnp.zeros((nb, LANES), F32)
    for k in range(nb):
        row = jnp.where(trait_col == y, s.arhs[:, k * LANES:(k + 1) * LANES], 0.0)
        r_a = jnp.where(blk == k, jnp.sum(row, axis=0, keepdims=True), r_a)
    gblk = gblk_s[0]
    cuts = [slice(b * wide, (b + 1) * wide) for b in range(JB)]
    col = jnp.zeros((traits, 1), F32)

    def plan():
        own = s.owner[...]
        names = (iota((nz * NJ, tiles), 0) == own).astype(F32)
        before = (iota((tiles, tiles), 0) < iota((tiles, tiles), 1)).astype(F32)
        earlier = jnp.dot(names.astype(BF16), before.astype(BF16), preferred_element_type=F32)
        rank = jnp.sum(names * earlier, axis=0, keepdims=True)
        slot = (lax.rem(own, NJ) * slots + lax.div(own, NJ) * CAP).astype(F32) + rank
        slot = jnp.where(iota((1, tiles), 1) < count_s[0], slot, -1.0)
        hit = (iota((all_slots, tiles), 0).astype(F32) == slot).astype(F32)
        asked = jnp.sum(hit * (s.local[...] + 1).astype(F32), axis=1, keepdims=True)
        asked = jnp.broadcast_to(asked, (all_slots, LANES))
        s.id_send[...] = asked.reshape(NJ, slots, LANES).astype(BF16)
        each(peers_j, lambda jj: push(s.id_send.at[jj], s.id_recv.at[j], s.once_send.at[0], s.once_recv.at[0], to_j(jj)))
        s.id_recv[j] = s.id_send[j]
        s.row_hot[...] = jnp.zeros_like(s.row_hot)
        s.row_hot[:, :tiles] = (iota((8, tiles), 0) == s.row_names[...]).astype(F32)
        s.table[...] = jnp.zeros_like(s.table)
        s.table[:, :tiles] = hit
        table = s.table[...]
        s.placed_t[...] = table.astype(BF16)
        s.placed[...] = table.T.astype(BF16)
        s.back[...] = jnp.zeros_like(s.back)

    def serve():
        await_bytes(s.id_recv.at[pl.ds(0, NJ - 1)], s.once_recv.at[0])
        ids = s.id_recv[...].astype(F32).reshape(all_slots, LANES)[:, :dense]
        source = lax.div(lax.rem(iota((all_slots, dense), 0), slots), CAP) * nb
        named = iota((all_slots, dense), 1).astype(F32) == source.astype(F32) + ids - 1.0
        pmat = ((ids > 0.5) & named).astype(F32)
        s.pmat[...] = pmat.astype(BF16)
        s.pmat_t[...] = pmat.T.astype(BF16)

    def begin():
        for cut in cuts:
            s.m_inv[:, cut] = 1.0 / s.mdiag[:, cut]
            mres[:, cut] = s.mrhs[:, cut]
            for ref in (s.x, s.q, s.m, msol):
                ref[:, cut] = jnp.zeros((traits, wide), F32)
        s.g2_recv[0] = jnp.zeros(s.g2_recv.shape[1:], BF16)

    pl.semaphore_wait(barrier, nz + NJ + ny - 3)

    def start(it, stage, src, dst, device):
        push(src, dst, s.send.at[it, stage], s.recv.at[it, stage], device)

    def arrived(it, stage, ref):
        await_bytes(ref, s.recv.at[it, stage])

    def scalar_push(n, step, src, dst, device):
        push(src, dst, s.sum_send.at[n, step], s.sum_recv.at[n, step], device)

    def scalar_z(n, parts):
        row = jnp.zeros((1, LANES), F32)
        for k, part in enumerate(parts):
            row = jnp.where(lane4[:1] == k, part, row)
        s.sz_send[n] = row
        s.sz_recv[n, z] = row
        each(peers_z, lambda zz: scalar_push(n, SZ, s.sz_send.at[n], s.sz_recv.at[n, z], to_z(zz)))

    def scalar_x(n):
        await_bytes(s.sz_recv.at[n, pl.ds(0, nz - 1)], s.sum_recv.at[n, SZ])
        row = jnp.sum(s.sz_recv[n], axis=0)
        s.sx_send[n] = row
        s.sx_recv[n, j] = row
        each(peers_j, lambda jj: scalar_push(n, SX, s.sx_send.at[n], s.sx_recv.at[n, j], to_j(jj)))

    def scalar_y(n, parts):
        await_bytes(s.sx_recv.at[n, pl.ds(0, NJ - 1)], s.sum_recv.at[n, SX])
        row = jnp.sum(s.sx_recv[n], axis=0)
        full = jnp.where(trait_col == y, row, 0.0)
        for k, part in enumerate(parts):
            full += jnp.where(lane4 == k, part, 0.0)
        s.sy_send[n] = full
        s.sy_recv[n, y] = full
        each(peers_y, lambda yy: scalar_push(n, SY, s.sy_send.at[n], s.sy_recv.at[n, y], to_y(yy)))

    def scalar_end(n):
        await_bytes(s.sy_recv.at[n, pl.ds(0, ny - 1)], s.sum_recv.at[n, SY])
        return jnp.sum(s.sy_recv[n], axis=0)

    def mine(col):
        return jnp.sum(jnp.where(trait_col == y, col, 0.0), axis=0, keepdims=True)

    def gather_wide(it):
        @pl.when(in_jb)
        def _():
            @pl.when(in_zb)
            def _():
                arrived(it, G1, s.g1_recv.at[it, pl.ds(0, ZB - 1)])

            @pl.when(jnp.logical_not(in_zb))
            def _():
                arrived(it, G1, s.g1_recv.at[it])

            s.g2_recv[it + 1, j] = s.g1_recv[it]
            each(peers_j, lambda jj: start(it, G2, s.g1_recv.at[it], s.g2_recv.at[it + 1, j], to_j(jj)))

    def gather_end(it):
        @pl.when(in_jb)
        def _():
            arrived(it, G2, s.g2_recv.at[it + 1, pl.ds(0, JB - 1)])

        @pl.when(jnp.logical_not(in_jb))
        def _():
            arrived(it, G2, s.g2_recv.at[it + 1])

    def marker_step(n, b, alpha, beta):
        cut = cuts[b]
        m = s.x[:, cut] + beta * s.m[:, cut]
        s.m[:, cut] = m
        msol[:, cut] = msol[:, cut] + alpha * m
        summed = jnp.concatenate([s.g2_recv[n, b, c].astype(F32) for c in range(ZB)], axis=1)
        q_m = s.mdiag[:, cut] * s.x[:, cut] + s.mscale[:, cut] * summed + beta * s.q[:, cut]
        s.q[:, cut] = q_m
        r_m = mres[:, cut] - alpha * q_m
        mres[:, cut] = r_m
        return cut, q_m, r_m

    def iterate(it, held):
        z_a, r_a, q_a, u, sol_a, alpha, beta, rho, curv = held

        s.a1_send[it] = z_a.astype(BF16)
        s.a1_recv[it, z] = s.a1_send[it]
        each(peers_z, lambda zz: start(it, A1, s.a1_send.at[it], s.a1_recv.at[it, z], to_z(zz)))

        @pl.when(it == 0)
        def _():
            for get in gets[2:-1]:
                get.wait()
            plan()
            begin()
            serve()

        @pl.when(it > 0)
        def _():
            gather_wide(it - 1)

        arrived(it, A1, s.a1_recv.at[it, pl.ds(0, nz - 1)])
        blocks = s.a1_recv[it].astype(F32).reshape(dense, LANES).astype(BF16)
        served = jnp.dot(s.pmat[...], blocks, preferred_element_type=F32)
        s.a2_send[it] = served.reshape(NJ, slots, LANES).astype(BF16)
        s.a2_recv[it, j] = s.a2_send[it, j]
        each(peers_j, lambda jj: start(it, A2, s.a2_send.at[it, jj], s.a2_recv.at[it, j], to_j(jj)))

        @pl.when(it > 0)
        def _():
            gather_end(it - 1)

        dot_m, rho_m, eta_m, delta_m = jnp.zeros((traits, geno), F32), col, col, col
        for b in range(JB):
            cut, q_m, r_m = marker_step(it, b, alpha, beta)
            x_m = r_m * s.m_inv[:, cut]
            s.x[:, cut] = x_m
            rho_m += jnp.sum(r_m * x_m, axis=1, keepdims=True)
            eta_m += jnp.sum(q_m * x_m, axis=1, keepdims=True)
            delta_m += jnp.sum(s.mdiag[:, cut] * x_m * x_m, axis=1, keepdims=True)
            mb = (x_m * s.mscale[:, cut]).astype(BF16)
            dot_m += lax.dot_general(mb, s.g[:, cut], (((1,), (1,)), ((), ())), preferred_element_type=F32)
        own_rows = jnp.sum(jnp.where((blk == gblk) & (lane < geno), z_a, 0.0), axis=0, keepdims=True)
        s.y_send[it] = jnp.where(sub == traits, own_rows, 0.0)
        s.y_send[it, :traits, :geno] = dot_m
        s.y_recv[it, y] = s.y_send[it]
        each(peers_y, lambda yy: start(it, Y, s.y_send.at[it], s.y_recv.at[it, y], to_y(yy)))

        arrived(it, Y, s.y_recv.at[it, pl.ds(0, ny - 1)])
        g = jnp.zeros((traits, LANES), F32)
        for t in range(ny):
            g += s.y_recv[it, t, :traits, :]
            g += jnp.where(trait_col == t, s.y_recv[it, t, traits:traits + 1, :], 0.0)
        gb = g[:, :geno].astype(BF16)
        for b, cut in enumerate(cuts):
            s.r1_send[it, b] = jnp.dot(gb, s.g[:, cut], preferred_element_type=F32).astype(BF16)

        def send_r1(jj):
            @pl.when(jj < JB)
            def _():
                start(it, R1, s.r1_send.at[it, jj], s.r1_recv.at[it, j], to_j(jj))

        each(peers_j, send_r1)
        g_row = jnp.sum(jnp.where(trait_col == y, g, 0.0), axis=0, keepdims=True)
        known = [total(r_a * z_a), total(z_a * q_a), total(a_diag * z_a * z_a) + total(g_row * g_row)]

        @pl.when(it == 0)
        def _():
            gets[-1].wait()

        arrived(it, A2, s.a2_recv.at[it, pl.ds(0, NJ - 1)])
        fetched = jnp.dot(s.placed[...], s.a2_recv[it].reshape(all_slots, LANES), preferred_element_type=F32)
        blocks = fetched.T
        zero = jnp.zeros_like(blocks)
        both = jnp.concatenate([jnp.concatenate([blocks, zero], axis=1), jnp.concatenate([zero, blocks], axis=1)], axis=0)
        both = both.astype(BF16)

        def forward(n, acc):
            w = s.w[pl.ds(n * 8, 8)]
            left = jnp.concatenate([w[:4].reshape(4 * LANES, LANES), w[4:].reshape(4 * LANES, LANES)], axis=1)
            out = jnp.dot(left, both, preferred_element_type=F32)
            for k in range(8):
                down, across = k % 4 * LANES, k // 4 * LANES
                acc = jnp.where(column == n * 8 + k, out[down:down + LANES, across:across + LANES], acc)
            return acc

        column = iota((LANES, LANES), 1)
        acc = lax.fori_loop(0, tiles // 8, forward, zero, unroll=2)
        v = lax.dot_general(s.row_hot[...], acc, (((1,), (1,)), ((), ())), preferred_element_type=F32,
                            precision=lax.Precision.HIGHEST)

        scalar_z(it, known[:2] + [known[2] + total(v * v)])

        zero = jnp.zeros((8, LANES), F32)
        vb = v.astype(BF16).astype(F32)
        twice = jnp.concatenate([jnp.concatenate([vb, zero], axis=1), jnp.concatenate([zero, vb], axis=1)], axis=0)
        twice = twice.astype(BF16)

        def four(first):
            w = s.w[pl.ds(first, 4)]
            return jnp.concatenate([w[0:2].reshape(2 * LANES, LANES), w[2:4].reshape(2 * LANES, LANES)], axis=1)

        def backward(n, c):
            rows = jnp.zeros((8, LANES), F32)
            for h in (0, 4):
                out = jnp.dot(twice, four(n * 8 + h), preferred_element_type=F32)
                for k in range(4):
                    up, across = k % 2, k // 2
                    part = out[8 * up:8 * up + 8, across * LANES:(across + 1) * LANES]
                    picked = jnp.sum(jnp.where(sub == s.rows[n * 8 + h + k], part, 0.0), axis=0, keepdims=True)
                    rows = jnp.where(sub == h + k, picked, rows)
            s.back[n] = rows
            return c

        lax.fori_loop(0, tiles // 8, backward, 0, unroll=7)
        back = s.back[...].reshape(LANES, LANES).astype(BF16)
        outgoing = jnp.dot(s.placed_t[...], back, preferred_element_type=F32)
        s.b1_send[it] = outgoing.reshape(NJ, slots, LANES).astype(BF16)
        s.b1_recv[it, j] = s.b1_send[it, j]
        each(peers_j, lambda jj: start(it, B1, s.b1_send.at[it, jj], s.b1_recv.at[it, j], to_j(jj)))

        @pl.when(in_jb)
        def _():
            s.r1_recv[it, j] = s.r1_send[it, j]
            arrived(it, R1, s.r1_recv.at[it, pl.ds(0, NJ - 1)])
            part = jnp.sum(s.r1_recv[it].astype(F32), axis=0)
            for b in range(ZB):
                s.r2_send[it, b] = part[:, b * LANES:(b + 1) * LANES].astype(BF16)

            for b in range(ZB):
                @pl.when(b * ZS != z)
                def _(b=b):
                    start(it, R2, s.r2_send.at[it, b], s.r2_recv.at[it, z], to_z(b * ZS))

        scalar_x(it)

        arrived(it, B1, s.b1_recv.at[it, pl.ds(0, NJ - 1)])
        returned = s.b1_recv[it].reshape(all_slots, LANES)
        summed = jnp.dot(s.pmat_t[...], returned, preferred_element_type=F32)
        s.b2_send[it] = summed.reshape(nz, nb, LANES).astype(BF16)
        s.b2_recv[it, z] = s.b2_send[it, z]
        each(peers_z, lambda zz: start(it, B2, s.b2_send.at[it, zz], s.b2_recv.at[it, z], to_z(zz)))

        @pl.when(in_jb & in_zb)
        def _():
            s.r2_recv[it, z] = s.r2_send[it, lax.div(z, ZS)]
            arrived(it, R2, s.r2_recv.at[it, pl.ds(0, nz - 1)])
            part = jnp.sum(s.r2_recv[it].astype(F32), axis=0).astype(BF16)
            s.g1_send[it] = part
            s.g1_recv[it, lax.div(z, ZS)] = part
            each(peers_z, lambda zz: start(it, G1, s.g1_send.at[it], s.g1_recv.at[it, lax.div(z, ZS)], to_z(zz)))

        scalar_y(it, [rho_m, eta_m, delta_m])

        arrived(it, B2, s.b2_recv.at[it, pl.ds(0, nz - 1)])
        ped = jnp.sum(s.b2_recv[it].astype(F32), axis=0)
        image = a_diag * z_a + ped + jnp.where(blk == gblk, g_row, 0.0)
        sums = scalar_end(it)
        rho_next = sums[:, 0:1]
        beta = jnp.where(it == 0, 0.0, rho_next / rho)
        curv = sums[:, 2:3] + 2.0 * beta * sums[:, 1:2] + beta * beta * curv
        alpha = rho_next / curv
        alpha_y, beta_y = mine(alpha), mine(beta)
        u = z_a + beta_y * u
        q_a = image + beta_y * q_a
        sol_a = sol_a + alpha_y * u
        r_a = r_a - alpha_y * q_a
        return r_a * a_inv, r_a, q_a, u, sol_a, alpha, beta, rho_next, curv

    none = jnp.zeros((nb, LANES), F32)
    held = lax.fori_loop(0, ITERS, iterate, (r_a * a_inv, r_a, none, none, none, col, col, jnp.ones((traits, 1), F32), col),
                         unroll=True)
    _, r_a, _, _, sol_a, alpha, beta, _, _ = held
    last = ITERS - 1
    s.f_send[0] = sol_a
    s.f_send[1] = r_a
    s.f_recv[y] = s.f_send[...]
    each(peers_y, lambda yy: push(s.f_send, s.f_recv.at[y], s.once_send.at[1], s.once_recv.at[1], to_y(yy)))
    gather_wide(last)
    await_bytes(s.id_recv.at[pl.ds(0, NJ - 1)], s.once_send.at[0])
    for n in range(ITERS):
        for step, ref, count in ((SZ, s.sz_recv, nz - 1), (SX, s.sx_recv, NJ - 1), (SY, s.sy_recv, ny - 1)):
            await_bytes(ref.at[n, pl.ds(0, count)], s.sum_send.at[n, step])
    for it in range(ITERS):
        def gone(stage, ref, count, it=it):
            await_bytes(ref.at[it, pl.ds(0, count)], s.send.at[it, stage])

        for stage, ref, count in ((A1, s.a1_recv, nz - 1), (A2, s.a2_recv, NJ - 1), (B1, s.b1_recv, NJ - 1),
                                  (B2, s.b2_recv, nz - 1), (Y, s.y_recv, ny - 1)):
            gone(stage, ref, count)

        @pl.when(in_jb)
        def _():
            gone(R1, s.r1_recv, JB - 1)
            gone(G2, s.g2_recv, NJ - 1)

            @pl.when(in_zb)
            def _():
                gone(R2, s.r2_recv, ZB - 1)
                gone(G1, s.r2_recv, nz - 1)

            @pl.when(jnp.logical_not(in_zb))
            def _():
                gone(R2, s.r2_recv, ZB)

        @pl.when(jnp.logical_not(in_jb))
        def _():
            gone(R1, s.r1_recv, JB)

    gather_end(last)
    for b in range(JB):
        marker_step(ITERS, b, alpha, beta)
    await_bytes(s.f_recv.at[pl.ds(0, ny - 1)], s.once_recv.at[1])
    await_bytes(s.f_recv.at[pl.ds(0, ny - 1)], s.once_send.at[1])
    for t in range(traits):
        for k in range(nb):
            asol[t:t + 1, k * LANES:(k + 1) * LANES] = s.f_recv[t, 0, k:k + 1, :]
            ares[t:t + 1, k * LANES:(k + 1) * LANES] = s.f_recv[t, 1, k:k + 1, :]


def body(animal_rhs, marker_rhs, animal_diagonal, marker_diagonal, marker_scale, genotypes, tile_weights,
         tile_rows, tile_owner, tile_local, tile_count, genotyped_block):
    traits, animals = animal_rhs.shape
    markers = marker_rhs.shape[1]
    tiles = tile_weights.shape[0]
    nz, ny = lax.axis_size(ANIMALS) // NJ, lax.axis_size(SNPS)
    nb, slots = animals // LANES, nz * CAP
    every = NJ * slots
    wide = ZB * LANES

    def f32(*shape):
        return pltpu.VMEM(shape, F32)

    def b16(*shape):
        return pltpu.VMEM(shape, BF16)

    dma = pltpu.SemaphoreType.DMA
    scratch = dict(
        arhs=f32(traits, animals), adiag=f32(nb, LANES), mrhs=f32(traits, markers), mdiag=f32(1, markers),
        mscale=f32(1, markers), owner=pltpu.VMEM((1, tiles), I32), local=pltpu.VMEM((1, tiles), I32),
        rows=pltpu.SMEM((tiles,), I32),
        w=b16(*tile_weights.shape), g=b16(*genotypes.shape),
        placed=b16(LANES, every), placed_t=b16(every, LANES), table=f32(every, LANES),
        pmat=b16(every, nz * nb), pmat_t=b16(nz * nb, every),
        row_names=pltpu.VMEM((1, tiles), I32), row_hot=f32(8, LANES), back=f32(LANES // 8, 8, LANES),
        m=f32(traits, markers), q=f32(traits, markers), x=f32(traits, markers),
        m_inv=f32(1, markers),
        id_send=b16(NJ, slots, LANES), id_recv=b16(NJ, slots, LANES),
        a1_send=b16(ITERS, nb, LANES), a1_recv=b16(ITERS, nz, nb, LANES),
        a2_send=b16(ITERS, NJ, slots, LANES), a2_recv=b16(ITERS, NJ, slots, LANES),
        b1_send=b16(ITERS, NJ, slots, LANES), b1_recv=b16(ITERS, NJ, slots, LANES),
        b2_send=b16(ITERS, nz, nb, LANES), b2_recv=b16(ITERS, nz, nb, LANES),
        y_send=f32(ITERS, 8, LANES), y_recv=f32(ITERS, ny, 8, LANES),
        r1_send=b16(ITERS, JB, traits, wide), r1_recv=b16(ITERS, NJ, traits, wide),
        r2_send=b16(ITERS, ZB, traits, LANES), r2_recv=b16(ITERS, nz, traits, LANES),
        g1_send=b16(ITERS, traits, LANES), g1_recv=b16(ITERS, ZB, traits, LANES),
        g2_recv=b16(ITERS + 1, JB, ZB, traits, LANES),
        sz_send=f32(ITERS, 1, LANES), sz_recv=f32(ITERS, nz, 1, LANES),
        sx_send=f32(ITERS, 1, LANES), sx_recv=f32(ITERS, NJ, 1, LANES),
        sy_send=f32(ITERS, traits, LANES), sy_recv=f32(ITERS, ny, traits, LANES),
        f_send=f32(2, nb, LANES), f_recv=f32(ny, 2, nb, LANES),
        get=dma((11,)), once_send=dma((2,)), once_recv=dma((2,)),
        send=dma((ITERS, STAGES)), recv=dma((ITERS, STAGES)),
        sum_send=dma((ITERS, STEPS)), sum_recv=dma((ITERS, STEPS)),
    )

    def run(*refs):
        first = len(refs) - len(scratch)
        kernel(nz, ny, *refs[:first], SimpleNamespace(**dict(zip(scratch, refs[first:]))))

    outs = pl.pallas_call(
        run,
        out_shape=[jax.ShapeDtypeStruct(a.shape, F32) for a in (animal_rhs, marker_rhs, animal_rhs, marker_rhs)],
        in_specs=[pl.BlockSpec(memory_space=pl.ANY)] * 10 + [pl.BlockSpec(memory_space=pltpu.SMEM)] * 2,
        out_specs=[pl.BlockSpec(memory_space=pltpu.VMEM)] * 4,
        scratch_shapes=list(scratch.values()),
        compiler_params=pltpu.CompilerParams(collective_id=0, has_side_effects=True, vmem_limit_bytes=60 * 2**20),
    )(animal_rhs, marker_rhs, animal_diagonal.reshape(nb, LANES), marker_diagonal,
      marker_scale, genotypes, tile_weights, tile_rows, tile_owner.reshape(1, tiles),
      tile_local.reshape(1, tiles), tile_count, genotyped_block)

    def leave(*refs):
        sources, results, stages, sems = refs[:4], refs[4:8], refs[8:12], refs[12]
        reads = [pltpu.make_async_copy(a, b, sems.at[k]) for k, (a, b) in enumerate(zip(sources, stages))]
        writes = [pltpu.make_async_copy(a, b, sems.at[4 + k]) for k, (a, b) in enumerate(zip(stages, results))]
        for read in reads:
            read.start()
        for read, write in zip(reads, writes):
            read.wait()
            write.start()
        for write in writes:
            write.wait()

    return pl.pallas_call(
        leave,
        out_shape=[jax.ShapeDtypeStruct(a.shape, F32) for a in outs],
        in_specs=[pl.BlockSpec(memory_space=pl.ANY)] * 4,
        out_specs=[pl.BlockSpec(memory_space=pl.ANY)] * 4,
        scratch_shapes=[pltpu.VMEM(a.shape, F32) for a in outs] + [dma((8,))],
        compiler_params=pltpu.CompilerParams(vmem_limit_bytes=60 * 2**20),
    )(*outs)


def solution(mesh):
    placed = (P(None, ANIMALS), P(None, SNPS), P(ANIMALS), P(SNPS), P(SNPS), P(ANIMALS, SNPS),
              P(ANIMALS, None, None), P(ANIMALS), P(ANIMALS, None), P(ANIMALS), P(ANIMALS), P(ANIMALS))
    return jax.shard_map(
        body, mesh=mesh, in_specs=placed,
        out_specs=(P(None, ANIMALS), P(None, SNPS), P(None, ANIMALS), P(None, SNPS)), check_vma=False)
```

```python
from types import SimpleNamespace

import jax
import jax.numpy as jnp
from jax import lax
from jax.experimental import pallas as pl
from jax.experimental.pallas import tpu as pltpu
from jax.sharding import PartitionSpec as P

ITERS = 3
CAP = 2
NJ = 8
JB, ZB, ZS = 7, 7, 2
LANES = 128
A1, A2, B1, B2, Y, R1, R2, G1, G2, STAGES = range(10)
SZ, SX, SY, STEPS = range(4)
ANIMALS, SNPS = "animals", "snps"
MESH = pl.DeviceIdType.MESH
F32, BF16, I32 = jnp.float32, jnp.bfloat16, jnp.int32


def iota(shape, dim):
    return lax.broadcasted_iota(I32, shape, dim)


def total(x):
    return jnp.sum(jnp.sum(x, axis=1, keepdims=True), axis=0, keepdims=True)


def kernel(nz, ny, arhs_h, mrhs_h, adiag_h, mdiag_h, mscale_h, geno_h, w_h, rows_h, owner_h, local_h, count_s,
           gblk_s, asol, msol, ares, mres, s):
    traits, markers = mrhs_h.shape
    tiles = w_h.shape[0]
    nb = adiag_h.shape[0]
    geno = geno_h.shape[0]
    slots = nz * CAP
    all_slots, dense = NJ * slots, nz * nb
    wide = ZB * LANES
    me, y = lax.axis_index(ANIMALS), lax.axis_index(SNPS)
    z, j = lax.div(me, NJ), lax.rem(me, NJ)
    in_jb = j < JB
    in_zb = (lax.rem(z, ZS) == 0) & (z < ZB * ZS)

    def to_z(zz):
        return {ANIMALS: zz * NJ + j, SNPS: y}

    def to_j(jj):
        return {ANIMALS: z * NJ + jj, SNPS: y}

    def to_y(yy):
        return {ANIMALS: me, SNPS: yy}

    def others(here, count):
        half = count // 2
        order = [half] + [half + d for k in range(1, half) for d in (-k, k)]
        return [lax.rem(here + d, count) for d in order]

    peers_z, peers_j, peers_y = others(z, nz), others(j, NJ), others(y, ny)

    def each(peers, act):
        for peer in peers:
            act(peer)

    def push(src, dst, send, recv, device):
        pltpu.make_async_remote_copy(src_ref=src, dst_ref=dst, send_sem=send, recv_sem=recv,
                                     device_id=device, device_id_type=MESH).start()

    def await_bytes(ref, sem):
        pltpu.make_async_copy(ref, ref, sem).wait()

    barrier = pltpu.get_barrier_semaphore()

    def greet(device):
        pl.semaphore_signal(barrier, inc=1, device_id=device, device_id_type=MESH)

    each(peers_z, lambda zz: greet(to_z(zz)))
    each(peers_j, lambda jj: greet(to_j(jj)))
    each(peers_y, lambda yy: greet(to_y(yy)))

    pairs = ((arhs_h, s.arhs), (adiag_h, s.adiag), (mrhs_h, s.mrhs), (mdiag_h, s.mdiag.at[0]), (mscale_h, s.mscale.at[0]),
             (owner_h, s.owner), (local_h, s.local), (rows_h, s.rows), (geno_h, s.g), (w_h, s.w))
    gets = [pltpu.make_async_copy(src, dst, s.get.at[k]) for k, (src, dst) in enumerate(pairs)]
    for get in gets:
        get.start()
    gets[0].wait()
    gets[1].wait()

    blk = iota((nb, LANES), 0)
    lane = iota((nb, LANES), 1)
    sub = iota((8, LANES), 0)
    trait_col = iota((traits, 1), 0)
    lane4 = iota((traits, LANES), 1)
    a_diag = s.adiag[...]
    a_inv = 1.0 / a_diag
    r_a = jnp.zeros((nb, LANES), F32)
    for k in range(nb):
        row = jnp.where(trait_col == y, s.arhs[:, k * LANES:(k + 1) * LANES], 0.0)
        r_a = jnp.where(blk == k, jnp.sum(row, axis=0, keepdims=True), r_a)
    gblk = gblk_s[0]
    cuts = [slice(b * wide, (b + 1) * wide) for b in range(JB)]
    col = jnp.zeros((traits, 1), F32)

    def plan():
        own = s.owner[...]
        names = (iota((nz * NJ, tiles), 0) == own).astype(F32)
        before = (iota((tiles, tiles), 0) < iota((tiles, tiles), 1)).astype(F32)
        earlier = jnp.dot(names.astype(BF16), before.astype(BF16), preferred_element_type=F32)
        rank = jnp.sum(names * earlier, axis=0, keepdims=True)
        slot = (lax.rem(own, NJ) * slots + lax.div(own, NJ) * CAP).astype(F32) + rank
        slot = jnp.where(iota((1, tiles), 1) < count_s[0], slot, -1.0)
        hit = (iota((all_slots, tiles), 0).astype(F32) == slot).astype(F32)
        asked = jnp.sum(hit * (s.local[...] + 1).astype(F32), axis=1, keepdims=True)
        asked = jnp.broadcast_to(asked, (all_slots, LANES))
        s.id_send[...] = asked.reshape(NJ, slots, LANES).astype(BF16)
        each(peers_j, lambda jj: push(s.id_send.at[jj], s.id_recv.at[j], s.once_send.at[0], s.once_recv.at[0], to_j(jj)))
        s.id_recv[j] = s.id_send[j]
        s.table[...] = jnp.zeros_like(s.table)
        s.table[:, :tiles] = hit
        table = s.table[...]
        s.placed_t[...] = table.astype(BF16)
        s.placed[...] = table.T.astype(BF16)
        s.back[...] = jnp.zeros_like(s.back)

    def serve():
        await_bytes(s.id_recv.at[pl.ds(0, NJ - 1)], s.once_recv.at[0])
        ids = s.id_recv[...].astype(F32).reshape(all_slots, LANES)[:, :dense]
        source = lax.div(lax.rem(iota((all_slots, dense), 0), slots), CAP) * nb
        named = iota((all_slots, dense), 1).astype(F32) == source.astype(F32) + ids - 1.0
        pmat = ((ids > 0.5) & named).astype(F32)
        s.pmat[...] = pmat.astype(BF16)
        s.pmat_t[...] = pmat.T.astype(BF16)

    def begin():
        for cut in cuts:
            s.m_inv[:, cut] = 1.0 / s.mdiag[:, cut]
            mres[:, cut] = s.mrhs[:, cut]
            for ref in (s.x, s.q, s.m, msol):
                ref[:, cut] = jnp.zeros((traits, wide), F32)
        s.g2_recv[0] = jnp.zeros(s.g2_recv.shape[1:], BF16)

    pl.semaphore_wait(barrier, nz + NJ + ny - 3)

    def start(it, stage, src, dst, device):
        push(src, dst, s.send.at[it, stage], s.recv.at[it, stage], device)

    def arrived(it, stage, ref):
        await_bytes(ref, s.recv.at[it, stage])

    def scalar_push(n, step, src, dst, device):
        push(src, dst, s.sum_send.at[n, step], s.sum_recv.at[n, step], device)

    def scalar_z(n, parts):
        row = jnp.zeros((1, LANES), F32)
        for k, part in enumerate(parts):
            row = jnp.where(lane4[:1] == k, part, row)
        s.sz_send[n] = row
        s.sz_recv[n, z] = row
        each(peers_z, lambda zz: scalar_push(n, SZ, s.sz_send.at[n], s.sz_recv.at[n, z], to_z(zz)))

    def scalar_x(n):
        await_bytes(s.sz_recv.at[n, pl.ds(0, nz - 1)], s.sum_recv.at[n, SZ])
        row = jnp.sum(s.sz_recv[n], axis=0)
        s.sx_send[n] = row
        s.sx_recv[n, j] = row
        each(peers_j, lambda jj: scalar_push(n, SX, s.sx_send.at[n], s.sx_recv.at[n, j], to_j(jj)))

    def scalar_y(n, parts):
        await_bytes(s.sx_recv.at[n, pl.ds(0, NJ - 1)], s.sum_recv.at[n, SX])
        row = jnp.sum(s.sx_recv[n], axis=0)
        full = jnp.where(trait_col == y, row, 0.0)
        for k, part in enumerate(parts):
            full += jnp.where(lane4 == k, part, 0.0)
        s.sy_send[n] = full
        s.sy_recv[n, y] = full
        each(peers_y, lambda yy: scalar_push(n, SY, s.sy_send.at[n], s.sy_recv.at[n, y], to_y(yy)))

    def scalar_end(n):
        await_bytes(s.sy_recv.at[n, pl.ds(0, ny - 1)], s.sum_recv.at[n, SY])
        return jnp.sum(s.sy_recv[n], axis=0)

    def mine(col):
        return jnp.sum(jnp.where(trait_col == y, col, 0.0), axis=0, keepdims=True)

    def gather_wide(it):
        @pl.when(in_jb)
        def _():
            @pl.when(in_zb)
            def _():
                arrived(it, G1, s.g1_recv.at[it, pl.ds(0, ZB - 1)])

            @pl.when(jnp.logical_not(in_zb))
            def _():
                arrived(it, G1, s.g1_recv.at[it])

            s.g2_recv[it + 1, j] = s.g1_recv[it]
            each(peers_j, lambda jj: start(it, G2, s.g1_recv.at[it], s.g2_recv.at[it + 1, j], to_j(jj)))

    def gather_end(it):
        @pl.when(in_jb)
        def _():
            arrived(it, G2, s.g2_recv.at[it + 1, pl.ds(0, JB - 1)])

        @pl.when(jnp.logical_not(in_jb))
        def _():
            arrived(it, G2, s.g2_recv.at[it + 1])

    def marker_step(n, b, alpha, beta):
        cut = cuts[b]
        m = s.x[:, cut] + beta * s.m[:, cut]
        s.m[:, cut] = m
        msol[:, cut] = msol[:, cut] + alpha * m
        summed = jnp.concatenate([s.g2_recv[n, b, c].astype(F32) for c in range(ZB)], axis=1)
        q_m = s.mdiag[:, cut] * s.x[:, cut] + s.mscale[:, cut] * summed + beta * s.q[:, cut]
        s.q[:, cut] = q_m
        r_m = mres[:, cut] - alpha * q_m
        mres[:, cut] = r_m
        return cut, q_m, r_m

    def iterate(it, held):
        z_a, r_a, q_a, u, sol_a, alpha, beta, rho, curv = held

        s.a1_send[it] = z_a.astype(BF16)
        s.a1_recv[it, z] = s.a1_send[it]
        each(peers_z, lambda zz: start(it, A1, s.a1_send.at[it], s.a1_recv.at[it, z], to_z(zz)))

        @pl.when(it == 0)
        def _():
            for get in gets[2:-1]:
                get.wait()
            plan()
            begin()
            serve()

        @pl.when(it > 0)
        def _():
            gather_wide(it - 1)

        arrived(it, A1, s.a1_recv.at[it, pl.ds(0, nz - 1)])
        blocks = s.a1_recv[it].astype(F32).reshape(dense, LANES).astype(BF16)
        served = jnp.dot(s.pmat[...], blocks, preferred_element_type=F32)
        s.a2_send[it] = served.reshape(NJ, slots, LANES).astype(BF16)
        s.a2_recv[it, j] = s.a2_send[it, j]
        each(peers_j, lambda jj: start(it, A2, s.a2_send.at[it, jj], s.a2_recv.at[it, j], to_j(jj)))

        @pl.when(it > 0)
        def _():
            gather_end(it - 1)

        dot_m, rho_m, eta_m, delta_m = jnp.zeros((traits, geno), F32), col, col, col
        for b in range(JB):
            cut, q_m, r_m = marker_step(it, b, alpha, beta)
            x_m = r_m * s.m_inv[:, cut]
            s.x[:, cut] = x_m
            rho_m += jnp.sum(r_m * x_m, axis=1, keepdims=True)
            eta_m += jnp.sum(q_m * x_m, axis=1, keepdims=True)
            delta_m += jnp.sum(s.mdiag[:, cut] * x_m * x_m, axis=1, keepdims=True)
            mb = (x_m * s.mscale[:, cut]).astype(BF16)
            dot_m += lax.dot_general(mb, s.g[:, cut], (((1,), (1,)), ((), ())), preferred_element_type=F32)
        own_rows = jnp.sum(jnp.where((blk == gblk) & (lane < geno), z_a, 0.0), axis=0, keepdims=True)
        s.y_send[it] = jnp.where(sub == traits, own_rows, 0.0)
        s.y_send[it, :traits, :geno] = dot_m
        s.y_recv[it, y] = s.y_send[it]
        each(peers_y, lambda yy: start(it, Y, s.y_send.at[it], s.y_recv.at[it, y], to_y(yy)))

        arrived(it, Y, s.y_recv.at[it, pl.ds(0, ny - 1)])
        g = jnp.zeros((traits, LANES), F32)
        for t in range(ny):
            g += s.y_recv[it, t, :traits, :]
            g += jnp.where(trait_col == t, s.y_recv[it, t, traits:traits + 1, :], 0.0)
        gb = g[:, :geno].astype(BF16)
        for b, cut in enumerate(cuts):
            s.r1_send[it, b] = jnp.dot(gb, s.g[:, cut], preferred_element_type=F32).astype(BF16)

        def send_r1(jj):
            @pl.when(jj < JB)
            def _():
                start(it, R1, s.r1_send.at[it, jj], s.r1_recv.at[it, j], to_j(jj))

        each(peers_j, send_r1)
        g_row = jnp.sum(jnp.where(trait_col == y, g, 0.0), axis=0, keepdims=True)
        known = [total(r_a * z_a), total(z_a * q_a), total(a_diag * z_a * z_a) + total(g_row * g_row)]

        @pl.when(it == 0)
        def _():
            gets[-1].wait()

        arrived(it, A2, s.a2_recv.at[it, pl.ds(0, NJ - 1)])
        fetched = s.a2_recv[it].reshape(all_slots, LANES)
        s.fetched[...] = jnp.dot(s.placed[...], fetched, preferred_element_type=F32).reshape(LANES // 8, 8, LANES)

        def four(first):
            w = s.w[pl.ds(first, 4)]
            return jnp.concatenate([w[0:2].reshape(2 * LANES, LANES), w[2:4].reshape(2 * LANES, LANES)], axis=1)

        def forward(n, acc):
            rows = s.fetched[n]
            for h in (0, 4):
                a, b, c, d = [jnp.where(sub == s.rows[n * 8 + h + k], rows[h + k:h + k + 1], 0.0) for k in range(4)]
                left = jnp.concatenate([jnp.concatenate([a, c], axis=1), jnp.concatenate([b, d], axis=1)], axis=0)
                acc += lax.dot_general(left.astype(BF16), four(n * 8 + h), (((1,), (1,)), ((), ())),
                                       preferred_element_type=F32)
            return acc

        acc = lax.fori_loop(0, tiles // 8, forward, jnp.zeros((16, 2 * LANES), F32), unroll=True)
        v = acc[:8, :LANES] + acc[8:, LANES:]

        scalar_z(it, known[:2] + [known[2] + total(v * v)])

        zero = jnp.zeros((8, LANES), F32)
        vb = v.astype(BF16).astype(F32)
        twice = jnp.concatenate([jnp.concatenate([vb, zero], axis=1), jnp.concatenate([zero, vb], axis=1)], axis=0)
        twice = twice.astype(BF16)

        def backward(n, c):
            rows = jnp.zeros((8, LANES), F32)
            for h in (0, 4):
                out = jnp.dot(twice, four(n * 8 + h), preferred_element_type=F32)
                for k in range(4):
                    up, across = k % 2, k // 2
                    part = out[8 * up:8 * up + 8, across * LANES:(across + 1) * LANES]
                    picked = jnp.sum(jnp.where(sub == s.rows[n * 8 + h + k], part, 0.0), axis=0, keepdims=True)
                    rows = jnp.where(sub == h + k, picked, rows)
            s.back[n] = rows
            return c

        lax.fori_loop(0, tiles // 8, backward, 0, unroll=True)
        back = s.back[...].reshape(LANES, LANES).astype(BF16)
        outgoing = jnp.dot(s.placed_t[...], back, preferred_element_type=F32)
        s.b1_send[it] = outgoing.reshape(NJ, slots, LANES).astype(BF16)
        s.b1_recv[it, j] = s.b1_send[it, j]
        each(peers_j, lambda jj: start(it, B1, s.b1_send.at[it, jj], s.b1_recv.at[it, j], to_j(jj)))

        @pl.when(in_jb)
        def _():
            s.r1_recv[it, j] = s.r1_send[it, j]
            arrived(it, R1, s.r1_recv.at[it, pl.ds(0, NJ - 1)])
            part = jnp.sum(s.r1_recv[it].astype(F32), axis=0)
            for b in range(ZB):
                s.r2_send[it, b] = part[:, b * LANES:(b + 1) * LANES].astype(BF16)

            for b in range(ZB):
                @pl.when(b * ZS != z)
                def _(b=b):
                    start(it, R2, s.r2_send.at[it, b], s.r2_recv.at[it, z], to_z(b * ZS))

        scalar_x(it)

        arrived(it, B1, s.b1_recv.at[it, pl.ds(0, NJ - 1)])
        returned = s.b1_recv[it].reshape(all_slots, LANES)
        summed = jnp.dot(s.pmat_t[...], returned, preferred_element_type=F32)
        s.b2_send[it] = summed.reshape(nz, nb, LANES).astype(BF16)
        s.b2_recv[it, z] = s.b2_send[it, z]
        each(peers_z, lambda zz: start(it, B2, s.b2_send.at[it, zz], s.b2_recv.at[it, z], to_z(zz)))

        @pl.when(in_jb & in_zb)
        def _():
            s.r2_recv[it, z] = s.r2_send[it, lax.div(z, ZS)]
            arrived(it, R2, s.r2_recv.at[it, pl.ds(0, nz - 1)])
            part = jnp.sum(s.r2_recv[it].astype(F32), axis=0).astype(BF16)
            s.g1_send[it] = part
            s.g1_recv[it, lax.div(z, ZS)] = part
            each(peers_z, lambda zz: start(it, G1, s.g1_send.at[it], s.g1_recv.at[it, lax.div(z, ZS)], to_z(zz)))

        scalar_y(it, [rho_m, eta_m, delta_m])

        arrived(it, B2, s.b2_recv.at[it, pl.ds(0, nz - 1)])
        ped = jnp.sum(s.b2_recv[it].astype(F32), axis=0)
        image = a_diag * z_a + ped + jnp.where(blk == gblk, g_row, 0.0)
        sums = scalar_end(it)
        rho_next = sums[:, 0:1]
        beta = jnp.where(it == 0, 0.0, rho_next / rho)
        curv = sums[:, 2:3] + 2.0 * beta * sums[:, 1:2] + beta * beta * curv
        alpha = rho_next / curv
        alpha_y, beta_y = mine(alpha), mine(beta)
        u = z_a + beta_y * u
        q_a = image + beta_y * q_a
        sol_a = sol_a + alpha_y * u
        r_a = r_a - alpha_y * q_a
        return r_a * a_inv, r_a, q_a, u, sol_a, alpha, beta, rho_next, curv

    none = jnp.zeros((nb, LANES), F32)
    held = lax.fori_loop(0, ITERS, iterate, (r_a * a_inv, r_a, none, none, none, col, col, jnp.ones((traits, 1), F32), col),
                         unroll=True)
    _, r_a, _, _, sol_a, alpha, beta, _, _ = held
    last = ITERS - 1
    s.f_send[0] = sol_a
    s.f_send[1] = r_a
    s.f_recv[y] = s.f_send[...]
    each(peers_y, lambda yy: push(s.f_send, s.f_recv.at[y], s.once_send.at[1], s.once_recv.at[1], to_y(yy)))
    gather_wide(last)
    await_bytes(s.id_recv.at[pl.ds(0, NJ - 1)], s.once_send.at[0])
    for n in range(ITERS):
        for step, ref, count in ((SZ, s.sz_recv, nz - 1), (SX, s.sx_recv, NJ - 1), (SY, s.sy_recv, ny - 1)):
            await_bytes(ref.at[n, pl.ds(0, count)], s.sum_send.at[n, step])
    for it in range(ITERS):
        def gone(stage, ref, count, it=it):
            await_bytes(ref.at[it, pl.ds(0, count)], s.send.at[it, stage])

        for stage, ref, count in ((A1, s.a1_recv, nz - 1), (A2, s.a2_recv, NJ - 1), (B1, s.b1_recv, NJ - 1),
                                  (B2, s.b2_recv, nz - 1), (Y, s.y_recv, ny - 1)):
            gone(stage, ref, count)

        @pl.when(in_jb)
        def _():
            gone(R1, s.r1_recv, JB - 1)
            gone(G2, s.g2_recv, NJ - 1)

            @pl.when(in_zb)
            def _():
                gone(R2, s.r2_recv, ZB - 1)
                gone(G1, s.r2_recv, nz - 1)

            @pl.when(jnp.logical_not(in_zb))
            def _():
                gone(R2, s.r2_recv, ZB)

        @pl.when(jnp.logical_not(in_jb))
        def _():
            gone(R1, s.r1_recv, JB)

    gather_end(last)
    for b in range(JB):
        marker_step(ITERS, b, alpha, beta)
    await_bytes(s.f_recv.at[pl.ds(0, ny - 1)], s.once_recv.at[1])
    await_bytes(s.f_recv.at[pl.ds(0, ny - 1)], s.once_send.at[1])
    for t in range(traits):
        for k in range(nb):
            asol[t:t + 1, k * LANES:(k + 1) * LANES] = s.f_recv[t, 0, k:k + 1, :]
            ares[t:t + 1, k * LANES:(k + 1) * LANES] = s.f_recv[t, 1, k:k + 1, :]


def body(animal_rhs, marker_rhs, animal_diagonal, marker_diagonal, marker_scale, genotypes, tile_weights,
         tile_rows, tile_owner, tile_local, tile_count, genotyped_block):
    traits, animals = animal_rhs.shape
    markers = marker_rhs.shape[1]
    tiles = tile_weights.shape[0]
    nz, ny = lax.axis_size(ANIMALS) // NJ, lax.axis_size(SNPS)
    nb, slots = animals // LANES, nz * CAP
    every = NJ * slots
    wide = ZB * LANES

    def f32(*shape):
        return pltpu.VMEM(shape, F32)

    def b16(*shape):
        return pltpu.VMEM(shape, BF16)

    dma = pltpu.SemaphoreType.DMA
    scratch = dict(
        arhs=f32(traits, animals), adiag=f32(nb, LANES), mrhs=f32(traits, markers), mdiag=f32(1, markers),
        mscale=f32(1, markers), owner=pltpu.VMEM((1, tiles), I32), local=pltpu.VMEM((1, tiles), I32),
        rows=pltpu.SMEM((tiles,), I32),
        w=b16(*tile_weights.shape), g=b16(*genotypes.shape),
        placed=b16(LANES, every), placed_t=b16(every, LANES), table=f32(every, LANES),
        pmat=b16(every, nz * nb), pmat_t=b16(nz * nb, every),
        fetched=f32(LANES // 8, 8, LANES), back=f32(LANES // 8, 8, LANES),
        m=f32(traits, markers), q=f32(traits, markers), x=f32(traits, markers),
        m_inv=f32(1, markers),
        id_send=b16(NJ, slots, LANES), id_recv=b16(NJ, slots, LANES),
        a1_send=b16(ITERS, nb, LANES), a1_recv=b16(ITERS, nz, nb, LANES),
        a2_send=b16(ITERS, NJ, slots, LANES), a2_recv=b16(ITERS, NJ, slots, LANES),
        b1_send=b16(ITERS, NJ, slots, LANES), b1_recv=b16(ITERS, NJ, slots, LANES),
        b2_send=b16(ITERS, nz, nb, LANES), b2_recv=b16(ITERS, nz, nb, LANES),
        y_send=f32(ITERS, 8, LANES), y_recv=f32(ITERS, ny, 8, LANES),
        r1_send=b16(ITERS, JB, traits, wide), r1_recv=b16(ITERS, NJ, traits, wide),
        r2_send=b16(ITERS, ZB, traits, LANES), r2_recv=b16(ITERS, nz, traits, LANES),
        g1_send=b16(ITERS, traits, LANES), g1_recv=b16(ITERS, ZB, traits, LANES),
        g2_recv=b16(ITERS + 1, JB, ZB, traits, LANES),
        sz_send=f32(ITERS, 1, LANES), sz_recv=f32(ITERS, nz, 1, LANES),
        sx_send=f32(ITERS, 1, LANES), sx_recv=f32(ITERS, NJ, 1, LANES),
        sy_send=f32(ITERS, traits, LANES), sy_recv=f32(ITERS, ny, traits, LANES),
        f_send=f32(2, nb, LANES), f_recv=f32(ny, 2, nb, LANES),
        get=dma((10,)), once_send=dma((2,)), once_recv=dma((2,)),
        send=dma((ITERS, STAGES)), recv=dma((ITERS, STAGES)),
        sum_send=dma((ITERS, STEPS)), sum_recv=dma((ITERS, STEPS)),
    )

    def run(*refs):
        first = len(refs) - len(scratch)
        kernel(nz, ny, *refs[:first], SimpleNamespace(**dict(zip(scratch, refs[first:]))))

    outs = pl.pallas_call(
        run,
        out_shape=[jax.ShapeDtypeStruct(a.shape, F32) for a in (animal_rhs, marker_rhs, animal_rhs, marker_rhs)],
        in_specs=[pl.BlockSpec(memory_space=pl.ANY)] * 10 + [pl.BlockSpec(memory_space=pltpu.SMEM)] * 2,
        out_specs=[pl.BlockSpec(memory_space=pltpu.VMEM)] * 4,
        scratch_shapes=list(scratch.values()),
        compiler_params=pltpu.CompilerParams(collective_id=0, has_side_effects=True, vmem_limit_bytes=60 * 2**20),
    )(animal_rhs, marker_rhs, animal_diagonal.reshape(nb, LANES), marker_diagonal,
      marker_scale, genotypes, tile_weights, tile_rows, tile_owner.reshape(1, tiles),
      tile_local.reshape(1, tiles), tile_count, genotyped_block)

    def leave(*refs):
        sources, results, stages, sems = refs[:4], refs[4:8], refs[8:12], refs[12]
        reads = [pltpu.make_async_copy(a, b, sems.at[k]) for k, (a, b) in enumerate(zip(sources, stages))]
        writes = [pltpu.make_async_copy(a, b, sems.at[4 + k]) for k, (a, b) in enumerate(zip(stages, results))]
        for read in reads:
            read.start()
        for read, write in zip(reads, writes):
            read.wait()
            write.start()
        for write in writes:
            write.wait()

    return pl.pallas_call(
        leave,
        out_shape=[jax.ShapeDtypeStruct(a.shape, F32) for a in outs],
        in_specs=[pl.BlockSpec(memory_space=pl.ANY)] * 4,
        out_specs=[pl.BlockSpec(memory_space=pl.ANY)] * 4,
        scratch_shapes=[pltpu.VMEM(a.shape, F32) for a in outs] + [dma((8,))],
        compiler_params=pltpu.CompilerParams(vmem_limit_bytes=60 * 2**20),
    )(*outs)


def solution(mesh):
    placed = (P(None, ANIMALS), P(None, SNPS), P(ANIMALS), P(SNPS), P(SNPS), P(ANIMALS, SNPS),
              P(ANIMALS, None, None), P(ANIMALS), P(ANIMALS, None), P(ANIMALS), P(ANIMALS), P(ANIMALS))
    return jax.shard_map(
        body, mesh=mesh, in_specs=placed,
        out_specs=(P(None, ANIMALS), P(None, SNPS), P(None, ANIMALS), P(None, SNPS)), check_vma=False)
```

```python
from types import SimpleNamespace

import jax
import jax.numpy as jnp
from jax import lax
from jax.experimental import pallas as pl
from jax.experimental.pallas import tpu as pltpu
from jax.sharding import PartitionSpec as P

ITERS = 3
CAP = 2
NJ = 8
JB, ZB, ZS = 7, 7, 2
LANES = 128
A1, A2, B1, B2, Y, R1, R2, G1, G2, STAGES = range(10)
SZ, SX, SY, STEPS = range(4)
ANIMALS, SNPS = "animals", "snps"
MESH = pl.DeviceIdType.MESH
F32, BF16, I32 = jnp.float32, jnp.bfloat16, jnp.int32


def iota(shape, dim):
    return lax.broadcasted_iota(I32, shape, dim)


def total(x):
    return jnp.sum(jnp.sum(x, axis=1, keepdims=True), axis=0, keepdims=True)


def kernel(nz, ny, arhs_h, mrhs_h, adiag_h, mdiag_h, mscale_h, geno_h, w_h, rows_h, owner_h, local_h, count_s,
           gblk_s, asol, msol, ares, mres, s):
    traits, markers = mrhs_h.shape
    tiles = w_h.shape[0]
    nb = adiag_h.shape[0]
    geno = geno_h.shape[0]
    slots = nz * CAP
    all_slots, dense = NJ * slots, nz * nb
    wide = ZB * LANES
    me, y = lax.axis_index(ANIMALS), lax.axis_index(SNPS)
    z, j = lax.div(me, NJ), lax.rem(me, NJ)
    in_jb = j < JB
    in_zb = (lax.rem(z, ZS) == 0) & (z < ZB * ZS)

    def to_z(zz):
        return {ANIMALS: zz * NJ + j, SNPS: y}

    def to_j(jj):
        return {ANIMALS: z * NJ + jj, SNPS: y}

    def to_y(yy):
        return {ANIMALS: me, SNPS: yy}

    def others(here, count):
        half = count // 2
        order = [half] + [half + d for k in range(1, half) for d in (-k, k)]
        return [lax.rem(here + d, count) for d in order]

    peers_z, peers_j, peers_y = others(z, nz), others(j, NJ), others(y, ny)

    def each(peers, act):
        for peer in peers:
            act(peer)

    def push(src, dst, send, recv, device):
        pltpu.make_async_remote_copy(src_ref=src, dst_ref=dst, send_sem=send, recv_sem=recv,
                                     device_id=device, device_id_type=MESH).start()

    def await_bytes(ref, sem):
        pltpu.make_async_copy(ref, ref, sem).wait()

    barrier = pltpu.get_barrier_semaphore()

    def greet(device):
        pl.semaphore_signal(barrier, inc=1, device_id=device, device_id_type=MESH)

    each(peers_z, lambda zz: greet(to_z(zz)))
    each(peers_j, lambda jj: greet(to_j(jj)))
    each(peers_y, lambda yy: greet(to_y(yy)))

    pairs = ((arhs_h, s.arhs), (adiag_h, s.adiag), (mrhs_h, s.mrhs), (mdiag_h, s.mdiag.at[0]), (mscale_h, s.mscale.at[0]),
             (owner_h, s.owner), (local_h, s.local), (rows_h, s.rows), (geno_h, s.g), (w_h, s.w))
    gets = [pltpu.make_async_copy(src, dst, s.get.at[k]) for k, (src, dst) in enumerate(pairs)]
    for get in gets:
        get.start()
    gets[0].wait()
    gets[1].wait()

    blk = iota((nb, LANES), 0)
    lane = iota((nb, LANES), 1)
    sub = iota((8, LANES), 0)
    trait_col = iota((traits, 1), 0)
    lane4 = iota((traits, LANES), 1)
    a_diag = s.adiag[...]
    a_inv = 1.0 / a_diag
    r_a = jnp.zeros((nb, LANES), F32)
    for k in range(nb):
        row = jnp.where(trait_col == y, s.arhs[:, k * LANES:(k + 1) * LANES], 0.0)
        r_a = jnp.where(blk == k, jnp.sum(row, axis=0, keepdims=True), r_a)
    gblk = gblk_s[0]
    cuts = [slice(b * wide, (b + 1) * wide) for b in range(JB)]
    col = jnp.zeros((traits, 1), F32)

    def plan():
        own = s.owner[...]
        names = (iota((nz * NJ, tiles), 0) == own).astype(F32)
        before = (iota((tiles, tiles), 0) < iota((tiles, tiles), 1)).astype(F32)
        earlier = jnp.dot(names.astype(BF16), before.astype(BF16), preferred_element_type=F32)
        rank = jnp.sum(names * earlier, axis=0, keepdims=True)
        slot = (lax.rem(own, NJ) * slots + lax.div(own, NJ) * CAP).astype(F32) + rank
        slot = jnp.where(iota((1, tiles), 1) < count_s[0], slot, -1.0)
        hit = (iota((all_slots, tiles), 0).astype(F32) == slot).astype(F32)
        asked = jnp.sum(hit * (s.local[...] + 1).astype(F32), axis=1, keepdims=True)
        asked = jnp.broadcast_to(asked, (all_slots, LANES))
        s.id_send[...] = asked.reshape(NJ, slots, LANES).astype(BF16)
        each(peers_j, lambda jj: push(s.id_send.at[jj], s.id_recv.at[j], s.once_send.at[0], s.once_recv.at[0], to_j(jj)))
        s.id_recv[j] = s.id_send[j]
        s.table[...] = jnp.zeros_like(s.table)
        s.table[:, :tiles] = hit
        table = s.table[...]
        s.placed_t[...] = table.astype(BF16)
        s.placed[...] = table.T.astype(BF16)
        s.back[...] = jnp.zeros_like(s.back)

    def serve():
        await_bytes(s.id_recv.at[pl.ds(0, NJ - 1)], s.once_recv.at[0])
        ids = s.id_recv[...].astype(F32).reshape(all_slots, LANES)[:, :dense]
        source = lax.div(lax.rem(iota((all_slots, dense), 0), slots), CAP) * nb
        named = iota((all_slots, dense), 1).astype(F32) == source.astype(F32) + ids - 1.0
        pmat = ((ids > 0.5) & named).astype(F32)
        s.pmat[...] = pmat.astype(BF16)
        s.pmat_t[...] = pmat.T.astype(BF16)

    def begin():
        for cut in cuts:
            s.m_inv[:, cut] = 1.0 / s.mdiag[:, cut]
            mres[:, cut] = s.mrhs[:, cut]
            for ref in (s.x, s.q, s.m, msol):
                ref[:, cut] = jnp.zeros((traits, wide), F32)
        s.g2_recv[0] = jnp.zeros(s.g2_recv.shape[1:], BF16)

    pl.semaphore_wait(barrier, nz + NJ + ny - 3)

    def start(it, stage, src, dst, device):
        push(src, dst, s.send.at[it, stage], s.recv.at[it, stage], device)

    def arrived(it, stage, ref):
        await_bytes(ref, s.recv.at[it, stage])

    def scalar_push(n, step, src, dst, device):
        push(src, dst, s.sum_send.at[n, step], s.sum_recv.at[n, step], device)

    def scalar_z(n, parts):
        row = jnp.zeros((1, LANES), F32)
        for k, part in enumerate(parts):
            row = jnp.where(lane4[:1] == k, part, row)
        s.sz_send[n] = row
        s.sz_recv[n, z] = row
        each(peers_z, lambda zz: scalar_push(n, SZ, s.sz_send.at[n], s.sz_recv.at[n, z], to_z(zz)))

    def scalar_x(n):
        await_bytes(s.sz_recv.at[n, pl.ds(0, nz - 1)], s.sum_recv.at[n, SZ])
        row = jnp.sum(s.sz_recv[n], axis=0)
        s.sx_send[n] = row
        s.sx_recv[n, j] = row
        each(peers_j, lambda jj: scalar_push(n, SX, s.sx_send.at[n], s.sx_recv.at[n, j], to_j(jj)))

    def scalar_y(n, parts):
        await_bytes(s.sx_recv.at[n, pl.ds(0, NJ - 1)], s.sum_recv.at[n, SX])
        row = jnp.sum(s.sx_recv[n], axis=0)
        full = jnp.where(trait_col == y, row, 0.0)
        for k, part in enumerate(parts):
            full += jnp.where(lane4 == k, part, 0.0)
        s.sy_send[n] = full
        s.sy_recv[n, y] = full
        each(peers_y, lambda yy: scalar_push(n, SY, s.sy_send.at[n], s.sy_recv.at[n, y], to_y(yy)))

    def scalar_end(n):
        await_bytes(s.sy_recv.at[n, pl.ds(0, ny - 1)], s.sum_recv.at[n, SY])
        return jnp.sum(s.sy_recv[n], axis=0)

    def mine(col):
        return jnp.sum(jnp.where(trait_col == y, col, 0.0), axis=0, keepdims=True)

    def gather_wide(it):
        @pl.when(in_jb)
        def _():
            @pl.when(in_zb)
            def _():
                arrived(it, G1, s.g1_recv.at[it, pl.ds(0, ZB - 1)])

            @pl.when(jnp.logical_not(in_zb))
            def _():
                arrived(it, G1, s.g1_recv.at[it])

            s.g2_recv[it + 1, j] = s.g1_recv[it]
            each(peers_j, lambda jj: start(it, G2, s.g1_recv.at[it], s.g2_recv.at[it + 1, j], to_j(jj)))

    def gather_end(it):
        @pl.when(in_jb)
        def _():
            arrived(it, G2, s.g2_recv.at[it + 1, pl.ds(0, JB - 1)])

        @pl.when(jnp.logical_not(in_jb))
        def _():
            arrived(it, G2, s.g2_recv.at[it + 1])

    def marker_step(n, b, alpha, beta):
        cut = cuts[b]
        m = s.x[:, cut] + beta * s.m[:, cut]
        s.m[:, cut] = m
        msol[:, cut] = msol[:, cut] + alpha * m
        summed = jnp.concatenate([s.g2_recv[n, b, c].astype(F32) for c in range(ZB)], axis=1)
        q_m = s.mdiag[:, cut] * s.x[:, cut] + s.mscale[:, cut] * summed + beta * s.q[:, cut]
        s.q[:, cut] = q_m
        r_m = mres[:, cut] - alpha * q_m
        mres[:, cut] = r_m
        return cut, q_m, r_m

    def iterate(it, held):
        z_a, r_a, q_a, u, sol_a, alpha, beta, rho, curv = held

        s.a1_send[it] = z_a.astype(BF16)
        s.a1_recv[it, z] = s.a1_send[it]
        each(peers_z, lambda zz: start(it, A1, s.a1_send.at[it], s.a1_recv.at[it, z], to_z(zz)))

        @pl.when(it == 0)
        def _():
            for get in gets[2:-1]:
                get.wait()
            plan()
            begin()
            serve()

        @pl.when(it > 0)
        def _():
            gather_wide(it - 1)

        arrived(it, A1, s.a1_recv.at[it, pl.ds(0, nz - 1)])
        blocks = s.a1_recv[it].astype(F32).reshape(dense, LANES).astype(BF16)
        served = jnp.dot(s.pmat[...], blocks, preferred_element_type=F32)
        s.a2_send[it] = served.reshape(NJ, slots, LANES).astype(BF16)
        s.a2_recv[it, j] = s.a2_send[it, j]
        each(peers_j, lambda jj: start(it, A2, s.a2_send.at[it, jj], s.a2_recv.at[it, j], to_j(jj)))

        @pl.when(it > 0)
        def _():
            gather_end(it - 1)

        dot_m, rho_m, eta_m, delta_m = jnp.zeros((traits, geno), F32), col, col, col
        for b in range(JB):
            cut, q_m, r_m = marker_step(it, b, alpha, beta)
            x_m = r_m * s.m_inv[:, cut]
            s.x[:, cut] = x_m
            rho_m += jnp.sum(r_m * x_m, axis=1, keepdims=True)
            eta_m += jnp.sum(q_m * x_m, axis=1, keepdims=True)
            delta_m += jnp.sum(s.mdiag[:, cut] * x_m * x_m, axis=1, keepdims=True)
            mb = (x_m * s.mscale[:, cut]).astype(BF16)
            dot_m += lax.dot_general(mb, s.g[:, cut], (((1,), (1,)), ((), ())), preferred_element_type=F32)
        own_rows = jnp.sum(jnp.where((blk == gblk) & (lane < geno), z_a, 0.0), axis=0, keepdims=True)
        s.y_send[it] = jnp.where(sub == traits, own_rows, 0.0)
        s.y_send[it, :traits, :geno] = dot_m
        s.y_recv[it, y] = s.y_send[it]
        each(peers_y, lambda yy: start(it, Y, s.y_send.at[it], s.y_recv.at[it, y], to_y(yy)))

        arrived(it, Y, s.y_recv.at[it, pl.ds(0, ny - 1)])
        g = jnp.zeros((traits, LANES), F32)
        for t in range(ny):
            g += s.y_recv[it, t, :traits, :]
            g += jnp.where(trait_col == t, s.y_recv[it, t, traits:traits + 1, :], 0.0)
        gb = g[:, :geno].astype(BF16)
        for b, cut in enumerate(cuts):
            s.r1_send[it, b] = jnp.dot(gb, s.g[:, cut], preferred_element_type=F32).astype(BF16)

        def send_r1(jj):
            @pl.when(jj < JB)
            def _():
                start(it, R1, s.r1_send.at[it, jj], s.r1_recv.at[it, j], to_j(jj))

        each(peers_j, send_r1)
        g_row = jnp.sum(jnp.where(trait_col == y, g, 0.0), axis=0, keepdims=True)
        known = [total(r_a * z_a), total(z_a * q_a), total(a_diag * z_a * z_a) + total(g_row * g_row)]

        @pl.when(it == 0)
        def _():
            gets[-1].wait()

        arrived(it, A2, s.a2_recv.at[it, pl.ds(0, NJ - 1)])
        fetched = s.a2_recv[it].reshape(all_slots, LANES)
        s.fetched[...] = jnp.dot(s.placed[...], fetched, preferred_element_type=F32).reshape(LANES // 8, 8, LANES)

        def four(first):
            w = s.w[pl.ds(first, 4)]
            return jnp.concatenate([w[0:2].reshape(2 * LANES, LANES), w[2:4].reshape(2 * LANES, LANES)], axis=1)

        def forward(n, acc):
            rows = s.fetched[n]
            for h in (0, 4):
                a, b, c, d = [jnp.where(sub == s.rows[n * 8 + h + k], rows[h + k:h + k + 1], 0.0) for k in range(4)]
                left = jnp.concatenate([jnp.concatenate([a, c], axis=1), jnp.concatenate([b, d], axis=1)], axis=0)
                acc += lax.dot_general(left.astype(BF16), four(n * 8 + h), (((1,), (1,)), ((), ())),
                                       preferred_element_type=F32)
            return acc

        acc = lax.fori_loop(0, tiles // 8, forward, jnp.zeros((16, 2 * LANES), F32), unroll=2)
        v = acc[:8, :LANES] + acc[8:, LANES:]

        scalar_z(it, known[:2] + [known[2] + total(v * v)])

        zero = jnp.zeros((8, LANES), F32)
        vb = v.astype(BF16).astype(F32)
        twice = jnp.concatenate([jnp.concatenate([vb, zero], axis=1), jnp.concatenate([zero, vb], axis=1)], axis=0)
        twice = twice.astype(BF16)

        def backward(n, c):
            rows = jnp.zeros((8, LANES), F32)
            for h in (0, 4):
                out = jnp.dot(twice, four(n * 8 + h), preferred_element_type=F32)
                for k in range(4):
                    up, across = k % 2, k // 2
                    part = out[8 * up:8 * up + 8, across * LANES:(across + 1) * LANES]
                    picked = jnp.sum(jnp.where(sub == s.rows[n * 8 + h + k], part, 0.0), axis=0, keepdims=True)
                    rows = jnp.where(sub == h + k, picked, rows)
            s.back[n] = rows
            return c

        lax.fori_loop(0, tiles // 8, backward, 0, unroll=2)
        back = s.back[...].reshape(LANES, LANES).astype(BF16)
        outgoing = jnp.dot(s.placed_t[...], back, preferred_element_type=F32)
        s.b1_send[it] = outgoing.reshape(NJ, slots, LANES).astype(BF16)
        s.b1_recv[it, j] = s.b1_send[it, j]
        each(peers_j, lambda jj: start(it, B1, s.b1_send.at[it, jj], s.b1_recv.at[it, j], to_j(jj)))

        @pl.when(in_jb)
        def _():
            s.r1_recv[it, j] = s.r1_send[it, j]
            arrived(it, R1, s.r1_recv.at[it, pl.ds(0, NJ - 1)])
            part = jnp.sum(s.r1_recv[it].astype(F32), axis=0)
            for b in range(ZB):
                s.r2_send[it, b] = part[:, b * LANES:(b + 1) * LANES].astype(BF16)

            for b in range(ZB):
                @pl.when(b * ZS != z)
                def _(b=b):
                    start(it, R2, s.r2_send.at[it, b], s.r2_recv.at[it, z], to_z(b * ZS))

        scalar_x(it)

        arrived(it, B1, s.b1_recv.at[it, pl.ds(0, NJ - 1)])
        returned = s.b1_recv[it].reshape(all_slots, LANES)
        summed = jnp.dot(s.pmat_t[...], returned, preferred_element_type=F32)
        s.b2_send[it] = summed.reshape(nz, nb, LANES).astype(BF16)
        s.b2_recv[it, z] = s.b2_send[it, z]
        each(peers_z, lambda zz: start(it, B2, s.b2_send.at[it, zz], s.b2_recv.at[it, z], to_z(zz)))

        @pl.when(in_jb & in_zb)
        def _():
            s.r2_recv[it, z] = s.r2_send[it, lax.div(z, ZS)]
            arrived(it, R2, s.r2_recv.at[it, pl.ds(0, nz - 1)])
            part = jnp.sum(s.r2_recv[it].astype(F32), axis=0).astype(BF16)
            s.g1_send[it] = part
            s.g1_recv[it, lax.div(z, ZS)] = part
            each(peers_z, lambda zz: start(it, G1, s.g1_send.at[it], s.g1_recv.at[it, lax.div(z, ZS)], to_z(zz)))

        scalar_y(it, [rho_m, eta_m, delta_m])

        arrived(it, B2, s.b2_recv.at[it, pl.ds(0, nz - 1)])
        ped = jnp.sum(s.b2_recv[it].astype(F32), axis=0)
        image = a_diag * z_a + ped + jnp.where(blk == gblk, g_row, 0.0)
        sums = scalar_end(it)
        rho_next = sums[:, 0:1]
        beta = jnp.where(it == 0, 0.0, rho_next / rho)
        curv = sums[:, 2:3] + 2.0 * beta * sums[:, 1:2] + beta * beta * curv
        alpha = rho_next / curv
        alpha_y, beta_y = mine(alpha), mine(beta)
        u = z_a + beta_y * u
        q_a = image + beta_y * q_a
        sol_a = sol_a + alpha_y * u
        r_a = r_a - alpha_y * q_a
        return r_a * a_inv, r_a, q_a, u, sol_a, alpha, beta, rho_next, curv

    none = jnp.zeros((nb, LANES), F32)
    held = lax.fori_loop(0, ITERS, iterate, (r_a * a_inv, r_a, none, none, none, col, col, jnp.ones((traits, 1), F32), col),
                         unroll=True)
    _, r_a, _, _, sol_a, alpha, beta, _, _ = held
    last = ITERS - 1
    s.f_send[0] = sol_a
    s.f_send[1] = r_a
    s.f_recv[y] = s.f_send[...]
    each(peers_y, lambda yy: push(s.f_send, s.f_recv.at[y], s.once_send.at[1], s.once_recv.at[1], to_y(yy)))
    gather_wide(last)
    await_bytes(s.id_recv.at[pl.ds(0, NJ - 1)], s.once_send.at[0])
    for n in range(ITERS):
        for step, ref, count in ((SZ, s.sz_recv, nz - 1), (SX, s.sx_recv, NJ - 1), (SY, s.sy_recv, ny - 1)):
            await_bytes(ref.at[n, pl.ds(0, count)], s.sum_send.at[n, step])
    for it in range(ITERS):
        def gone(stage, ref, count, it=it):
            await_bytes(ref.at[it, pl.ds(0, count)], s.send.at[it, stage])

        for stage, ref, count in ((A1, s.a1_recv, nz - 1), (A2, s.a2_recv, NJ - 1), (B1, s.b1_recv, NJ - 1),
                                  (B2, s.b2_recv, nz - 1), (Y, s.y_recv, ny - 1)):
            gone(stage, ref, count)

        @pl.when(in_jb)
        def _():
            gone(R1, s.r1_recv, JB - 1)
            gone(G2, s.g2_recv, NJ - 1)

            @pl.when(in_zb)
            def _():
                gone(R2, s.r2_recv, ZB - 1)
                gone(G1, s.r2_recv, nz - 1)

            @pl.when(jnp.logical_not(in_zb))
            def _():
                gone(R2, s.r2_recv, ZB)

        @pl.when(jnp.logical_not(in_jb))
        def _():
            gone(R1, s.r1_recv, JB)

    gather_end(last)
    for b in range(JB):
        marker_step(ITERS, b, alpha, beta)
    await_bytes(s.f_recv.at[pl.ds(0, ny - 1)], s.once_recv.at[1])
    await_bytes(s.f_recv.at[pl.ds(0, ny - 1)], s.once_send.at[1])
    for t in range(traits):
        for k in range(nb):
            asol[t:t + 1, k * LANES:(k + 1) * LANES] = s.f_recv[t, 0, k:k + 1, :]
            ares[t:t + 1, k * LANES:(k + 1) * LANES] = s.f_recv[t, 1, k:k + 1, :]


def body(animal_rhs, marker_rhs, animal_diagonal, marker_diagonal, marker_scale, genotypes, tile_weights,
         tile_rows, tile_owner, tile_local, tile_count, genotyped_block):
    traits, animals = animal_rhs.shape
    markers = marker_rhs.shape[1]
    tiles = tile_weights.shape[0]
    nz, ny = lax.axis_size(ANIMALS) // NJ, lax.axis_size(SNPS)
    nb, slots = animals // LANES, nz * CAP
    every = NJ * slots
    wide = ZB * LANES

    def f32(*shape):
        return pltpu.VMEM(shape, F32)

    def b16(*shape):
        return pltpu.VMEM(shape, BF16)

    dma = pltpu.SemaphoreType.DMA
    scratch = dict(
        arhs=f32(traits, animals), adiag=f32(nb, LANES), mrhs=f32(traits, markers), mdiag=f32(1, markers),
        mscale=f32(1, markers), owner=pltpu.VMEM((1, tiles), I32), local=pltpu.VMEM((1, tiles), I32),
        rows=pltpu.SMEM((tiles,), I32),
        w=b16(*tile_weights.shape), g=b16(*genotypes.shape),
        placed=b16(LANES, every), placed_t=b16(every, LANES), table=f32(every, LANES),
        pmat=b16(every, nz * nb), pmat_t=b16(nz * nb, every),
        fetched=f32(LANES // 8, 8, LANES), back=f32(LANES // 8, 8, LANES),
        m=f32(traits, markers), q=f32(traits, markers), x=f32(traits, markers),
        m_inv=f32(1, markers),
        id_send=b16(NJ, slots, LANES), id_recv=b16(NJ, slots, LANES),
        a1_send=b16(ITERS, nb, LANES), a1_recv=b16(ITERS, nz, nb, LANES),
        a2_send=b16(ITERS, NJ, slots, LANES), a2_recv=b16(ITERS, NJ, slots, LANES),
        b1_send=b16(ITERS, NJ, slots, LANES), b1_recv=b16(ITERS, NJ, slots, LANES),
        b2_send=b16(ITERS, nz, nb, LANES), b2_recv=b16(ITERS, nz, nb, LANES),
        y_send=f32(ITERS, 8, LANES), y_recv=f32(ITERS, ny, 8, LANES),
        r1_send=b16(ITERS, JB, traits, wide), r1_recv=b16(ITERS, NJ, traits, wide),
        r2_send=b16(ITERS, ZB, traits, LANES), r2_recv=b16(ITERS, nz, traits, LANES),
        g1_send=b16(ITERS, traits, LANES), g1_recv=b16(ITERS, ZB, traits, LANES),
        g2_recv=b16(ITERS + 1, JB, ZB, traits, LANES),
        sz_send=f32(ITERS, 1, LANES), sz_recv=f32(ITERS, nz, 1, LANES),
        sx_send=f32(ITERS, 1, LANES), sx_recv=f32(ITERS, NJ, 1, LANES),
        sy_send=f32(ITERS, traits, LANES), sy_recv=f32(ITERS, ny, traits, LANES),
        f_send=f32(2, nb, LANES), f_recv=f32(ny, 2, nb, LANES),
        get=dma((10,)), once_send=dma((2,)), once_recv=dma((2,)),
        send=dma((ITERS, STAGES)), recv=dma((ITERS, STAGES)),
        sum_send=dma((ITERS, STEPS)), sum_recv=dma((ITERS, STEPS)),
    )

    def run(*refs):
        first = len(refs) - len(scratch)
        kernel(nz, ny, *refs[:first], SimpleNamespace(**dict(zip(scratch, refs[first:]))))

    outs = pl.pallas_call(
        run,
        out_shape=[jax.ShapeDtypeStruct(a.shape, F32) for a in (animal_rhs, marker_rhs, animal_rhs, marker_rhs)],
        in_specs=[pl.BlockSpec(memory_space=pl.ANY)] * 10 + [pl.BlockSpec(memory_space=pltpu.SMEM)] * 2,
        out_specs=[pl.BlockSpec(memory_space=pltpu.VMEM)] * 4,
        scratch_shapes=list(scratch.values()),
        compiler_params=pltpu.CompilerParams(collective_id=0, has_side_effects=True, vmem_limit_bytes=60 * 2**20),
    )(animal_rhs, marker_rhs, animal_diagonal.reshape(nb, LANES), marker_diagonal,
      marker_scale, genotypes, tile_weights, tile_rows, tile_owner.reshape(1, tiles),
      tile_local.reshape(1, tiles), tile_count, genotyped_block)

    def leave(*refs):
        sources, results, stages, sems = refs[:4], refs[4:8], refs[8:12], refs[12]
        reads = [pltpu.make_async_copy(a, b, sems.at[k]) for k, (a, b) in enumerate(zip(sources, stages))]
        writes = [pltpu.make_async_copy(a, b, sems.at[4 + k]) for k, (a, b) in enumerate(zip(stages, results))]
        for read in reads:
            read.start()
        for read, write in zip(reads, writes):
            read.wait()
            write.start()
        for write in writes:
            write.wait()

    return pl.pallas_call(
        leave,
        out_shape=[jax.ShapeDtypeStruct(a.shape, F32) for a in outs],
        in_specs=[pl.BlockSpec(memory_space=pl.ANY)] * 4,
        out_specs=[pl.BlockSpec(memory_space=pl.ANY)] * 4,
        scratch_shapes=[pltpu.VMEM(a.shape, F32) for a in outs] + [dma((8,))],
        compiler_params=pltpu.CompilerParams(vmem_limit_bytes=60 * 2**20),
    )(*outs)


def solution(mesh):
    placed = (P(None, ANIMALS), P(None, SNPS), P(ANIMALS), P(SNPS), P(SNPS), P(ANIMALS, SNPS),
              P(ANIMALS, None, None), P(ANIMALS), P(ANIMALS, None), P(ANIMALS), P(ANIMALS), P(ANIMALS))
    return jax.shard_map(
        body, mesh=mesh, in_specs=placed,
        out_specs=(P(None, ANIMALS), P(None, SNPS), P(None, ANIMALS), P(None, SNPS)), check_vma=False)
```
